32 devices in a mesh: rep: 4 (over y, core), wide: 8 (over z, x).
Axes of the slice: x: 2, y: 2, z: 4, core: 2. Of those that a mesh axis runs over, the one named last changes fastest.
Arguments:
- tokens: bfloat16 [32768, 768], P(('rep', 'wide')), may hold values from -6 to 6
- segment_ids: int32 [64, 512], P(('rep', 'wide')), may hold values from 0 to 3, never falling along the last dimension, each value on 1 to 256 neighbouring positions
- cotangent: bfloat16 [32768, 768], P(('rep', 'wide')), may hold values from -6 to 6
- w_query: bfloat16 [768, 768], P('rep'), may hold values from -0.21875 to 0.21875
- w_key: bfloat16 [768, 768], P('rep'), may hold values from -0.21875 to 0.21875
- w_value: bfloat16 [768, 768], P('rep'), may hold values from -0.21875 to 0.21875
- w_output: bfloat16 [768, 768], P('rep'), may hold values from -0.625 to 0.625
- w_inner: bfloat16 [768, 3072], P('rep'), may hold values from -0.21875 to 0.21875
- w_outer: bfloat16 [3072, 768], P('rep'), may hold values from -0.109375 to 0.109375
- b_query: float32 [768], replicated, may hold values from -3 to 3
- b_value: float32 [768], replicated, may hold values from -3 to 3
- b_output: float32 [768], replicated, may hold values from -3 to 3
- b_inner: float32 [3072], replicated, may hold values from -3 to 3
- b_outer: float32 [768], replicated, may hold values from -3 to 3
- norm1_gain: float32 [768], replicated, may hold values from 0.5 to 1.5
- norm1_shift: float32 [768], replicated, may hold values from -3 to 3
- norm2_gain: float32 [768], replicated, may hold values from 0.5 to 1.5
- norm2_shift: float32 [768], replicated, may hold values from -3 to 3
- factors: float32 [24576], replicated, may hold values from -3 to 3, as said below
- first_moment: float32 [24576], P('wide'), may hold values from -0.005740992 to 0.005740992
- second_moment: float32 [24576], P('wide'), may hold values from 2.0345052e-08 to 2.0345052e-07
Outputs:
- layer_out: bfloat16 [32768, 768], P(('rep', 'wide'))
- input_grad: bfloat16 [32768, 768], P(('rep', 'wide'))
- factor_grads: float32 [24576], P('wide')
- new_factors: float32 [24576], replicated
- new_first: float32 [24576], P('wide')
- new_second: float32 [24576], P('wide')
The draws below stay inside these ranges and needn't reach their ends.
Inputs may be any that keep to these rules, and one draw needn't show every extreme that they name: `factors`: entries of the A half are at most a few times 768^-0.5 in size, those of the B half at most a few times 8^-0.5.
All inputs are finite; a program needn't handle non-finite values.
Results may differ from the reference program's by a relative error of at most 0.028.
The reference program's roundings to bfloat16 on the way (of `ctx`) count: a program that leaves them out, or rounds other values in their place, can miss the bound.
Values may be sent and summed in bfloat16 or wider, within the bound.
No kernel may reach another device: no remote copies, remote signals or barrier semaphores. Data moves between devices by JAX's collectives and lax.ppermute only.
A program may use at most 192 MiB of HBM per device.

```python
import math
import jax
import jax.numpy as jnp
import numpy as np
from jax import lax

D = 768
HEADS = 12
HEAD_DIM = 64
FF = 3072
ADAPTER_RANK = 8
STEP = 10
PACK = 512
PACKS = 64
TOKENS = 32768


def draw_factors(key, part):
    key = jax.random.fold_in(key, 7)
    total = 4 * ADAPTER_RANK * D
    base = jnp.clip(jax.random.normal(key, (total,), jnp.float32), -3.0, 3.0)
    position = jnp.arange(total)
    scale = jnp.where(position < 2 * ADAPTER_RANK * D, D ** (-0.5), ADAPTER_RANK ** (-0.5))
    ranks = jnp.arange(ADAPTER_RANK).astype(jnp.float32)
    row_scales = jnp.power(16.0, ranks / (ADAPTER_RANK - 1))
    row_scales = row_scales / jnp.sqrt(jnp.mean(row_scales * row_scales))
    row_of = position // D % ADAPTER_RANK
    return (base * scale * row_scales[row_of]).astype(jnp.float32)


def draw_first_moment(key, part):
    key = jax.random.fold_in(key, 11)
    total = 4 * ADAPTER_RANK * D
    spread = float(total) ** (-0.5)
    base = 0.3 * jnp.clip(jax.random.normal(key, (total,), jnp.float32), -3.0, 3.0)
    return (base * spread).astype(jnp.float32)


def draw_second_moment(key, part):
    key = jax.random.fold_in(key, 13)
    total = 4 * ADAPTER_RANK * D
    base = jnp.exp(jax.random.uniform(key, (total,), jnp.float32, jnp.log(0.0005), jnp.log(0.005)))
    return (base / float(total)).astype(jnp.float32)


def block_scale(rng, dims, split, low, largest):
    factor_of = 1.0
    for axis_at, blocks in split:
        draws = jax.random.uniform(jax.random.fold_in(jax.random.fold_in(rng, 6), axis_at), (blocks,), jnp.float32, low / len(split), largest / len(split))
        factor_of = factor_of * jnp.repeat(jnp.exp(draws), dims[axis_at] // blocks).reshape((-1,) + (1,) * (len(dims) - 1 - axis_at))
    return factor_of


def split_up(count, total, reach, lean):
    loads = [(1 << 20) // math.isqrt(rank ** lean) + 1 for rank in range(2, count + 1)]
    rest, holding = total - reach - (count - 1), [1] * (count - 1)
    while rest > 0:
        free = [i for i in range(count - 1) if holding[i] < reach]
        whole, remaining = sum([loads[i] for i in free]), rest
        for i in free:
            addition = min(reach - holding[i], max(1, remaining * loads[i] // whole), rest)
            holding[i] = holding[i] + addition
            rest = rest - addition
    return np.array([reach] + holding)


def uneven(rng, amount, total, limit, slope):
    if amount == 2:
        one = jax.random.randint(rng, (), max(1, total - limit), min(limit, total - 1) + 1)
        return jnp.stack([one, total - one])
    sizes = jnp.asarray(split_up(amount, total, limit, slope), jnp.int32)
    pairs = (amount - 1) // 2
    giver, taker = sizes[1:1 + 2 * pairs:2], sizes[2:2 + 2 * pairs:2]
    room = jnp.minimum(giver - 1, limit - taker)
    moved = jax.random.randint(jax.random.fold_in(rng, 1), (pairs,), 0, 1 << 20) % (room + 1)
    sizes = sizes.at[1:1 + 2 * pairs:2].set(giver - moved).at[2:2 + 2 * pairs:2].set(taker + moved)
    return sizes[jax.random.permutation(jax.random.fold_in(rng, 2), amount)]


def scatter_about(key, shape, scale, limit, split=(), held_as=jnp.bfloat16):
    level = block_scale(key, shape, split, -0.22, 0.18) if split else 1.0
    result = jax.random.normal(key, shape, jnp.float32) * scale * level
    return jnp.minimum(jnp.maximum(result, -limit), limit).astype(held_as)


def setup_inputs(seed: int = 0) -> dict:
    key_of = jax.random.split(jax.random.key(seed), 22)
    tokens = scatter_about(key_of[0], (TOKENS, D), 1.0, 6.0, ((0, 32),))
    segment_ids = jax.vmap(lambda own: jnp.searchsorted(jnp.cumsum(uneven(own, 4, PACK, PACK // 2, 1)), jnp.arange(PACK), side="right"))(jax.random.split(key_of[1], PACKS)).reshape((PACKS, PACK)).astype(jnp.int32)
    cotangent = scatter_about(key_of[2], (TOKENS, D), 1.0, 6.0, ((0, 32),))
    w_query = scatter_about(key_of[3], (D, D), D ** -0.5, 0.21875, ((0, 4),))
    w_key = scatter_about(key_of[4], (D, D), D ** -0.5, 0.21875, ((0, 4),))
    w_value = scatter_about(key_of[5], (D, D), D ** -0.5, 0.21875, ((0, 4),))
    w_output = scatter_about(key_of[6], (D, D), (D // 8) ** -0.5, 0.625, ((0, 4),))
    w_inner = scatter_about(key_of[7], (D, FF), D ** -0.5, 0.21875, ((0, 4),))
    w_outer = scatter_about(key_of[8], (FF, D), FF ** -0.5, 0.109375, ((0, 4),))
    b_query = scatter_about(key_of[9], (D,), 0.5, 3.0, (), jnp.float32)
    b_value = scatter_about(key_of[10], (D,), 0.5, 3.0, (), jnp.float32)
    b_output = scatter_about(key_of[11], (D,), 0.5, 3.0, (), jnp.float32)
    b_inner = scatter_about(key_of[12], (FF,), 0.5, 3.0, (), jnp.float32)
    b_outer = scatter_about(key_of[13], (D,), 0.5, 3.0, (), jnp.float32)
    norm1_gain = jnp.clip(1.0 + 0.1 * jax.random.normal(key_of[14], (D,), jnp.float32), 0.5, 1.5)
    norm1_shift = scatter_about(key_of[15], (D,), 0.5, 3.0, (), jnp.float32)
    norm2_gain = jnp.clip(1.0 + 0.1 * jax.random.normal(key_of[16], (D,), jnp.float32), 0.5, 1.5)
    norm2_shift = scatter_about(key_of[17], (D,), 0.5, 3.0, (), jnp.float32)
    factors = draw_factors(jax.random.fold_in(key_of[21], 71), 0)
    first_moment = draw_first_moment(jax.random.fold_in(key_of[21], 71), 0)
    second_moment = draw_second_moment(jax.random.fold_in(key_of[21], 71), 0)
    return {"tokens": tokens, "segment_ids": segment_ids, "cotangent": cotangent, "w_query": w_query, "w_key": w_key, "w_value": w_value, "w_output": w_output, "w_inner": w_inner, "w_outer": w_outer, "b_query": b_query, "b_value": b_value, "b_output": b_output, "b_inner": b_inner, "b_outer": b_outer, "norm1_gain": norm1_gain, "norm1_shift": norm1_shift, "norm2_gain": norm2_gain, "norm2_shift": norm2_shift, "factors": factors, "first_moment": first_moment, "second_moment": second_moment}


@jax.custom_vjp
def low(v):
    return lax.optimization_barrier(v.astype(jnp.bfloat16)).astype(jnp.float32)

@jax.custom_vjp
def low_back(v):
    return v

def low_keep(v):
    return (low(v), None)

def low_pass(kept, grad):
    return (grad,)

def back_keep(v):
    return (v, None)

def back_low(kept, grad):
    return (low(grad),)
low.defvjp(low_keep, low_pass)
low_back.defvjp(back_keep, back_low)
rate_low = 0.015
rate_high = 0.24
decay_rate = 0.01

def matmul(left, right):
    return jnp.dot(left, right, precision=lax.Precision.HIGHEST)

def layer_norm(hidden, gain, shift):
    mean = lax.optimization_barrier(jnp.mean(hidden, -1, keepdims=True))
    centre = hidden - mean
    return centre * lax.rsqrt(lax.optimization_barrier(jnp.mean(centre * centre, -1, keepdims=True)) + 1e-05) * gain + shift

def attend_pack(item):
    query, key, value, seg = item
    scale = HEAD_DIM ** (-0.5)
    qh = query.reshape(PACK, HEADS, HEAD_DIM)
    kh = key.reshape(PACK, HEADS, HEAD_DIM)
    vh = value.reshape(PACK, HEADS, HEAD_DIM)
    scores = jnp.einsum('qhd,khd->hqk', qh, kh, precision=lax.Precision.HIGHEST) * scale
    scores = low_back(scores)
    same = seg[:, None] == seg[None, :]
    scores = jnp.where(same[None], scores, -1e+30)
    probs = jax.nn.softmax(scores, axis=-1)
    ctx = jnp.einsum('hqk,khd->qhd', low(probs), vh, precision=lax.Precision.HIGHEST)
    return ctx.reshape(PACK, D)

def forward(x, fac, seg, weights, vectors):
    wq, wk, wv, wo, w1, w2 = weights
    bq, bv, bo, bi, bo2, g1, s1, g2, s2 = vectors
    rd = ADAPTER_RANK * D
    aq = low(fac[0:rd].reshape(ADAPTER_RANK, D))
    av = low(fac[rd:2 * rd].reshape(ADAPTER_RANK, D))
    query_factor = low(fac[2 * rd:3 * rd].reshape(ADAPTER_RANK, D))
    value_factor = low(fac[3 * rd:4 * rd].reshape(ADAPTER_RANK, D))
    lq = low(low_back(matmul(x, aq.T)))
    lv = low(low_back(matmul(x, av.T)))
    query = low(low_back(matmul(x, wq) + bq + 2.0 * matmul(lq, query_factor)))
    key = low(low_back(matmul(x, wk)))
    value = low(low_back(matmul(x, wv) + bv + 2.0 * matmul(lv, value_factor)))
    count = x.shape[0] // PACK
    ctx = lax.map(jax.checkpoint(attend_pack), (query.reshape(count, PACK, D), key.reshape(count, PACK, D), value.reshape(count, PACK, D), seg))
    ctx = low(low_back(ctx.reshape(count * PACK, D)))
    attn = low_back(matmul(ctx, wo) + bo)
    first = layer_norm(x + attn, g1, s1)
    inner = low_back(matmul(low(first), w1) + bi)
    act = low(jax.nn.gelu(inner, approximate=False))
    ffn = low_back(matmul(act, w2) + bo2)
    return layer_norm(first + ffn, g2, s2)

def reference(tokens, segment_ids, cotangent, w_query, w_key, w_value, w_output, w_inner, w_outer, b_query, b_value, b_output, b_inner, b_outer, norm1_gain, norm1_shift, norm2_gain, norm2_shift, factors, first_moment, second_moment):
    weights = tuple((w.astype(jnp.float32) for w in (w_query, w_key, w_value, w_output, w_inner, w_outer)))
    vectors = (b_query, b_value, b_output, b_inner, b_outer, norm1_gain, norm1_shift, norm2_gain, norm2_shift)
    group = 8 if PACKS % 8 == 0 else 1
    steps_n = PACKS // group
    xs = tokens.astype(jnp.float32).reshape(steps_n, group * PACK, D)
    segs = segment_ids.reshape(steps_n, group, PACK)
    cots = cotangent.astype(jnp.float32).reshape(steps_n, group * PACK, D)

    def one(carry, item):
        xval, seg, cot = item
        out, pull = jax.vjp(lambda xv, value_factor: forward(xv, value_factor, seg, weights, vectors), xval, factors)
        dx, dfac = pull(cot)
        return (carry + dfac, (out, dx))
    grad, (outs, dxs) = lax.scan(one, jnp.zeros_like(factors), (xs, segs, cots))
    layer_out = outs.reshape(TOKENS, D).astype(jnp.bfloat16)
    input_grad = dxs.reshape(TOKENS, D).astype(jnp.bfloat16)
    clip = jnp.minimum(1.0, 1.0 / (jnp.sqrt(jnp.sum(grad * grad)) + 1e-06))
    clipped = grad * clip
    new_first = 0.9 * first_moment + 0.1 * clipped
    new_second = 0.999 * second_moment + 0.001 * clipped * clipped
    steps_done = jnp.float32(STEP)
    fix_first = 1.0 - jnp.power(jnp.float32(0.9), steps_done)
    fix_second = 1.0 - jnp.power(jnp.float32(0.999), steps_done)
    position = jnp.arange(factors.shape[0], dtype=jnp.int32)
    rate = jnp.where(position < 2 * ADAPTER_RANK * D, rate_low, rate_high)
    update = new_first / fix_first / (jnp.sqrt(new_second / fix_second) + 1e-08) + decay_rate * factors
    new_factors = factors - rate * update
    return (layer_out, input_grad, grad, new_factors, new_first, new_second)
```

```python
import functools

import jax
import jax.numpy as jnp
from jax import lax
from jax.experimental import pallas as pl
from jax.experimental.pallas import tpu as pltpu
from jax.sharding import PartitionSpec as P

HEADS = 12
ADAPTER_RANK = 8
STEP = 10
LANES = 128
MASKED = 1e30

rate_low = 0.015
rate_high = 0.24
decay_rate = 0.01

BF16 = jnp.bfloat16
F32 = jnp.float32
NN = (((1,), (0,)), ((), ()))
NT = (((1,), (1,)), ((), ()))
TN = (((0,), (0,)), ((), ()))
ANY = pl.BlockSpec(memory_space=pl.ANY)
VMEM_LIMIT = 56 * 2**20


def dot(left, right, dims):
    return lax.dot_general(left, right, dims, preferred_element_type=F32)


def beside(*parts):
    return jnp.concatenate(parts, axis=1)


def mean(value):
    return jnp.mean(value, -1, keepdims=True)


def layer_norm(hidden):
    centre = hidden - mean(hidden)
    rstd = lax.rsqrt(mean(centre * centre) + 1e-05)
    return (centre * rstd, rstd)


def norm_back(grad, normal, rstd, gain):
    scaled = grad * gain
    return rstd * (scaled - mean(scaled) - normal * mean(scaled * normal))


def gelu_pair(value):
    below = 0.5 + 0.5 * lax.erf(value * 2.0 ** (-0.5))
    density = jnp.exp(-0.5 * value * value) * 0.3989422804014327
    return (value * below, below + value * density)


def three_parts(value):
    high = value.astype(BF16).astype(F32)
    rest = value - high
    middle = rest.astype(BF16).astype(F32)
    return (high, middle, rest - middle)


def pieces(rank, refs, target, semaphores):
    rows = refs[0].shape[0]
    return [
        pltpu.make_async_copy(
            ref,
            target.at[pl.ds(pl.multiple_of(jnp.bitwise_xor(rank, flip) * rows, 16), rows)],
            semaphores.at[flip],
        )
        for flip, ref in enumerate(refs)
    ]


def attend_kernel(group, rank_ref, seg_ref, x_ref, fac_ref, bq_ref, bv_ref, *rest):
    shards, rest = rest[:group], rest[group:]
    q_ref, k_ref, v_ref, ctx_ref, aug_ref, down_ref, weights, low, semaphores = rest
    at = pl.program_id(1)
    width = q_ref.shape[1]
    total = x_ref.shape[1]
    rows = x_ref.shape[0]

    @pl.when((pl.program_id(0) == 0) & (at == 0))
    def _():
        copies = pieces(rank_ref[0], shards, weights, semaphores)
        for copy in copies:
            copy.start()
        for copy in copies:
            copy.wait()

    rank2 = 2 * ADAPTER_RANK

    @pl.when(at == 0)
    def _():
        down = fac_ref[0:rank2, :].astype(BF16)
        low[...] = dot(x_ref[...], down, NT).astype(BF16)
        down_ref[...] = low[...]

    start = pl.multiple_of(at * width, LANES)
    columns = pl.ds(start, width)
    up = fac_ref[rank2 : 2 * rank2, columns]
    row = lax.broadcasted_iota(jnp.int32, up.shape, 0)
    up_q = jnp.where(row < ADAPTER_RANK, up, 0.0).astype(BF16)
    up_v = jnp.where(row < ADAPTER_RANK, 0.0, up).astype(BF16)
    x = x_ref[...]
    q_ref[...] = (
        dot(x, weights[:, columns], NN) + bq_ref[:, columns] + 2.0 * dot(low[...], up_q, NN)
    ).astype(BF16)
    k_ref[...] = dot(
        x, weights[:, pl.ds(pl.multiple_of(total + start, LANES), width)], NN
    ).astype(BF16)
    v_ref[...] = (
        dot(x, weights[:, pl.ds(pl.multiple_of(2 * total + start, LANES), width)], NN)
        + bv_ref[:, columns]
        + 2.0 * dot(low[...], up_v, NN)
    ).astype(BF16)

    lane = lax.broadcasted_iota(jnp.int32, (rows, LANES), 1)
    seg = seg_ref[0].astype(F32).T.astype(jnp.int32)
    own = jnp.where(lane == seg, 1.0, 0.0)
    aug_k = jnp.where((lane < 4) & (lane != seg), -MASKED, 0.0).astype(BF16)
    aug_q = own.astype(BF16)
    ones = jnp.ones((rows, LANES), BF16)
    half = LANES // 2
    scale = BF16(half ** (-0.5))
    for pair in range(width // LANES):
        here = slice(LANES * pair, LANES * (pair + 1))
        keys = beside(k_ref[:, here], aug_k)
        values = beside(v_ref[:, here], ones)
        query = q_ref[:, here] * scale
        out = None
        for side in range(2):
            mask = (lane // half) == side
            scores = dot(beside(jnp.where(mask, query, BF16(0)), aug_q), keys, NT)
            top = jnp.max(scores, axis=1, keepdims=True)
            expo = jnp.exp(scores - top).astype(BF16)
            both = dot(expo, values, NN)
            sums = both[:, LANES:]
            ctx = both[:, :LANES] / sums
            out = ctx if side == 0 else jnp.where(mask, ctx, out)
            high, middle, little = three_parts(-(top + jnp.log(sums)))
            aug = jnp.where(
                lane == 4, high, jnp.where(lane == 5, middle, jnp.where(lane == 6, little, own))
            )
            aug_ref[:, (2 * pair + side) * LANES : (2 * pair + side + 1) * LANES] = aug.astype(BF16)
        ctx_ref[:, here] = out.astype(BF16)


def attend(rank, seg, x, factors, bq, bv, shards, pairs):
    packs, size = seg.shape
    rows, width = x.shape
    cut = pairs * LANES
    block = pl.BlockSpec((size, cut), lambda p, g: (p, g))
    whole = lambda shape: pl.BlockSpec(shape, lambda p, g: (0, 0), pipeline_mode=pl.Buffered(1))
    like = jax.ShapeDtypeStruct
    return pl.pallas_call(
        functools.partial(attend_kernel, len(shards)),
        grid=(packs, width // cut),
        in_specs=[
            pl.BlockSpec(memory_space=pltpu.SMEM),
            pl.BlockSpec((1, 1, size), lambda p, g: (p, 0, 0)),
            pl.BlockSpec((size, width), lambda p, g: (p, 0)),
            whole(factors.shape),
            whole(bq.shape),
            whole(bv.shape),
        ]
        + [ANY] * len(shards),
        out_specs=[
            block,
            block,
            block,
            block,
            pl.BlockSpec((size, 2 * cut), lambda p, g: (p, g)),
            pl.BlockSpec((size, 2 * ADAPTER_RANK), lambda p, g: (p, 0)),
        ],
        out_shape=[like((rows, width), BF16)] * 4
        + [like((rows, 2 * width), BF16), like((rows, 2 * ADAPTER_RANK), BF16)],
        scratch_shapes=[
            pltpu.VMEM((width, 3 * width), BF16),
            pltpu.VMEM((size, 2 * ADAPTER_RANK), BF16),
            pltpu.SemaphoreType.DMA((len(shards),)),
        ],
        compiler_params=pltpu.CompilerParams(vmem_limit_bytes=VMEM_LIMIT),
        cost_estimate=pl.CostEstimate(
            flops=rows * width * (6 * width + 16 * size),
            bytes_accessed=16 * rows * width,
            transcendentals=rows * size * HEADS,
        ),
        name="project_and_attend",
    )(rank, seg.reshape(packs, 1, size), x, factors, bq, bv, *shards)


def dense_kernel(group, cut, rank_ref, x_ref, ctx_ref, cot_ref, *rest):
    vectors, rest = rest[:7], rest[7:]
    bo_ref, bi_ref, bo2_ref, g1_ref, s1_ref, g2_ref, s2_ref = vectors
    first, second, rest = rest[:group], rest[group : 2 * group], rest[2 * group :]
    out_ref, dh_ref, dctx_ref, ahead, outer, slope, semaphores = rest
    width = x_ref.shape[1]
    hidden = outer.shape[0]

    @pl.when(pl.program_id(0) == 0)
    def _():
        copies = pieces(rank_ref[0], first, ahead, semaphores.at[0])
        copies += pieces(rank_ref[0], second, outer, semaphores.at[1])
        for copy in copies:
            copy.start()
        for copy in copies:
            copy.wait()

    wo = lambda: ahead[:, :width]
    w1 = lambda j: ahead[:, width + j : width + j + cut]
    h1 = x_ref[...].astype(F32) + dot(ctx_ref[...], wo(), NN) + bo_ref[...]
    norm1, rstd1 = layer_norm(h1)
    y1 = norm1 * g1_ref[...] + s1_ref[...]
    y1_low = y1.astype(BF16)
    h2 = y1 + bo2_ref[...]
    for j in range(0, hidden, cut):
        inner = dot(y1_low, w1(j), NN) + bi_ref[:, j : j + cut]
        act, gradient = gelu_pair(inner)
        slope[:, j : j + cut] = gradient
        h2 = h2 + dot(act.astype(BF16), outer[j : j + cut, :], NN)
    norm2, rstd2 = layer_norm(h2)
    out_ref[...] = (norm2 * g2_ref[...] + s2_ref[...]).astype(BF16)
    dh2 = norm_back(cot_ref[...].astype(F32), norm2, rstd2, g2_ref[...])
    df = dh2.astype(BF16)
    dy1 = dh2
    for j in range(0, hidden, cut):
        du = (dot(df, outer[j : j + cut, :], NT) * slope[:, j : j + cut]).astype(BF16)
        dy1 = dy1 + dot(du, w1(j), NT)
    dh1 = norm_back(dy1, norm1, rstd1, g1_ref[...]).astype(BF16)
    dh_ref[...] = dh1
    dctx_ref[...] = dot(dh1, wo(), NT).astype(BF16)


def dense(rank, x, ctx, cot, vectors, first, second, size, cut):
    rows, width = x.shape
    hidden = vectors[1].shape[1]
    block = pl.BlockSpec((size, width), lambda i: (i, 0))
    whole = lambda shape: pl.BlockSpec(shape, lambda i: (0, 0), pipeline_mode=pl.Buffered(1))
    return pl.pallas_call(
        functools.partial(dense_kernel, len(first), cut),
        grid=(rows // size,),
        in_specs=[pl.BlockSpec(memory_space=pltpu.SMEM), block, block, block]
        + [whole(vector.shape) for vector in vectors]
        + [ANY] * (2 * len(first)),
        out_specs=[block] * 3,
        out_shape=[jax.ShapeDtypeStruct((rows, width), BF16)] * 3,
        scratch_shapes=[
            pltpu.VMEM((width, width + hidden), BF16),
            pltpu.VMEM((hidden, width), BF16),
            pltpu.VMEM((size, hidden), F32),
            pltpu.SemaphoreType.DMA((2, len(first))),
        ],
        compiler_params=pltpu.CompilerParams(vmem_limit_bytes=VMEM_LIMIT),
        cost_estimate=pl.CostEstimate(
            flops=rows * width * (4 * width + 8 * hidden),
            bytes_accessed=12 * rows * width + 4 * width * hidden,
            transcendentals=2 * rows * hidden,
        ),
        name="dense_both_ways",
    )(rank, x, ctx, cot, *vectors, *first, *second)


def attend_back_kernel(seg_ref, x_ref, fac_ref, down_ref, *rest):
    q_ref, k_ref, v_ref, dctx_ref, ctx_ref, aug_ref, *rest = rest
    dq_ref, dk_ref, dv_ref, dlow_ref, grad_ref, low, total = rest
    pack, at = pl.program_id(0), pl.program_id(1)
    rows, width = q_ref.shape
    rank2 = 2 * ADAPTER_RANK
    columns = pl.ds(pl.multiple_of(at * width, LANES), width)
    lane = lax.broadcasted_iota(jnp.int32, (rows, LANES), 1)
    seg = seg_ref[0].astype(F32).T.astype(jnp.int32)
    aug_k = jnp.where(
        (lane < 4) & (lane != seg), -MASKED, jnp.where((lane >= 4) & (lane < 7), 1.0, 0.0)
    ).astype(BF16)
    aug_v = jnp.where(lane < 3, 1.0, 0.0).astype(BF16)
    zero = BF16(0)
    half = LANES // 2
    scale = BF16(half ** (-0.5))
    for pair in range(width // LANES):
        here = slice(LANES * pair, LANES * (pair + 1))
        key = k_ref[:, here]
        query = q_ref[:, here] * scale
        grad = dctx_ref[:, here]
        keys = beside(key, aug_k)
        values = beside(v_ref[:, here], aug_v)
        key = key * scale
        product = grad.astype(F32) * ctx_ref[:, here].astype(F32)
        dq = dk = dv = 0.0
        for side in range(2):
            mask = (lane // half) == side
            one_query = jnp.where(mask, query, zero)
            one_grad = jnp.where(mask, grad, zero)
            one_key = jnp.where(mask, key, zero)
            inner = -jnp.sum(jnp.where(mask, product, 0.0), axis=1, keepdims=True)
            high, middle, little = three_parts(inner)
            aug_d = jnp.where(
                lane == 0, high, jnp.where(lane == 1, middle, jnp.where(lane == 2, little, 0.0))
            ).astype(BF16)
            aug_q = aug_ref[:, (2 * pair + side) * LANES : (2 * pair + side + 1) * LANES]
            probs = jnp.exp(dot(keys, beside(one_query, aug_q), NT))
            dprobs = dot(values, beside(one_grad, aug_d), NT)
            dscores = (probs * dprobs).astype(BF16)
            dv = dv + dot(probs.astype(BF16), one_grad, NN)
            dk = dk + dot(dscores, one_query, NN)
            dq = dq + dot(dscores, one_key, TN)
        dq_ref[:, here] = dq.astype(BF16)
        dk_ref[:, here] = dk.astype(BF16)
        dv_ref[:, here] = dv.astype(BF16)

    up = fac_ref[rank2 : 2 * rank2, columns]
    row = lax.broadcasted_iota(jnp.int32, up.shape, 0)
    up_q = jnp.where(row < ADAPTER_RANK, up, 0.0).astype(BF16)
    up_v = jnp.where(row < ADAPTER_RANK, 0.0, up).astype(BF16)
    dlow = dot(dq_ref[...], up_q, NT) + dot(dv_ref[...], up_v, NT)
    low[...] = dlow + jnp.where(at == 0, 0.0, low[...])
    down = down_ref[...]
    from_q = dot(down, dq_ref[...], TN)
    from_v = dot(down, dv_ref[...], TN)
    share = 2.0 * jnp.where(row < ADAPTER_RANK, from_q, from_v)
    later = pack > 0
    total[rank2 : 2 * rank2, columns] = share + jnp.where(
        later, total[rank2 : 2 * rank2, columns], 0.0
    )

    @pl.when(at == pl.num_programs(1) - 1)
    def _():
        dlow_low = (2.0 * low[...]).astype(BF16)
        dlow_ref[...] = dlow_low
        total[0:rank2, :] = dot(dlow_low, x_ref[...], TN) + jnp.where(
            later, total[0:rank2, :], 0.0
        )
        grad_ref[...] = total[...].astype(BF16)


def attend_back(seg, x, factors, down, q, k, v, dctx, ctx, aug, pairs):
    packs, size = seg.shape
    rows, width = x.shape
    cut = pairs * LANES
    rank2 = 2 * ADAPTER_RANK
    block = pl.BlockSpec((size, cut), lambda p, g: (p, g))
    whole = lambda shape: pl.BlockSpec(shape, lambda p, g: (0, 0), pipeline_mode=pl.Buffered(1))
    like = jax.ShapeDtypeStruct
    return pl.pallas_call(
        attend_back_kernel,
        grid=(packs, width // cut),
        in_specs=[
            pl.BlockSpec((1, 1, size), lambda p, g: (p, 0, 0)),
            pl.BlockSpec((size, width), lambda p, g: (p, 0)),
            whole(factors.shape),
            pl.BlockSpec((size, rank2), lambda p, g: (p, 0)),
            block,
            block,
            block,
            block,
            block,
            pl.BlockSpec((size, 2 * cut), lambda p, g: (p, g)),
        ],
        out_specs=[
            block,
            block,
            block,
            pl.BlockSpec((size, rank2), lambda p, g: (p, 0)),
            whole(factors.shape),
        ],
        out_shape=[like((rows, width), BF16)] * 3
        + [like((rows, rank2), BF16), like(factors.shape, BF16)],
        scratch_shapes=[pltpu.VMEM((size, rank2), F32), pltpu.VMEM(factors.shape, F32)],
        compiler_params=pltpu.CompilerParams(vmem_limit_bytes=VMEM_LIMIT),
        cost_estimate=pl.CostEstimate(
            flops=rows * width * 30 * size,
            bytes_accessed=24 * rows * width,
            transcendentals=rows * size * HEADS,
        ),
        name="attend_back",
    )(seg.reshape(packs, 1, size), x, factors, down, q, k, v, dctx, ctx, aug)


def input_kernel(group, rank_ref, dh_ref, dq_ref, dk_ref, dv_ref, dlow_ref, fac_ref, *rest):
    shards, (out_ref, weights, semaphores) = rest[:group], rest[group:]
    width = dh_ref.shape[1]

    @pl.when(pl.program_id(0) == 0)
    def _():
        copies = pieces(rank_ref[0], shards, weights, semaphores)
        for copy in copies:
            copy.start()
        for copy in copies:
            copy.wait()

    down = fac_ref[0 : 2 * ADAPTER_RANK, :].astype(BF16)
    out_ref[...] = (
        dh_ref[...].astype(F32)
        + dot(dq_ref[...], weights[:, :width], NT)
        + dot(dk_ref[...], weights[:, width : 2 * width], NT)
        + dot(dv_ref[...], weights[:, 2 * width :], NT)
        + dot(dlow_ref[...], down, NN)
    ).astype(BF16)


def input_back(rank, dh, dq, dk, dv, dlow, factors, shards, size):
    rows, width = dh.shape
    block = pl.BlockSpec((size, width), lambda i: (i, 0))
    return pl.pallas_call(
        functools.partial(input_kernel, len(shards)),
        grid=(rows // size,),
        in_specs=[
            pl.BlockSpec(memory_space=pltpu.SMEM),
            block,
            block,
            block,
            block,
            pl.BlockSpec((size, dlow.shape[1]), lambda i: (i, 0)),
            pl.BlockSpec(factors.shape, lambda i: (0, 0)),
        ]
        + [ANY] * len(shards),
        out_specs=block,
        out_shape=jax.ShapeDtypeStruct((rows, width), BF16),
        scratch_shapes=[
            pltpu.VMEM((width, 3 * width), BF16),
            pltpu.SemaphoreType.DMA((len(shards),)),
        ],
        compiler_params=pltpu.CompilerParams(vmem_limit_bytes=VMEM_LIMIT),
        cost_estimate=pl.CostEstimate(
            flops=6 * rows * width * width,
            bytes_accessed=10 * rows * width + 6 * width * width,
            transcendentals=0,
        ),
        name="input_gradient",
    )(rank, dh, dq, dk, dv, dlow, factors, *shards)


def update_kernel(near_ref, far_ref, fac_ref, first_ref, second_ref, *outs):
    grad_ref, new_ref, new_first_ref, new_second_ref = outs
    grad = near_ref[...].astype(F32) + far_ref[...].astype(F32)
    grad_ref[...] = grad
    clip = jnp.minimum(1.0, 1.0 / (jnp.sqrt(jnp.sum(grad * grad)) + 1e-06))
    clipped = grad * clip
    new_first = 0.9 * first_ref[...] + 0.1 * clipped
    new_second = 0.999 * second_ref[...] + 0.001 * clipped * clipped
    new_first_ref[...] = new_first
    new_second_ref[...] = new_second
    factors = fac_ref[...]
    row = lax.broadcasted_iota(jnp.int32, factors.shape, 0)
    rate = jnp.where(row < 2 * ADAPTER_RANK, rate_low, rate_high)
    fix_first = 1.0 - 0.9**STEP
    fix_second = 1.0 - 0.999**STEP
    step = new_first / fix_first / (jnp.sqrt(new_second / fix_second) + 1e-08)
    new_ref[...] = factors - rate * (step + decay_rate * factors)


def update(near, far, factors, first, second):
    return pl.pallas_call(
        update_kernel,
        out_shape=[jax.ShapeDtypeStruct(factors.shape, F32)] * 4,
        name="adapter_update",
    )(near, far, factors, first, second)


def swap(value, axis, size, flip):
    return lax.ppermute(value, axis, [(i, i ^ flip) for i in range(size)])


def bits(size):
    return [1 << at for at in range(size.bit_length() - 1)]


def group_shards(shard, size):
    held = [shard]
    for flip in bits(size)[1:]:
        held += [swap(value, "rep", size, flip) for value in held]
    return [value for near in held for value in (near, swap(near, "rep", size, 1))]


def gather_moments(first, second, size):
    length = first.shape[0]
    place = lax.axis_index("wide")
    held = jnp.stack([first, second])
    for flip in bits(size):
        other = swap(held, "wide", size, flip)
        low = (place // flip) % 2 == 0
        held = jnp.where(
            low, jnp.concatenate([held, other], 1), jnp.concatenate([other, held], 1)
        )
    return (held[0], held[1])


def local(sizes, *args):
    (
        tokens,
        segment_ids,
        cotangent,
        w_query,
        w_key,
        w_value,
        w_output,
        w_inner,
        w_outer,
        b_query,
        b_value,
        b_output,
        b_inner,
        b_outer,
        norm1_gain,
        norm1_shift,
        norm2_gain,
        norm2_shift,
        factors,
        first_moment,
        second_moment,
    ) = args
    reps, wide = sizes
    width = tokens.shape[1]
    size = segment_ids.shape[1]
    flat = lambda vector: vector.reshape(1, -1)
    rank = lax.axis_index("rep").reshape(1)
    table = factors.reshape(4 * ADAPTER_RANK, width)
    qkv = group_shards(jnp.concatenate([w_query, w_key, w_value], 1), reps)
    ahead = group_shards(jnp.concatenate([w_output, w_inner], 1), reps)
    outer = group_shards(w_outer, reps)
    first, second = gather_moments(first_moment, second_moment, wide)
    q, k, v, ctx, aug, down = attend(
        rank, segment_ids, tokens, table, flat(b_query), flat(b_value), qkv, 3
    )
    vectors = [
        flat(vector)
        for vector in (
            b_output,
            b_inner,
            b_outer,
            norm1_gain,
            norm1_shift,
            norm2_gain,
            norm2_shift,
        )
    ]
    layer_out, dh, dctx = dense(rank, tokens, ctx, cotangent, vectors, ahead, outer, size, 1024)
    dq, dk, dv, dlow, grad = attend_back(
        segment_ids, tokens, table, down, q, k, v, dctx, ctx, aug, 3
    )
    input_grad = input_back(rank, dh, dq, dk, dv, dlow, table, qkv, size)
    rounds = [("rep", reps, flip) for flip in bits(reps)]
    rounds += [("wide", wide, flip) for flip in bits(wide)]
    for axis, count, flip in rounds[:-1]:
        grad = grad + swap(grad, axis, count, flip)
    axis, count, flip = rounds[-1]
    new = update(
        grad,
        swap(grad, axis, count, flip),
        table,
        first.reshape(table.shape),
        second.reshape(table.shape),
    )
    length = first_moment.shape[0]
    start = lax.axis_index("wide") * length
    whole_grad, new_factors, new_first, new_second = [value.reshape(-1) for value in new]
    mine = lambda value: lax.dynamic_slice_in_dim(value, start, length)
    return (
        layer_out,
        input_grad,
        mine(whole_grad),
        new_factors,
        mine(new_first),
        mine(new_second),
    )


def solution(mesh):
    rows = P(("rep", "wide"), None)
    shard = P("rep", None)
    piece = P("wide")
    placed = (rows,) * 3 + (shard,) * 6 + (P(),) * 10 + (piece,) * 2
    return jax.shard_map(
        functools.partial(local, (mesh.shape["rep"], mesh.shape["wide"])),
        mesh=mesh,
        in_specs=placed,
        out_specs=(rows, rows, piece, P(), piece, piece),
        check_vma=False,
    )
```

```python
import functools

import jax
import jax.numpy as jnp
from jax import lax
from jax.experimental import pallas as pl
from jax.experimental.pallas import tpu as pltpu
from jax.sharding import PartitionSpec as P

HEADS = 12
ADAPTER_RANK = 8
STEP = 10
LANES = 128
MASKED = 1e30

rate_low = 0.015
rate_high = 0.24
decay_rate = 0.01

BF16 = jnp.bfloat16
F32 = jnp.float32
NN = (((1,), (0,)), ((), ()))
NT = (((1,), (1,)), ((), ()))
TN = (((0,), (0,)), ((), ()))
ANY = pl.BlockSpec(memory_space=pl.ANY)
HBM = pl.BlockSpec(memory_space=pltpu.HBM)
VMEM_LIMIT = 56 * 2**20
INPUT_VMEM = 24 * 2**20
BACK_VMEM = 44 * 2**20
GATE = 5 * 10**9


def dot(left, right, dims):
    return lax.dot_general(left, right, dims, preferred_element_type=F32)


def beside(*parts):
    return jnp.concatenate(parts, axis=1)


def mean(value):
    return jnp.mean(value, -1, keepdims=True)


def layer_norm(hidden):
    centre = hidden - mean(hidden)
    rstd = lax.rsqrt(mean(centre * centre) + 1e-05)
    return (centre * rstd, rstd)


def norm_back(grad, normal, rstd, gain):
    scaled = grad * gain
    return rstd * (scaled - mean(scaled) - normal * mean(scaled * normal))


def gelu_pair(value):
    below = 0.5 + 0.5 * lax.erf(value * 2.0 ** (-0.5))
    density = jnp.exp(-0.5 * value * value) * 0.3989422804014327
    return (value * below, below + value * density)


def adapter_rows(lines_ref, first, count, width):
    step = width // LANES
    return beside(
        *[lines_ref[pl.ds(first * step + at, count, stride=step), :] for at in range(step)]
    )


def three_parts(value):
    high = value.astype(BF16).astype(F32)
    rest = value - high
    middle = rest.astype(BF16).astype(F32)
    return (high, middle, rest - middle)


def rows_at(rank, flip, side, rows):
    return pl.multiple_of((jnp.bitwise_xor(rank, flip) * 2 + side) * rows, 16)


def side_of(place):
    return jnp.bitwise_and(jnp.bitwise_xor(place, place >> 1), 1)


class Parts:
    def __init__(self, own, blocks, near, others):
        self.own, self.blocks, self.near = own, blocks, near
        self.flips = [flip for flip, _ in others]
        self.operands = list(own) + [near] + [piece for _, piece in others]
        self.copies = len(blocks) * (3 + len(others))

    def into(self, refs, rank, place, views, semaphores):
        count = len(self.own)
        own, near, others = refs[:count], refs[count], refs[count + 1 :]
        rows, width = near.shape[2:]
        mine = side_of(place)
        found = []
        for at, ((source, start), view) in enumerate(zip(self.blocks, views)):
            whole = own[source].at[:, pl.ds(start, width)]
            found.append((whole, view(rows_at(rank, 0, 0, rows), 2 * rows)))
            for side in range(2):
                found.append((near.at[side, at], view(rows_at(rank, 1, side, rows), rows)))
            for (flip, other), ref in zip(self.flips, others):
                if other is None:
                    target = view(rows_at(rank, flip, 0, rows), 2 * rows)
                else:
                    target = view(rows_at(rank, flip, jnp.bitwise_xor(mine, other), rows), rows)
                found.append((ref.at[at], target))
        return [
            pltpu.make_async_copy(source, target, semaphores.at[at])
            for at, (source, target) in enumerate(found)
        ]


def stacked(weights):
    def view(at):
        return lambda row, rows: weights.at[at, pl.ds(row, rows)]

    return [view(at) for at in range(weights.shape[0])]


def in_columns(weights, width):
    def view(start):
        return lambda row, rows: weights.at[pl.ds(row, rows), start : start + width]

    return [view(start) for start in range(0, weights.shape[1], width)]


def run_copies(copies):
    for copy in copies:
        copy.start()
    for copy in copies:
        copy.wait()


def pack_kernel(sets, count, place_ref, *rest):
    sources, rest = rest[:count], rest[count:]
    outs, rest = rest[: 2 * len(sets)], rest[2 * len(sets) :]
    holds, (arrive, leave) = rest[:-2], rest[-2:]
    side = side_of(place_ref[0])
    incoming, outgoing = [], []
    copy = pltpu.make_async_copy
    for blocks, near_ref, mine_ref, hold in zip(sets, outs[::2], outs[1::2], holds):
        rows, width = mine_ref.shape[1:]
        for block, (source, first) in enumerate(blocks):
            for half in range(2):
                part = sources[source].at[pl.ds(half * rows, rows), pl.ds(first, width)]
                incoming.append(copy(part, hold.at[half, block], arrive.at[len(incoming)]))
        outgoing.append((len(incoming), copy(hold.at[side], mine_ref, leave.at[len(outgoing)])))
        outgoing.append((len(incoming), copy(hold, near_ref, leave.at[len(outgoing)])))
    for one in incoming:
        one.start()
    done = 0
    for needed, one in outgoing:
        for other in incoming[done:needed]:
            other.wait()
        done = needed
        one.start()
    for _, one in outgoing:
        one.wait()


def pack(place, shards, sets):
    shapes = []
    holds = []
    copies = 0
    for blocks, width in sets:
        rows = shards[blocks[0][0]].shape[0] // 2
        holds.append((2, len(blocks), rows, width))
        shapes += [holds[-1], holds[-1][1:]]
        copies += 2 * len(blocks)
    found = pl.pallas_call(
        functools.partial(pack_kernel, [blocks for blocks, _ in sets], len(shards)),
        in_specs=[pl.BlockSpec(memory_space=pltpu.SMEM)] + [HBM] * len(shards),
        out_specs=[HBM] * len(shapes),
        out_shape=[jax.ShapeDtypeStruct(shape, BF16) for shape in shapes],
        scratch_shapes=[pltpu.VMEM(shape, BF16) for shape in holds]
        + [pltpu.SemaphoreType.DMA((copies,)), pltpu.SemaphoreType.DMA((len(shapes),))],
        compiler_params=pltpu.CompilerParams(vmem_limit_bytes=VMEM_LIMIT),
        name="pack_shards",
    )(place, *shards)
    return list(zip(found[::2], found[1::2]))


def attend_kernel(parts, rank_ref, place_ref, seg_ref, x_ref, fac_ref, bq_ref, bv_ref, *rest):
    shards, rest = rest[: len(parts.operands)], rest[len(parts.operands) :]
    q_ref, k_ref, v_ref, ctx_ref, aug_ref, down_ref, weights, bias, table, semaphores = rest
    at = pl.program_id(1)
    width = q_ref.shape[1]
    rows = x_ref.shape[0]

    @pl.when((pl.program_id(0) == 0) & (at == 0))
    def _():
        run_copies(parts.into(shards, rank_ref[0], place_ref[0], stacked(weights), semaphores))
        bias[0:1, :] = bq_ref[...].reshape(1, -1)
        bias[1:2, :] = bv_ref[...].reshape(1, -1)
        table[...] = adapter_rows(fac_ref, 0, *table.shape)

    rank2 = 2 * ADAPTER_RANK
    columns = pl.ds(pl.multiple_of(at * width, LANES), width)
    x = x_ref[...]
    low = dot(x, table[0:rank2, :].astype(BF16), NT).astype(BF16)
    down_ref[...] = low
    up = table[rank2 : 2 * rank2, columns]
    row = lax.broadcasted_iota(jnp.int32, up.shape, 0)
    up_q = jnp.where(row < ADAPTER_RANK, up, 0.0).astype(BF16)
    up_v = jnp.where(row < ADAPTER_RANK, 0.0, up).astype(BF16)
    q_ref[...] = (dot(x, weights[0, :, columns], NN) + bias[0:1, columns] + 2.0 * dot(low, up_q, NN)).astype(BF16)
    k_ref[...] = dot(x, weights[1, :, columns], NN).astype(BF16)
    v_ref[...] = (dot(x, weights[2, :, columns], NN) + bias[1:2, columns] + 2.0 * dot(low, up_v, NN)).astype(BF16)

    lane = lax.broadcasted_iota(jnp.int32, (rows, LANES), 1)
    seg = seg_ref[pl.ds(pl.program_id(0), 1), :].astype(F32).T.astype(jnp.int32)
    own = jnp.where(lane == seg, 1.0, 0.0)
    aug_k = jnp.where((lane < 4) & (lane != seg), -MASKED, 0.0).astype(BF16)
    aug_q = own.astype(BF16)
    ones = jnp.ones((rows, LANES), BF16)
    half = LANES // 2
    scale = BF16(half ** (-0.5))
    for pair in range(width // LANES):
        here = slice(LANES * pair, LANES * (pair + 1))
        keys = beside(k_ref[:, here], aug_k)
        values = beside(v_ref[:, here], ones)
        query = q_ref[:, here] * scale
        out = None
        for side in range(2):
            mask = (lane // half) == side
            scores = dot(beside(jnp.where(mask, query, BF16(0)), aug_q), keys, NT)
            top = jnp.max(scores, axis=1, keepdims=True)
            expo = jnp.exp(scores - top).astype(BF16)
            both = dot(expo, values, NN)
            sums = both[:, LANES:]
            ctx = both[:, :LANES] / sums
            out = ctx if side == 0 else jnp.where(mask, ctx, out)
            high, middle, little = three_parts(-(top + jnp.log(sums)))
            aug = jnp.where(
                lane == 4, high, jnp.where(lane == 5, middle, jnp.where(lane == 6, little, own))
            )
            aug_ref[:, (2 * pair + side) * LANES : (2 * pair + side + 1) * LANES] = aug.astype(BF16)
        ctx_ref[:, here] = out.astype(BF16)


def attend(rank, place, seg, x, factors, bq, bv, parts, pairs):
    packs, size = seg.shape
    rows, width = x.shape
    cut = pairs * LANES
    block = pl.BlockSpec((size, cut), lambda p, g: (p, g))
    vmem = pl.BlockSpec(memory_space=pltpu.VMEM)
    smem = pl.BlockSpec(memory_space=pltpu.SMEM)
    like = jax.ShapeDtypeStruct
    return pl.pallas_call(
        functools.partial(attend_kernel, parts),
        grid=(packs, width // cut),
        in_specs=[
            smem,
            smem,
            pl.BlockSpec(memory_space=pltpu.VMEM),
            pl.BlockSpec((size, width), lambda p, g: (p, 0)),
            vmem,
            vmem,
            vmem,
        ]
        + [ANY] * len(parts.operands),
        out_specs=[
            block,
            block,
            block,
            block,
            pl.BlockSpec((size, 2 * cut), lambda p, g: (p, g)),
            pl.BlockSpec((size, 2 * ADAPTER_RANK), lambda p, g: (p, 0)),
            pl.BlockSpec((3, width, width), lambda p, g: (0, 0, 0)),
        ],
        out_shape=[like((rows, width), BF16)] * 4
        + [
            like((rows, 2 * width), BF16),
            like((rows, 2 * ADAPTER_RANK), BF16),
            like((3, width, width), BF16),
        ],
        scratch_shapes=[
            pltpu.VMEM((8, width), F32),
            pltpu.VMEM((4 * ADAPTER_RANK, width), F32),
            pltpu.SemaphoreType.DMA((parts.copies,)),
        ],
        compiler_params=pltpu.CompilerParams(vmem_limit_bytes=VMEM_LIMIT),
        cost_estimate=pl.CostEstimate(flops=1, bytes_accessed=1, transcendentals=0),
        name="project_and_attend",
    )(rank, place, seg, x, factors, bq, bv, *parts.operands)


def dense_kernel(first, second, cut, rank_ref, place_ref, x_ref, ctx_ref, cot_ref, *rest):
    vectors, rest = rest[:7], rest[7:]
    bo_ref, bi_ref, bo2_ref, g1_ref, s1_ref, g2_ref, s2_ref = vectors
    one, two = len(first.operands), len(second.operands)
    near, far, rest = rest[:one], rest[one : one + two], rest[one + two :]
    out_ref, dh_ref, dctx_ref, ahead, outer, slope, semaphores = rest
    width = x_ref.shape[1]
    hidden = outer.shape[0]

    at = pl.program_id(0)
    rank, place = rank_ref[0], place_ref[0]
    start = first.into(near, rank, place, in_columns(ahead, width), semaphores.at[0])
    later = second.into(far, rank, place, in_columns(outer, width), semaphores.at[1])
    count = len(start) // len(first.blocks)
    start, later = start[:count], start[count:] + later

    @pl.when(at == 0)
    def _():
        for copy in start + later:
            copy.start()
        for copy in start:
            copy.wait()

    row = lambda ref: ref[...].reshape(1, -1)
    wo = lambda: ahead[:, :width]
    w1 = lambda j: ahead[:, width + j : width + j + cut]
    inner_bias = row(bi_ref)
    h1 = x_ref[...].astype(F32) + dot(ctx_ref[...], wo(), NN) + row(bo_ref)
    norm1, rstd1 = layer_norm(h1)
    y1 = norm1 * row(g1_ref) + row(s1_ref)
    y1_low = y1.astype(BF16)

    @pl.when(at == 0)
    def _():
        for copy in later:
            copy.wait()

    h2 = y1 + row(bo2_ref)
    for j in range(0, hidden, cut):
        inner = dot(y1_low, w1(j), NN) + inner_bias[:, j : j + cut]
        act, gradient = gelu_pair(inner)
        slope[:, j : j + cut] = gradient
        h2 = h2 + dot(act.astype(BF16), outer[j : j + cut, :], NN)
    norm2, rstd2 = layer_norm(h2)
    out_ref[...] = (norm2 * row(g2_ref) + row(s2_ref)).astype(BF16)
    dh2 = norm_back(cot_ref[...].astype(F32), norm2, rstd2, row(g2_ref))
    df = dh2.astype(BF16)
    dy1 = dh2
    for j in range(0, hidden, cut):
        du = (dot(df, outer[j : j + cut, :], NT) * slope[:, j : j + cut]).astype(BF16)
        dy1 = dy1 + dot(du, w1(j), NT)
    dh1 = norm_back(dy1, norm1, rstd1, row(g1_ref)).astype(BF16)
    dh_ref[...] = dh1
    dctx_ref[...] = dot(dh1, wo(), NT).astype(BF16)


def dense(rank, place, x, ctx, cot, vectors, first, second, size, cut):
    rows, width = x.shape
    hidden = vectors[1].shape[0]
    block = pl.BlockSpec((size, width), lambda i: (i, 0))
    smem = pl.BlockSpec(memory_space=pltpu.SMEM)
    return pl.pallas_call(
        functools.partial(dense_kernel, first, second, cut),
        grid=(rows // size,),
        in_specs=[smem, smem, block, block, block]
        + [pl.BlockSpec(memory_space=pltpu.VMEM)] * len(vectors)
        + [ANY] * (len(first.operands) + len(second.operands)),
        out_specs=[block] * 3,
        out_shape=[jax.ShapeDtypeStruct((rows, width), BF16)] * 3,
        scratch_shapes=[
            pltpu.VMEM((width, width + hidden), BF16),
            pltpu.VMEM((hidden, width), BF16),
            pltpu.VMEM((size, hidden), F32),
            pltpu.SemaphoreType.DMA((2, max(first.copies, second.copies))),
        ],
        compiler_params=pltpu.CompilerParams(vmem_limit_bytes=VMEM_LIMIT),
        cost_estimate=pl.CostEstimate(
            flops=rows * width * (4 * width + 8 * hidden),
            bytes_accessed=12 * rows * width + 4 * width * hidden,
            transcendentals=2 * rows * hidden,
        ),
        name="dense_both_ways",
    )(rank, place, x, ctx, cot, *vectors, *first.operands, *second.operands)


def attend_back_kernel(seg_ref, x_ref, fac_ref, down_ref, *rest):
    q_ref, k_ref, v_ref, dctx_ref, ctx_ref, aug_ref, *rest = rest
    dq_ref, dk_ref, dv_ref, dlow_ref, grad_ref, low, total, table = rest
    pack, at = pl.program_id(0), pl.program_id(1)
    rows, width = q_ref.shape
    rank2 = 2 * ADAPTER_RANK
    columns = pl.ds(pl.multiple_of(at * width, LANES), width)

    @pl.when((pack == 0) & (at == 0))
    def _():
        table[...] = adapter_rows(fac_ref, 0, *table.shape)

    lane = lax.broadcasted_iota(jnp.int32, (rows, LANES), 1)
    seg = seg_ref[pl.ds(pl.program_id(0), 1), :].astype(F32).T.astype(jnp.int32)
    aug_k = jnp.where(
        (lane < 4) & (lane != seg), -MASKED, jnp.where((lane >= 4) & (lane < 7), 1.0, 0.0)
    ).astype(BF16)
    aug_v = jnp.where(lane < 3, 1.0, 0.0).astype(BF16)
    zero = BF16(0)
    half = LANES // 2
    scale = BF16(half ** (-0.5))
    for pair in range(width // LANES):
        here = slice(LANES * pair, LANES * (pair + 1))
        key = k_ref[:, here]
        query = q_ref[:, here] * scale
        grad = dctx_ref[:, here]
        keys = beside(key, aug_k)
        values = beside(v_ref[:, here], aug_v)
        key = key * scale
        product = grad.astype(F32) * ctx_ref[:, here].astype(F32)
        dq = dk = dv = 0.0
        for side in range(2):
            mask = (lane // half) == side
            one_query = jnp.where(mask, query, zero)
            one_grad = jnp.where(mask, grad, zero)
            one_key = jnp.where(mask, key, zero)
            inner = -jnp.sum(jnp.where(mask, product, 0.0), axis=1, keepdims=True)
            high, middle, little = three_parts(inner)
            aug_d = jnp.where(
                lane == 0, high, jnp.where(lane == 1, middle, jnp.where(lane == 2, little, 0.0))
            ).astype(BF16)
            aug_q = aug_ref[:, (2 * pair + side) * LANES : (2 * pair + side + 1) * LANES]
            probs = jnp.exp(dot(keys, beside(one_query, aug_q), NT))
            dprobs = dot(values, beside(one_grad, aug_d), NT)
            dscores = (probs * dprobs).astype(BF16)
            dv = dv + dot(probs.astype(BF16), one_grad, NN)
            dk = dk + dot(dscores, one_query, NN)
            dq = dq + dot(dscores, one_key, TN)
        dq_ref[:, here] = dq.astype(BF16)
        dk_ref[:, here] = dk.astype(BF16)
        dv_ref[:, here] = dv.astype(BF16)

    up = table[rank2 : 2 * rank2, columns]
    row = lax.broadcasted_iota(jnp.int32, up.shape, 0)
    up_q = jnp.where(row < ADAPTER_RANK, up, 0.0).astype(BF16)
    up_v = jnp.where(row < ADAPTER_RANK, 0.0, up).astype(BF16)
    dlow = dot(dq_ref[...], up_q, NT) + dot(dv_ref[...], up_v, NT)
    low[...] = dlow + jnp.where(at == 0, 0.0, low[...])
    down = down_ref[...]
    from_q = dot(down, dq_ref[...], TN)
    from_v = dot(down, dv_ref[...], TN)
    share = 2.0 * jnp.where(row < ADAPTER_RANK, from_q, from_v)
    later = pack > 0
    total[rank2 : 2 * rank2, columns] = share + jnp.where(
        later, total[rank2 : 2 * rank2, columns], 0.0
    )

    @pl.when(at == pl.num_programs(1) - 1)
    def _():
        dlow_low = (2.0 * low[...]).astype(BF16)
        dlow_ref[...] = dlow_low
        total[0:rank2, :] = dot(dlow_low, x_ref[...], TN) + jnp.where(
            later, total[0:rank2, :], 0.0
        )
        grad_ref[...] = total[...].astype(BF16)


def attend_back(seg, x, factors, down, q, k, v, dctx, ctx, aug, pairs):
    packs, size = seg.shape
    rows, width = x.shape
    cut = pairs * LANES
    rank2 = 2 * ADAPTER_RANK
    block = pl.BlockSpec((size, cut), lambda p, g: (p, g))
    whole = lambda shape: pl.BlockSpec(shape, lambda p, g: (0, 0), pipeline_mode=pl.Buffered(1))
    like = jax.ShapeDtypeStruct
    return pl.pallas_call(
        attend_back_kernel,
        grid=(packs, width // cut),
        in_specs=[
            pl.BlockSpec(memory_space=pltpu.VMEM),
            pl.BlockSpec((size, width), lambda p, g: (p, 0)),
            pl.BlockSpec(memory_space=pltpu.VMEM),
            pl.BlockSpec((size, rank2), lambda p, g: (p, 0)),
            block,
            block,
            block,
            block,
            block,
            pl.BlockSpec((size, 2 * cut), lambda p, g: (p, g)),
        ],
        out_specs=[
            block,
            block,
            block,
            pl.BlockSpec((size, rank2), lambda p, g: (p, 0)),
            whole((2 * rank2, width)),
        ],
        out_shape=[like((rows, width), BF16)] * 3
        + [like((rows, rank2), BF16), like((2 * rank2, width), BF16)],
        scratch_shapes=[pltpu.VMEM((size, rank2), F32)]
        + [pltpu.VMEM((2 * rank2, width), F32)] * 2,
        compiler_params=pltpu.CompilerParams(vmem_limit_bytes=BACK_VMEM),
        cost_estimate=pl.CostEstimate(
            flops=rows * width * 30 * size,
            bytes_accessed=24 * rows * width,
            transcendentals=rows * size * HEADS,
        ),
        name="attend_back",
    )(seg, x, factors, down, q, k, v, dctx, ctx, aug)


def input_kernel(first, dh_ref, dq_ref, dk_ref, dv_ref, dlow_ref, fac_ref, weights, *rest):
    out_ref = rest[-1]
    size, width = out_ref.shape
    block = slice(first, first + size)
    down = adapter_rows(fac_ref, 0, 2 * ADAPTER_RANK, width).astype(BF16)
    total = dh_ref[block, :].astype(F32) + dot(dlow_ref[block, :], down, NN)
    for at, grad in enumerate((dq_ref, dk_ref, dv_ref)):
        total = total + dot(grad[block, :], weights[at], NT)
    out_ref[...] = total.astype(BF16)


def input_back(dh, dq, dk, dv, dlow, factors, weights, size, at, carry):
    rows, width = dh.shape
    vmem = pl.BlockSpec(memory_space=pltpu.VMEM)
    return pl.pallas_call(
        functools.partial(input_kernel, at * size),
        grid=(1,),
        in_specs=[vmem] * 7 + [ANY] * len(carry),
        out_specs=pl.BlockSpec((size, width), lambda i: (at, 0)),
        out_shape=jax.ShapeDtypeStruct((rows, width), BF16),
        input_output_aliases={7 + i: i for i in range(len(carry))},
        compiler_params=pltpu.CompilerParams(vmem_limit_bytes=INPUT_VMEM),
        cost_estimate=pl.CostEstimate(
            flops=6 * size * width * width,
            bytes_accessed=10 * size * width,
            transcendentals=0,
        ),
        name="input_gradient",
    )(dh, dq, dk, dv, dlow, factors, weights, *carry)


def update_kernel(place_ref, near_ref, far_ref, fac_ref, held_ref, other_ref, *rest):
    grad_ref, new_ref, new_first_ref, new_second_ref, lines, table, first, second = rest
    place = place_ref[0]
    owners, length, lanes = fac_ref.shape
    grad = near_ref[...].astype(F32) + far_ref[...].astype(F32)
    rows, width = grad.shape
    step = width // lanes
    for at in range(step):
        lines[pl.ds(at, rows, stride=step), :] = grad[:, at * lanes : (at + 1) * lanes]
    for owner in range(owners):
        table[owner] = lines[owner * length : (owner + 1) * length, :]
    half = owners // 2
    for at in range(owners):
        ref = held_ref if at < half else other_ref
        owner = jnp.bitwise_xor(place, at)
        first[owner] = ref[at % half, 0]
        second[owner] = ref[at % half, 1]
    clip = jnp.minimum(1.0, 1.0 / (jnp.sqrt(jnp.sum(grad * grad)) + 1e-06))
    clipped = table[...] * clip
    new_first = 0.9 * first[...] + 0.1 * clipped
    new_second = 0.999 * second[...] + 0.001 * clipped * clipped
    first[...] = new_first
    second[...] = new_second
    grad_ref[...] = table[place]
    new_first_ref[...] = first[place]
    new_second_ref[...] = second[place]
    factors = fac_ref[...]
    owner = lax.broadcasted_iota(jnp.int32, factors.shape, 0)
    rate = jnp.where(owner < half, rate_low, rate_high)
    fix_first = 1.0 - 0.9**STEP
    fix_second = 1.0 - 0.999**STEP
    move = new_first / fix_first / (jnp.sqrt(new_second / fix_second) + 1e-08)
    new_ref[...] = factors - rate * (move + decay_rate * factors)


def update(place, near, far, factors, held, other):
    like = lambda shape: jax.ShapeDtypeStruct(shape, F32)
    owners, length, lanes = factors.shape
    vmem = pl.BlockSpec(memory_space=pltpu.VMEM)
    piece = like((length, lanes))
    return pl.pallas_call(
        update_kernel,
        in_specs=[pl.BlockSpec(memory_space=pltpu.SMEM)] + [vmem] * 5,
        out_shape=[piece, like(factors.shape), piece, piece],
        scratch_shapes=[pltpu.VMEM((owners * length, lanes), F32)]
        + [pltpu.VMEM(factors.shape, F32)] * 3,
        name="adapter_update",
    )(place, near, far, factors, held, other)


def bits(size):
    return [1 << at for at in range(size.bit_length() - 1)]


def swap(value, axis, size, flip):
    return lax.ppermute(value, axis, [(i, i ^ flip) for i in range(size)])


def cross(value, reps, wide):
    pairs = []
    for rank in range(reps):
        for place in range(wide):
            other = place ^ (1 if rank % 2 == 0 else 2)
            pairs.append((rank * wide + place, rank * wide + other))
    return lax.ppermute(value, ("rep", "wide"), pairs)


def fetch(mine, reps):
    held = [(0, mine)]
    for flip in bits(reps)[1:]:
        held += [(have ^ flip, swap(value, "rep", reps, flip)) for have, value in held]
    return held[1:]


def both_cores(halves, reps):
    return [
        ((flip ^ core, other), swap(value, "rep", reps, 1) if core else value)
        for (flip, other), value in halves
        for core in range(2)
    ]


def finish(own, blocks, near, halves, crossed, reps):
    pieces = [((flip, 0), value) for flip, value in halves]
    pieces += [((flip, 1), value) for flip, value in crossed]
    return Parts(own, blocks, swap(near, "rep", reps, 1), both_cores(pieces, reps))


def across(halves, reps, wide):
    return [(flip, cross(value, reps, wide)) for flip, value in halves]


def together(*values):
    return lax.optimization_barrier(values)


def gate_kernel(value_ref, other_ref, out_ref):
    pass


def gate(value, other, flops=10**11):
    return pl.pallas_call(
        gate_kernel,
        in_specs=[ANY, ANY],
        out_specs=ANY,
        out_shape=jax.ShapeDtypeStruct(value.shape, value.dtype),
        input_output_aliases={0: 0},
        cost_estimate=pl.CostEstimate(flops=flops, bytes_accessed=1, transcendentals=0),
        name="gate",
    )(value, other)


def local(sizes, *args):
    (
        tokens,
        segment_ids,
        cotangent,
        w_query,
        w_key,
        w_value,
        w_output,
        w_inner,
        w_outer,
        b_query,
        b_value,
        *vectors,
        factors,
        first_moment,
        second_moment,
    ) = args
    reps, wide = sizes
    width = tokens.shape[1]
    packs, size = segment_ids.shape
    rank = lax.axis_index("rep").reshape(1)
    place = lax.axis_index("wide").reshape(1)
    table = factors.reshape(-1, LANES)

    hidden = w_inner.shape[1]
    own = [w_query, w_key, w_value]
    set_heads = [(at, 0) for at in range(3)]
    own_ahead = [w_output, w_inner]
    set_ahead = [(0, 0)] + [(1, start) for start in range(0, hidden, width)]
    near, mine = pack(place, own, [(set_heads, width)])[0]
    place, mine = together(place, mine)
    near_ahead, mine_ahead = pack(place, own_ahead, [(set_ahead, width)])[0]

    halves = fetch(mine, reps)
    length = first_moment.shape[0] // LANES
    held = jnp.stack([first_moment, second_moment]).reshape(1, 2, length, LANES)
    held, mine_ahead = together(held, mine_ahead)
    flips = bits(wide)
    held = jnp.concatenate([held, swap(held, "wide", wide, flips[0])])
    flip, sent = halves[-1]
    sent, mine_ahead, near, near_ahead, near_outer = together(
        sent, mine_ahead, near, near_ahead, w_outer
    )
    halves_ahead = fetch(mine_ahead, reps)
    sent = gate(sent, held)
    sent, whole_outer = together(sent, w_outer)
    whole_outer = fetch(whole_outer, reps)
    halves = halves[:-1] + [(flip, sent)]
    crossed = across(halves, reps, wide)
    heads = finish(own, set_heads, near, halves, crossed, reps)

    q, k, v, ctx, aug, down, weights = attend(
        rank, place, segment_ids, tokens, table, b_query, b_value, heads, 3
    )
    down, held, *values = together(down, held, *[value for _, value in halves_ahead])
    values = [gate(value, down, GATE) for value in values]
    halves_ahead = [(flip, value) for (flip, _), value in zip(halves_ahead, values)]
    for flip in flips[1:-1]:
        held = jnp.concatenate([held, swap(held, "wide", wide, flip)])
    other = swap(held, "wide", wide, flips[-1])
    crossed_ahead = across(halves_ahead, reps, wide)
    ahead = finish(own_ahead, set_ahead, near_ahead, halves_ahead, crossed_ahead, reps)
    whole = [(flip, value) for flip, value in whole_outer]
    near_outer = swap(near_outer, "rep", reps, 1)
    outer = Parts(
        [w_outer],
        [(0, 0)],
        near_outer.reshape(2, 1, -1, width),
        both_cores([((flip, None), value[None]) for flip, value in whole], reps),
    )
    layer_out, dh, dctx = dense(
        rank, place, tokens, ctx, cotangent, vectors, ahead, outer, size, 1024
    )
    dq, dk, dv, dlow, grad = attend_back(
        segment_ids, tokens, table, down, q, k, v, dctx, ctx, aug, 3
    )
    rounds = [("rep", reps, flip) for flip in bits(reps)]
    rounds += [("wide", wide, flip) for flip in bits(wide)]
    pieces = 4
    part = tokens.shape[0] // pieces
    input_grad = []
    for at, (axis, count, flip) in enumerate(rounds):
        far = swap(grad, axis, count, flip)
        start = at - (len(rounds) - pieces)
        if start >= 0:
            dh, grad = together(dh, grad)
            args = (dh, dq, dk, dv, dlow, table, weights, part, start)
            input_grad = [input_back(*args, input_grad)]
        if at < len(rounds) - 1:
            grad = grad + far
            if start >= 0:
                grad, *input_grad = together(grad, *input_grad)
    flat = factors.reshape(wide, length, LANES)
    new = update(place, grad, far, flat, held, other)
    piece, new_factors, new_first, new_second = [value.reshape(-1) for value in new]
    return (layer_out, input_grad[0], piece, new_factors, new_first, new_second)


def solution(mesh):
    rows = P(("rep", "wide"), None)
    shard = P("rep", None)
    piece = P("wide")
    placed = (rows,) * 3 + (shard,) * 6 + (P(),) * 10 + (piece,) * 2
    return jax.shard_map(
        functools.partial(local, (mesh.shape["rep"], mesh.shape["wide"])),
        mesh=mesh,
        in_specs=placed,
        out_specs=(rows, rows, piece, P(), piece, piece),
        check_vma=False,
    )
```

```python
import functools

import jax
import jax.numpy as jnp
from jax import lax
from jax.experimental import pallas as pl
from jax.experimental.pallas import tpu as pltpu
from jax.sharding import PartitionSpec as P

HEADS = 12
ADAPTER_RANK = 8
STEP = 10
LANES = 128
MASKED = 1e30

rate_low = 0.015
rate_high = 0.24
decay_rate = 0.01

BF16 = jnp.bfloat16
F32 = jnp.float32
NN = (((1,), (0,)), ((), ()))
NT = (((1,), (1,)), ((), ()))
TN = (((0,), (0,)), ((), ()))
ANY = pl.BlockSpec(memory_space=pl.ANY)
HBM = pl.BlockSpec(memory_space=pltpu.HBM)
VMEM_LIMIT = 56 * 2**20
INPUT_VMEM = 24 * 2**20
BACK_VMEM = 44 * 2**20
DENSE_VMEM = 56 * 2**20
ATTEND_VMEM = 56 * 2**20
GATE = 5 * 10**9


def dot(left, right, dims):
    return lax.dot_general(left, right, dims, preferred_element_type=F32)


def beside(*parts):
    return jnp.concatenate(parts, axis=1)


def mean(value):
    return jnp.mean(value, -1, keepdims=True)


def layer_norm(hidden):
    centre = hidden - mean(hidden)
    rstd = lax.rsqrt(mean(centre * centre) + 1e-05)
    return (centre * rstd, rstd)


def norm_back(grad, normal, rstd, gain):
    scaled = grad * gain
    return rstd * (scaled - mean(scaled) - normal * mean(scaled * normal))


def gelu_pair(value):
    below = 0.5 + 0.5 * lax.erf(value * 2.0 ** (-0.5))
    density = jnp.exp(-0.5 * value * value) * 0.3989422804014327
    return (value * below, below + value * density)


def adapter_rows(lines_ref, first, count, width):
    step = width // LANES
    return beside(
        *[lines_ref[pl.ds(first * step + at, count, stride=step), :] for at in range(step)]
    )


def three_parts(value):
    high = value.astype(BF16).astype(F32)
    rest = value - high
    middle = rest.astype(BF16).astype(F32)
    return (high, middle, rest - middle)


def rows_at(rank, flip, side, rows):
    return pl.multiple_of((jnp.bitwise_xor(rank, flip) * 2 + side) * rows, 16)


def side_of(place):
    return jnp.bitwise_and(jnp.bitwise_xor(place, place >> 1), 1)


class Parts:
    def __init__(self):
        self.operands, self.places = [], []

    def add(self, array, *places):
        self.places += [(len(self.operands),) + place for place in places]
        self.operands.append(array)

    @property
    def copies(self):
        return len(self.places)

    def into(self, refs, rank, place, views, semaphores):
        mine = side_of(place)
        found = [[] for _ in views]
        for at, (operand, index, block, flip, side, rows, halves) in enumerate(self.places):
            source = refs[operand].at[index] if index else refs[operand]
            if isinstance(side, tuple):
                side = jnp.bitwise_xor(mine, side[0])
            target = views[block](rows_at(rank, flip, side, rows), rows * halves)
            found[block].append(pltpu.make_async_copy(source, target, semaphores.at[at]))
        return found


def stacked(weights):
    def view(at):
        return lambda row, rows: weights.at[at, pl.ds(row, rows)]

    return [view(at) for at in range(weights.shape[0])]


def in_columns(weights, width):
    def view(start):
        return lambda row, rows: weights.at[pl.ds(row, rows), start : start + width]

    return [view(start) for start in range(0, weights.shape[1], width)]


def run_copies(copies):
    for copy in copies:
        copy.start()
    for copy in copies:
        copy.wait()


def pack_kernel(sets, count, place_ref, *rest):
    sources, rest = rest[:count], rest[count:]
    outs, rest = rest[: 2 * len(sets)], rest[2 * len(sets) :]
    holds, (arrive, leave) = rest[:-2], rest[-2:]
    side = side_of(place_ref[0])
    incoming, outgoing = [], []
    copy = pltpu.make_async_copy
    for blocks, near_ref, mine_ref, hold in zip(sets, outs[::2], outs[1::2], holds):
        rows, width = mine_ref.shape[1:]
        for block, (source, first) in enumerate(blocks):
            for half in range(2):
                part = sources[source].at[pl.ds(half * rows, rows), pl.ds(first, width)]
                incoming.append(copy(part, hold.at[half, block], arrive.at[len(incoming)]))
        outgoing.append((len(incoming), copy(hold.at[side], mine_ref, leave.at[len(outgoing)])))
        outgoing.append((len(incoming), copy(hold, near_ref, leave.at[len(outgoing)])))
    for one in incoming:
        one.start()
    done = 0
    for needed, one in outgoing:
        for other in incoming[done:needed]:
            other.wait()
        done = needed
        one.start()
    for _, one in outgoing:
        one.wait()


def pack(place, shards, sets):
    shapes = []
    holds = []
    copies = 0
    for blocks, width in sets:
        rows = shards[blocks[0][0]].shape[0] // 2
        holds.append((2, len(blocks), rows, width))
        shapes += [holds[-1], holds[-1][1:]]
        copies += 2 * len(blocks)
    found = pl.pallas_call(
        functools.partial(pack_kernel, [blocks for blocks, _ in sets], len(shards)),
        in_specs=[pl.BlockSpec(memory_space=pltpu.SMEM)] + [HBM] * len(shards),
        out_specs=[HBM] * len(shapes),
        out_shape=[jax.ShapeDtypeStruct(shape, BF16) for shape in shapes],
        scratch_shapes=[pltpu.VMEM(shape, BF16) for shape in holds]
        + [pltpu.SemaphoreType.DMA((copies,)), pltpu.SemaphoreType.DMA((len(shapes),))],
        compiler_params=pltpu.CompilerParams(vmem_limit_bytes=VMEM_LIMIT),
        name="pack_shards",
    )(place, *shards)
    return list(zip(found[::2], found[1::2]))


def attend_kernel(parts, first, rank_ref, place_ref, seg_ref, x_ref, fac_ref, bq_ref, bv_ref, *rest):
    at = pl.program_id(1)
    begin = (pl.program_id(0) == 0) & (at == 0)
    if parts is None:
        weights, rest = rest[0], rest[7:]
        q_ref, k_ref, v_ref, ctx_ref, aug_ref, down_ref, bias, table = rest
    else:
        shards, rest = rest[: len(parts.operands)], rest[len(parts.operands) :]
        q_ref, k_ref, v_ref, ctx_ref, aug_ref, down_ref, weights, bias, table, semaphores = rest

        @pl.when(begin)
        def _():
            blocks = parts.into(shards, rank_ref[0], place_ref[0], stacked(weights), semaphores)
            run_copies(sum(blocks, []))

    width = q_ref.shape[1]
    rows = x_ref.shape[0]

    @pl.when(begin)
    def _():
        bias[0:1, :] = bq_ref[...].reshape(1, -1)
        bias[1:2, :] = bv_ref[...].reshape(1, -1)
        table[...] = adapter_rows(fac_ref, 0, *table.shape)

    rank2 = 2 * ADAPTER_RANK
    columns = pl.ds(pl.multiple_of(at * width, LANES), width)
    x = x_ref[...]
    low = dot(x, table[0:rank2, :].astype(BF16), NT).astype(BF16)
    down_ref[...] = low
    up = table[rank2 : 2 * rank2, columns]
    row = lax.broadcasted_iota(jnp.int32, up.shape, 0)
    up_q = jnp.where(row < ADAPTER_RANK, up, 0.0).astype(BF16)
    up_v = jnp.where(row < ADAPTER_RANK, 0.0, up).astype(BF16)
    q_ref[...] = (dot(x, weights[0, :, columns], NN) + bias[0:1, columns] + 2.0 * dot(low, up_q, NN)).astype(BF16)
    k_ref[...] = dot(x, weights[1, :, columns], NN).astype(BF16)
    v_ref[...] = (dot(x, weights[2, :, columns], NN) + bias[1:2, columns] + 2.0 * dot(low, up_v, NN)).astype(BF16)

    lane = lax.broadcasted_iota(jnp.int32, (rows, LANES), 1)
    seg = seg_ref[pl.ds(first + pl.program_id(0), 1), :].astype(F32).T.astype(jnp.int32)
    own = jnp.where(lane == seg, 1.0, 0.0)
    aug_k = jnp.where((lane < 4) & (lane != seg), -MASKED, 0.0).astype(BF16)
    aug_q = own.astype(BF16)
    ones = jnp.ones((rows, LANES), BF16)
    half = LANES // 2
    scale = BF16(half ** (-0.5))
    for pair in range(width // LANES):
        here = slice(LANES * pair, LANES * (pair + 1))
        keys = beside(k_ref[:, here], aug_k)
        values = beside(v_ref[:, here], ones)
        query = q_ref[:, here] * scale
        out = None
        for side in range(2):
            mask = (lane // half) == side
            scores = dot(beside(jnp.where(mask, query, BF16(0)), aug_q), keys, NT)
            top = jnp.max(scores, axis=1, keepdims=True)
            expo = jnp.exp(scores - top).astype(BF16)
            both = dot(expo, values, NN)
            sums = both[:, LANES:]
            ctx = both[:, :LANES] / sums
            out = ctx if side == 0 else jnp.where(mask, ctx, out)
            high, middle, little = three_parts(-(top + jnp.log(sums)))
            aug = jnp.where(
                lane == 4, high, jnp.where(lane == 5, middle, jnp.where(lane == 6, little, own))
            )
            aug_ref[:, (2 * pair + side) * LANES : (2 * pair + side + 1) * LANES] = aug.astype(BF16)
        ctx_ref[:, here] = out.astype(BF16)


def attend(rank, place, seg, x, factors, bq, bv, pairs, first, count, parts, weights=None, carry=()):
    packs, size = seg.shape
    rows, width = x.shape
    cut = pairs * LANES
    block = pl.BlockSpec((size, cut), lambda p, g: (first + p, g))
    vmem = pl.BlockSpec(memory_space=pltpu.VMEM)
    smem = pl.BlockSpec(memory_space=pltpu.SMEM)
    like = jax.ShapeDtypeStruct
    out_specs = [
        block,
        block,
        block,
        block,
        pl.BlockSpec((size, 2 * cut), lambda p, g: (first + p, g)),
        pl.BlockSpec((size, 2 * ADAPTER_RANK), lambda p, g: (first + p, 0)),
    ]
    out_shape = [like((rows, width), BF16)] * 4
    out_shape += [like((rows, 2 * width), BF16), like((rows, 2 * ADAPTER_RANK), BF16)]
    scratch = [pltpu.VMEM((8, width), F32), pltpu.VMEM((4 * ADAPTER_RANK, width), F32)]
    if parts is None:
        operands, specs = [weights, *carry], [vmem] + [ANY] * len(carry)
    else:
        operands, specs = parts.operands, [ANY] * len(parts.operands)
        out_specs.append(pl.BlockSpec((3, width, width), lambda p, g: (0, 0, 0)))
        out_shape.append(like((3, width, width), BF16))
        scratch.append(pltpu.SemaphoreType.DMA((parts.copies,)))
    return pl.pallas_call(
        functools.partial(attend_kernel, parts, first),
        grid=(count, width // cut),
        in_specs=[
            smem,
            smem,
            vmem,
            pl.BlockSpec((size, width), lambda p, g: (first + p, 0)),
            vmem,
            vmem,
            vmem,
        ]
        + specs,
        out_specs=out_specs,
        out_shape=out_shape,
        input_output_aliases={8 + at: at for at in range(len(carry))},
        scratch_shapes=scratch,
        compiler_params=pltpu.CompilerParams(vmem_limit_bytes=ATTEND_VMEM),
        cost_estimate=pl.CostEstimate(
            flops=1 if carry == () else 10**10, bytes_accessed=1, transcendentals=0
        ),
        name="project_and_attend",
    )(rank, place, seg, x, factors, bq, bv, *operands)


def dense_kernel(first, second, cut, rank_ref, place_ref, x_ref, ctx_ref, cot_ref, *rest):
    vectors, rest = rest[:7], rest[7:]
    bo_ref, bi_ref, bo2_ref, g1_ref, s1_ref, g2_ref, s2_ref = vectors
    one, two = len(first.operands), len(second.operands)
    near, far, rest = rest[:one], rest[one : one + two], rest[one + two :]
    out_ref, dh_ref, dctx_ref, ahead, outer, slope, semaphores = rest
    width = x_ref.shape[1]
    hidden = outer.shape[0]

    at = pl.program_id(0)
    rank, place = rank_ref[0], place_ref[0]
    start, *later = first.into(near, rank, place, in_columns(ahead, width), semaphores.at[0])
    later = sum(later + second.into(far, rank, place, in_columns(outer, width), semaphores.at[1]), [])

    @pl.when(at == 0)
    def _():
        for copy in start + later:
            copy.start()
        for copy in start:
            copy.wait()

    row = lambda ref: ref[...].reshape(1, -1)
    wo = lambda: ahead[:, :width]
    w1 = lambda j: ahead[:, width + j : width + j + cut]
    inner_bias = row(bi_ref)
    h1 = x_ref[...].astype(F32) + dot(ctx_ref[...], wo(), NN) + row(bo_ref)
    norm1, rstd1 = layer_norm(h1)
    y1 = norm1 * row(g1_ref) + row(s1_ref)
    y1_low = y1.astype(BF16)

    @pl.when(at == 0)
    def _():
        for copy in later:
            copy.wait()

    h2 = y1 + row(bo2_ref)
    for j in range(0, hidden, cut):
        inner = dot(y1_low, w1(j), NN) + inner_bias[:, j : j + cut]
        act, gradient = gelu_pair(inner)
        slope[:, j : j + cut] = gradient
        h2 = h2 + dot(act.astype(BF16), outer[j : j + cut, :], NN)
    norm2, rstd2 = layer_norm(h2)
    out_ref[...] = (norm2 * row(g2_ref) + row(s2_ref)).astype(BF16)
    dh2 = norm_back(cot_ref[...].astype(F32), norm2, rstd2, row(g2_ref))
    df = dh2.astype(BF16)
    dy1 = dh2
    for j in range(0, hidden, cut):
        du = (dot(df, outer[j : j + cut, :], NT) * slope[:, j : j + cut]).astype(BF16)
        dy1 = dy1 + dot(du, w1(j), NT)
    dh1 = norm_back(dy1, norm1, rstd1, row(g1_ref)).astype(BF16)
    dh_ref[...] = dh1
    dctx_ref[...] = dot(dh1, wo(), NT).astype(BF16)


def dense(rank, place, x, ctx, cot, vectors, first, second, size, cut):
    rows, width = x.shape
    hidden = vectors[1].shape[0]
    block = pl.BlockSpec((size, width), lambda i: (i, 0))
    smem = pl.BlockSpec(memory_space=pltpu.SMEM)
    return pl.pallas_call(
        functools.partial(dense_kernel, first, second, cut),
        grid=(rows // size,),
        in_specs=[smem, smem, block, block, block]
        + [pl.BlockSpec(memory_space=pltpu.VMEM)] * len(vectors)
        + [ANY] * (len(first.operands) + len(second.operands)),
        out_specs=[block] * 3,
        out_shape=[jax.ShapeDtypeStruct((rows, width), BF16)] * 3,
        scratch_shapes=[
            pltpu.VMEM((width, width + hidden), BF16),
            pltpu.VMEM((hidden, width), BF16),
            pltpu.VMEM((size, hidden), F32),
            pltpu.SemaphoreType.DMA((2, max(first.copies, second.copies))),
        ],
        compiler_params=pltpu.CompilerParams(vmem_limit_bytes=DENSE_VMEM),
        cost_estimate=pl.CostEstimate(
            flops=rows * width * (4 * width + 8 * hidden),
            bytes_accessed=12 * rows * width + 4 * width * hidden,
            transcendentals=2 * rows * hidden,
        ),
        name="dense_both_ways",
    )(rank, place, x, ctx, cot, *vectors, *first.operands, *second.operands)


def attend_back_kernel(seg_ref, x_ref, fac_ref, down_ref, *rest):
    q_ref, k_ref, v_ref, dctx_ref, ctx_ref, aug_ref, *rest = rest
    dq_ref, dk_ref, dv_ref, dlow_ref, grad_ref, low, total, table = rest
    pack, at = pl.program_id(0), pl.program_id(1)
    rows, width = q_ref.shape
    rank2 = 2 * ADAPTER_RANK
    columns = pl.ds(pl.multiple_of(at * width, LANES), width)

    @pl.when((pack == 0) & (at == 0))
    def _():
        table[...] = adapter_rows(fac_ref, 0, *table.shape)

    lane = lax.broadcasted_iota(jnp.int32, (rows, LANES), 1)
    seg = seg_ref[pl.ds(pl.program_id(0), 1), :].astype(F32).T.astype(jnp.int32)
    aug_k = jnp.where(
        (lane < 4) & (lane != seg), -MASKED, jnp.where((lane >= 4) & (lane < 7), 1.0, 0.0)
    ).astype(BF16)
    aug_v = jnp.where(lane < 3, 1.0, 0.0).astype(BF16)
    zero = BF16(0)
    half = LANES // 2
    scale = BF16(half ** (-0.5))
    for pair in range(width // LANES):
        here = slice(LANES * pair, LANES * (pair + 1))
        key = k_ref[:, here]
        query = q_ref[:, here] * scale
        grad = dctx_ref[:, here]
        keys = beside(key, aug_k)
        values = beside(v_ref[:, here], aug_v)
        key = key * scale
        product = grad.astype(F32) * ctx_ref[:, here].astype(F32)
        dq = dk = dv = 0.0
        for side in range(2):
            mask = (lane // half) == side
            one_query = jnp.where(mask, query, zero)
            one_grad = jnp.where(mask, grad, zero)
            one_key = jnp.where(mask, key, zero)
            inner = -jnp.sum(jnp.where(mask, product, 0.0), axis=1, keepdims=True)
            high, middle, little = three_parts(inner)
            aug_d = jnp.where(
                lane == 0, high, jnp.where(lane == 1, middle, jnp.where(lane == 2, little, 0.0))
            ).astype(BF16)
            aug_q = aug_ref[:, (2 * pair + side) * LANES : (2 * pair + side + 1) * LANES]
            probs = jnp.exp(dot(keys, beside(one_query, aug_q), NT))
            dprobs = dot(values, beside(one_grad, aug_d), NT)
            dscores = (probs * dprobs).astype(BF16)
            dv = dv + dot(probs.astype(BF16), one_grad, NN)
            dk = dk + dot(dscores, one_query, NN)
            dq = dq + dot(dscores, one_key, TN)
        dq_ref[:, here] = dq.astype(BF16)
        dk_ref[:, here] = dk.astype(BF16)
        dv_ref[:, here] = dv.astype(BF16)

    up = table[rank2 : 2 * rank2, columns]
    row = lax.broadcasted_iota(jnp.int32, up.shape, 0)
    up_q = jnp.where(row < ADAPTER_RANK, up, 0.0).astype(BF16)
    up_v = jnp.where(row < ADAPTER_RANK, 0.0, up).astype(BF16)
    dlow = dot(dq_ref[...], up_q, NT) + dot(dv_ref[...], up_v, NT)
    low[...] = dlow + jnp.where(at == 0, 0.0, low[...])
    down = down_ref[...]
    from_q = dot(down, dq_ref[...], TN)
    from_v = dot(down, dv_ref[...], TN)
    share = 2.0 * jnp.where(row < ADAPTER_RANK, from_q, from_v)
    later = pack > 0
    total[rank2 : 2 * rank2, columns] = share + jnp.where(
        later, total[rank2 : 2 * rank2, columns], 0.0
    )

    @pl.when(at == pl.num_programs(1) - 1)
    def _():
        dlow_low = (2.0 * low[...]).astype(BF16)
        dlow_ref[...] = dlow_low
        total[0:rank2, :] = dot(dlow_low, x_ref[...], TN) + jnp.where(
            later, total[0:rank2, :], 0.0
        )
        grad_ref[...] = total[...].astype(BF16)


def attend_back(seg, x, factors, down, q, k, v, dctx, ctx, aug, pairs):
    packs, size = seg.shape
    rows, width = x.shape
    cut = pairs * LANES
    rank2 = 2 * ADAPTER_RANK
    block = pl.BlockSpec((size, cut), lambda p, g: (p, g))
    whole = lambda shape: pl.BlockSpec(shape, lambda p, g: (0, 0), pipeline_mode=pl.Buffered(1))
    like = jax.ShapeDtypeStruct
    return pl.pallas_call(
        attend_back_kernel,
        grid=(packs, width // cut),
        in_specs=[
            pl.BlockSpec(memory_space=pltpu.VMEM),
            pl.BlockSpec((size, width), lambda p, g: (p, 0)),
            pl.BlockSpec(memory_space=pltpu.VMEM),
            pl.BlockSpec((size, rank2), lambda p, g: (p, 0)),
            block,
            block,
            block,
            block,
            block,
            pl.BlockSpec((size, 2 * cut), lambda p, g: (p, g)),
        ],
        out_specs=[
            block,
            block,
            block,
            pl.BlockSpec((size, rank2), lambda p, g: (p, 0)),
            whole((2 * rank2, width)),
        ],
        out_shape=[like((rows, width), BF16)] * 3
        + [like((rows, rank2), BF16), like((2 * rank2, width), BF16)],
        scratch_shapes=[pltpu.VMEM((size, rank2), F32)]
        + [pltpu.VMEM((2 * rank2, width), F32)] * 2,
        compiler_params=pltpu.CompilerParams(vmem_limit_bytes=BACK_VMEM),
        cost_estimate=pl.CostEstimate(
            flops=rows * width * 30 * size,
            bytes_accessed=24 * rows * width,
            transcendentals=rows * size * HEADS,
        ),
        name="attend_back",
    )(seg, x, factors, down, q, k, v, dctx, ctx, aug)


def input_kernel(first, dh_ref, dq_ref, dk_ref, dv_ref, dlow_ref, fac_ref, weights, *rest):
    out_ref = rest[-1]
    size, width = out_ref.shape
    block = slice(first, first + size)
    down = adapter_rows(fac_ref, 0, 2 * ADAPTER_RANK, width).astype(BF16)
    total = dh_ref[block, :].astype(F32) + dot(dlow_ref[block, :], down, NN)
    for at, grad in enumerate((dq_ref, dk_ref, dv_ref)):
        total = total + dot(grad[block, :], weights[at], NT)
    out_ref[...] = total.astype(BF16)


def input_back(dh, dq, dk, dv, dlow, factors, weights, size, at, carry):
    rows, width = dh.shape
    vmem = pl.BlockSpec(memory_space=pltpu.VMEM)
    return pl.pallas_call(
        functools.partial(input_kernel, at * size),
        grid=(1,),
        in_specs=[vmem] * 7 + [ANY] * len(carry),
        out_specs=pl.BlockSpec((size, width), lambda i: (at, 0)),
        out_shape=jax.ShapeDtypeStruct((rows, width), BF16),
        input_output_aliases={7 + i: i for i in range(len(carry))},
        compiler_params=pltpu.CompilerParams(vmem_limit_bytes=INPUT_VMEM),
        cost_estimate=pl.CostEstimate(
            flops=6 * size * width * width,
            bytes_accessed=10 * size * width,
            transcendentals=0,
        ),
        name="input_gradient",
    )(dh, dq, dk, dv, dlow, factors, weights, *carry)


def update_kernel(place_ref, near_ref, far_ref, fac_ref, held_ref, other_ref, *rest):
    grad_ref, new_ref, new_first_ref, new_second_ref, lines, table, first, second = rest
    place = place_ref[0]
    owners, length, lanes = fac_ref.shape
    grad = near_ref[...].astype(F32) + far_ref[...].astype(F32)
    rows, width = grad.shape
    step = width // lanes
    for at in range(step):
        lines[pl.ds(at, rows, stride=step), :] = grad[:, at * lanes : (at + 1) * lanes]
    for owner in range(owners):
        table[owner] = lines[owner * length : (owner + 1) * length, :]
    half = owners // 2
    for at in range(owners):
        ref = held_ref if at < half else other_ref
        owner = jnp.bitwise_xor(place, at)
        first[owner] = ref[at % half, 0]
        second[owner] = ref[at % half, 1]
    clip = jnp.minimum(1.0, 1.0 / (jnp.sqrt(jnp.sum(grad * grad)) + 1e-06))
    clipped = table[...] * clip
    new_first = 0.9 * first[...] + 0.1 * clipped
    new_second = 0.999 * second[...] + 0.001 * clipped * clipped
    first[...] = new_first
    second[...] = new_second
    grad_ref[...] = table[place]
    new_first_ref[...] = first[place]
    new_second_ref[...] = second[place]
    factors = fac_ref[...]
    owner = lax.broadcasted_iota(jnp.int32, factors.shape, 0)
    rate = jnp.where(owner < half, rate_low, rate_high)
    fix_first = 1.0 - 0.9**STEP
    fix_second = 1.0 - 0.999**STEP
    move = new_first / fix_first / (jnp.sqrt(new_second / fix_second) + 1e-08)
    new_ref[...] = factors - rate * (move + decay_rate * factors)


def update(place, near, far, factors, held, other):
    like = lambda shape: jax.ShapeDtypeStruct(shape, F32)
    owners, length, lanes = factors.shape
    vmem = pl.BlockSpec(memory_space=pltpu.VMEM)
    piece = like((length, lanes))
    return pl.pallas_call(
        update_kernel,
        in_specs=[pl.BlockSpec(memory_space=pltpu.SMEM)] + [vmem] * 5,
        out_shape=[piece, like(factors.shape), piece, piece],
        scratch_shapes=[pltpu.VMEM((owners * length, lanes), F32)]
        + [pltpu.VMEM(factors.shape, F32)] * 3,
        name="adapter_update",
    )(place, near, far, factors, held, other)


def bits(size):
    return [1 << at for at in range(size.bit_length() - 1)]


def swap(value, axis, size, flip):
    return lax.ppermute(value, axis, [(i, i ^ flip) for i in range(size)])


def cross(value, reps, wide):
    pairs = []
    for rank in range(reps):
        for place in range(wide):
            other = place ^ (1 if rank % 2 == 0 else 2)
            pairs.append((rank * wide + place, rank * wide + other))
    return lax.ppermute(value, ("rep", "wide"), pairs)


def fetch(mine, reps):
    held = [(0, mine)]
    for flip in bits(reps)[1:]:
        held += [(have ^ flip, swap(value, "rep", reps, flip)) for have, value in held]
    return held[1:]


def finish(parts, block_of, halves, crossed, reps, early=None):
    for side, values in enumerate((halves, crossed)):
        for flip, value in values:
            for core in range(2):
                piece = swap(value, "rep", reps, 1) if core else value
                if core and side == 0 and early is not None:
                    piece = gate(piece, early, GATE)
                rows = value.shape[-2]
                places = [(index, block, flip ^ core, (side,), rows, 1) for index, block in block_of]
                parts.add(piece, *places)


def across(halves, reps, wide):
    return [(flip, cross(value, reps, wide)) for flip, value in halves]


def together(*values):
    return lax.optimization_barrier(values)


def gate_kernel(value_ref, other_ref, out_ref):
    pass


def gate(value, other, flops=10**11):
    return pl.pallas_call(
        gate_kernel,
        in_specs=[ANY, ANY],
        out_specs=ANY,
        out_shape=jax.ShapeDtypeStruct(value.shape, value.dtype),
        input_output_aliases={0: 0},
        cost_estimate=pl.CostEstimate(flops=flops, bytes_accessed=1, transcendentals=0),
        name="gate",
    )(value, other)


def local(sizes, *args):
    (
        tokens,
        segment_ids,
        cotangent,
        w_query,
        w_key,
        w_value,
        w_output,
        w_inner,
        w_outer,
        b_query,
        b_value,
        *vectors,
        factors,
        first_moment,
        second_moment,
    ) = args
    reps, wide = sizes
    width = tokens.shape[1]
    packs, size = segment_ids.shape
    rank = lax.axis_index("rep").reshape(1)
    place = lax.axis_index("wide").reshape(1)
    table = factors.reshape(-1, LANES)

    hidden = w_inner.shape[1]
    side = side_of(place[0])
    heads = Parts()
    sent = []
    for block, shard in enumerate((w_query, w_key, w_value)):
        rows = shard.shape[0] // 2
        heads.add(shard, ((), block, 0, 0, rows, 2))
        sent.append(fetch(lax.dynamic_slice_in_dim(shard, side * rows, rows), reps))

    own_ahead = [w_output, w_inner]
    set_ahead = [(0, 0)] + [(1, start) for start in range(0, hidden, width)]
    near_ahead, mine_ahead = pack(place, own_ahead, [(set_ahead, width)])[0]
    flip, value = sent[0][-1]
    value, near_outer, *shards = together(value, w_outer, w_query, w_key, w_value)
    sent[0][-1] = (flip, value)
    for block, shard in enumerate(shards):
        heads.add(swap(shard, "rep", reps, 1), ((), block, 1, 0, shard.shape[0] // 2, 2))
    flip, value = sent[-1][-1]
    length = first_moment.shape[0] // LANES
    held = jnp.stack([first_moment, second_moment]).reshape(1, 2, length, LANES)
    value, mine_ahead, near_ahead, held = together(value, mine_ahead, near_ahead, held)
    sent[-1][-1] = (flip, value)
    flips = bits(wide)
    pending = swap(held, "wide", wide, flips[0])
    crossed = [across(halves, reps, wide) for halves in sent]
    (flip, value), whole_outer = crossed[-1][-1], w_outer
    value, whole_outer = together(value, whole_outer)
    crossed[-1][-1] = (flip, value)
    for block, (halves, others) in enumerate(zip(sent, crossed)):
        finish(heads, [((), block)], halves, others, reps)
    whole_outer = fetch(whole_outer, reps)
    halves_ahead = fetch(mine_ahead, reps)

    early = packs // 2
    arguments = (rank, place, segment_ids, tokens, table, b_query, b_value, 3)
    *attended, weights = attend(*arguments, 0, early, heads)
    weights, *values = together(weights, *[value for _, value in halves_ahead])
    values = [gate(value, weights, GATE) for value in values]
    halves_ahead = [(flip, value) for (flip, _), value in zip(halves_ahead, values)]
    crossed_ahead = across(halves_ahead, reps, wide)
    q, k, v, ctx, aug, down = attend(
        *arguments, early, packs - early, None, weights, attended
    )
    flips_outer, whole_outer = zip(*whole_outer)
    flips_ahead, crossed_ahead = zip(*crossed_ahead)
    down, pending, held, *values = together(down, pending, held, *crossed_ahead, *whole_outer)
    crossed_ahead = list(zip(flips_ahead, values))
    whole_outer = list(zip(flips_outer, values[len(flips_ahead) :]))
    for flip in flips[1:-1]:
        held = jnp.concatenate([held, pending])
        pending = swap(held, "wide", wide, flip)
    rows = w_output.shape[0] // 2
    ahead = Parts()
    ahead.add(w_output, ((), 0, 0, 0, rows, 2))
    columns = [(slice(None), slice(start, start + width)) for start in range(0, hidden, width)]
    ahead.add(w_inner, *[(at, 1 + block, 0, 0, rows, 2) for block, at in enumerate(columns)])
    blocks = range(len(set_ahead))
    near_ahead = swap(near_ahead, "rep", reps, 1)
    ahead.add(near_ahead, *[((s, at), at, 1, s, rows, 1) for at in blocks for s in range(2)])
    finish(ahead, [((at,), at) for at in blocks], halves_ahead, crossed_ahead, reps, down)
    rows = w_outer.shape[0] // 2
    outer = Parts()
    outer.add(w_outer, ((), 0, 0, 0, rows, 2))
    outer.add(swap(near_outer, "rep", reps, 1), ((), 0, 1, 0, rows, 2))
    for flip, value in whole_outer:
        outer.add(value, ((), 0, flip, 0, rows, 2))
        outer.add(swap(value, "rep", reps, 1), ((), 0, flip ^ 1, 0, rows, 2))
    layer_out, dh, dctx = dense(
        rank, place, tokens, ctx, cotangent, vectors, ahead, outer, size, 1024
    )
    dctx, pending, held = together(dctx, pending, held)
    held = jnp.concatenate([held, pending])
    other = swap(held, "wide", wide, flips[-1])
    dq, dk, dv, dlow, grad = attend_back(
        segment_ids, tokens, table, down, q, k, v, dctx, ctx, aug, 3
    )
    rounds = [("rep", reps, flip) for flip in bits(reps)]
    rounds += [("wide", wide, flip) for flip in bits(wide)]
    pieces = 4
    part = tokens.shape[0] // pieces
    input_grad = []
    for at, (axis, count, flip) in enumerate(rounds):
        far = swap(grad, axis, count, flip)
        start = at - (len(rounds) - pieces)
        if start >= 0:
            dh, grad = together(dh, grad)
            args = (dh, dq, dk, dv, dlow, table, weights, part, start)
            input_grad = [input_back(*args, input_grad)]
        if at < len(rounds) - 1:
            grad = grad + far
            if start >= 0:
                grad, *input_grad = together(grad, *input_grad)
    flat = factors.reshape(wide, length, LANES)
    new = update(place, grad, far, flat, held, other)
    piece, new_factors, new_first, new_second = [value.reshape(-1) for value in new]
    return (layer_out, input_grad[0], piece, new_factors, new_first, new_second)


def solution(mesh):
    rows = P(("rep", "wide"), None)
    shard = P("rep", None)
    piece = P("wide")
    placed = (rows,) * 3 + (shard,) * 6 + (P(),) * 10 + (piece,) * 2
    return jax.shard_map(
        functools.partial(local, (mesh.shape["rep"], mesh.shape["wide"])),
        mesh=mesh,
        in_specs=placed,
        out_specs=(rows, rows, piece, P(), piece, piece),
        check_vma=False,
    )
```

```python
import functools

import jax
import jax.numpy as jnp
from jax import lax
from jax.experimental import pallas as pl
from jax.experimental.pallas import tpu as pltpu
from jax.sharding import PartitionSpec as P

HEADS = 12
ADAPTER_RANK = 8
STEP = 10
LANES = 128
MASKED = 1e30

rate_low = 0.015
rate_high = 0.24
decay_rate = 0.01

BF16 = jnp.bfloat16
F32 = jnp.float32
NN = (((1,), (0,)), ((), ()))
NT = (((1,), (1,)), ((), ()))
TN = (((0,), (0,)), ((), ()))
ANY = pl.BlockSpec(memory_space=pl.ANY)
HBM = pl.BlockSpec(memory_space=pltpu.HBM)
VMEM_LIMIT = 56 * 2**20
INPUT_VMEM = 24 * 2**20
BACK_VMEM = 44 * 2**20
DENSE_VMEM = 56 * 2**20
ATTEND_VMEM = 56 * 2**20
GATE = 5 * 10**9


def dot(left, right, dims):
    return lax.dot_general(left, right, dims, preferred_element_type=F32)


def beside(*parts):
    return jnp.concatenate(parts, axis=1)


def mean(value):
    return jnp.mean(value, -1, keepdims=True)


def layer_norm(hidden):
    centre = hidden - mean(hidden)
    rstd = lax.rsqrt(mean(centre * centre) + 1e-05)
    return (centre * rstd, rstd)


def norm_back(grad, normal, rstd, gain):
    scaled = grad * gain
    return rstd * (scaled - mean(scaled) - normal * mean(scaled * normal))


def gelu_pair(value):
    below = 0.5 + 0.5 * lax.erf(value * 2.0 ** (-0.5))
    density = jnp.exp(-0.5 * value * value) * 0.3989422804014327
    return (value * below, below + value * density)


def adapter_rows(lines_ref, first, count, width):
    step = width // LANES
    return beside(
        *[lines_ref[pl.ds(first * step + at, count, stride=step), :] for at in range(step)]
    )


def three_parts(value):
    high = value.astype(BF16).astype(F32)
    rest = value - high
    middle = rest.astype(BF16).astype(F32)
    return (high, middle, rest - middle)


def rows_at(rank, flip, side, rows):
    return pl.multiple_of((jnp.bitwise_xor(rank, flip) * 2 + side) * rows, 16)


def side_of(place):
    return jnp.bitwise_and(jnp.bitwise_xor(place, place >> 1), 1)


class Parts:
    def __init__(self):
        self.operands, self.places = [], []

    def add(self, array, *places):
        self.places += [(len(self.operands),) + place for place in places]
        self.operands.append(array)

    @property
    def copies(self):
        return len(self.places)

    def into(self, refs, rank, place, views, semaphores):
        mine = side_of(place)
        found = [[] for _ in views]
        for at, (operand, index, block, flip, side, rows, halves) in enumerate(self.places):
            source = refs[operand].at[index] if index else refs[operand]
            if isinstance(side, tuple):
                side = jnp.bitwise_xor(mine, side[0])
            target = views[block](rows_at(rank, flip, side, rows), rows * halves)
            found[block].append(pltpu.make_async_copy(source, target, semaphores.at[at]))
        return found


def stacked(weights):
    def view(at):
        return lambda row, rows: weights.at[at, pl.ds(row, rows)]

    return [view(at) for at in range(weights.shape[0])]


def in_columns(weights, width):
    def view(start):
        return lambda row, rows: weights.at[pl.ds(row, rows), start : start + width]

    return [view(start) for start in range(0, weights.shape[1], width)]


def run_copies(copies):
    for copy in copies:
        copy.start()
    for copy in copies:
        copy.wait()


def pack_kernel(sets, count, place_ref, *rest):
    sources, rest = rest[:count], rest[count:]
    outs, rest = rest[: 2 * len(sets)], rest[2 * len(sets) :]
    holds, (arrive, leave) = rest[:-2], rest[-2:]
    side = side_of(place_ref[0])
    incoming, outgoing = [], []
    copy = pltpu.make_async_copy
    for blocks, near_ref, mine_ref, hold in zip(sets, outs[::2], outs[1::2], holds):
        rows, width = mine_ref.shape[1:]
        for block, (source, first) in enumerate(blocks):
            for half in range(2):
                part = sources[source].at[pl.ds(half * rows, rows), pl.ds(first, width)]
                incoming.append(copy(part, hold.at[half, block], arrive.at[len(incoming)]))
        outgoing.append((len(incoming), copy(hold.at[side], mine_ref, leave.at[len(outgoing)])))
        outgoing.append((len(incoming), copy(hold, near_ref, leave.at[len(outgoing)])))
    for one in incoming:
        one.start()
    done = 0
    for needed, one in outgoing:
        for other in incoming[done:needed]:
            other.wait()
        done = needed
        one.start()
    for _, one in outgoing:
        one.wait()


def pack(place, shards, sets):
    shapes = []
    holds = []
    copies = 0
    for blocks, width in sets:
        rows = shards[blocks[0][0]].shape[0] // 2
        holds.append((2, len(blocks), rows, width))
        shapes += [holds[-1], holds[-1][1:]]
        copies += 2 * len(blocks)
    found = pl.pallas_call(
        functools.partial(pack_kernel, [blocks for blocks, _ in sets], len(shards)),
        in_specs=[pl.BlockSpec(memory_space=pltpu.SMEM)] + [HBM] * len(shards),
        out_specs=[HBM] * len(shapes),
        out_shape=[jax.ShapeDtypeStruct(shape, BF16) for shape in shapes],
        scratch_shapes=[pltpu.VMEM(shape, BF16) for shape in holds]
        + [pltpu.SemaphoreType.DMA((copies,)), pltpu.SemaphoreType.DMA((len(shapes),))],
        compiler_params=pltpu.CompilerParams(vmem_limit_bytes=VMEM_LIMIT),
        name="pack_shards",
    )(place, *shards)
    return list(zip(found[::2], found[1::2]))


def attend_kernel(parts, first, rank_ref, place_ref, seg_ref, x_ref, fac_ref, bq_ref, bv_ref, *rest):
    at = pl.program_id(1)
    begin = (pl.program_id(0) == 0) & (at == 0)
    if parts is None:
        weights, rest = rest[0], rest[7:]
        q_ref, k_ref, v_ref, ctx_ref, aug_ref, down_ref, bias, table = rest
    else:
        shards, rest = rest[: len(parts.operands)], rest[len(parts.operands) :]
        q_ref, k_ref, v_ref, ctx_ref, aug_ref, down_ref, weights, bias, table, semaphores = rest

        @pl.when(begin)
        def _():
            blocks = parts.into(shards, rank_ref[0], place_ref[0], stacked(weights), semaphores)
            run_copies(sum(blocks, []))

    width = q_ref.shape[1]
    rows = x_ref.shape[0]

    @pl.when(begin)
    def _():
        bias[0:1, :] = bq_ref[...].reshape(1, -1)
        bias[1:2, :] = bv_ref[...].reshape(1, -1)
        table[...] = adapter_rows(fac_ref, 0, *table.shape)

    rank2 = 2 * ADAPTER_RANK
    columns = pl.ds(pl.multiple_of(at * width, LANES), width)
    x = x_ref[...]
    low = dot(x, table[0:rank2, :].astype(BF16), NT).astype(BF16)
    down_ref[...] = low
    up = table[rank2 : 2 * rank2, columns]
    row = lax.broadcasted_iota(jnp.int32, up.shape, 0)
    up_q = jnp.where(row < ADAPTER_RANK, up, 0.0).astype(BF16)
    up_v = jnp.where(row < ADAPTER_RANK, 0.0, up).astype(BF16)
    q_ref[...] = (dot(x, weights[0, :, columns], NN) + bias[0:1, columns] + 2.0 * dot(low, up_q, NN)).astype(BF16)
    k_ref[...] = dot(x, weights[1, :, columns], NN).astype(BF16)
    v_ref[...] = (dot(x, weights[2, :, columns], NN) + bias[1:2, columns] + 2.0 * dot(low, up_v, NN)).astype(BF16)

    lane = lax.broadcasted_iota(jnp.int32, (rows, LANES), 1)
    seg = seg_ref[pl.ds(first + pl.program_id(0), 1), :].astype(F32).T.astype(jnp.int32)
    own = jnp.where(lane == seg, 1.0, 0.0)
    aug_k = jnp.where((lane < 4) & (lane != seg), -MASKED, 0.0).astype(BF16)
    aug_q = own.astype(BF16)
    ones = jnp.ones((rows, LANES), BF16)
    half = LANES // 2
    scale = BF16(half ** (-0.5))
    second = lane >= half
    spot = jnp.bitwise_and(lane, half - 1)

    def scores(head):
        here = slice(LANES * (head // 2), LANES * (head // 2 + 1))
        query = jnp.where(second == (head % 2 == 1), q_ref[:, here] * scale, BF16(0))
        return dot(beside(query, aug_q), beside(k_ref[:, here], aug_k), NT)

    heads = 2 * width // LANES
    ahead = scores(0)
    found = []
    for head in range(heads):
        now = ahead
        if head + 1 < heads:
            ahead = scores(head + 1)
        here = slice(LANES * (head // 2), LANES * (head // 2 + 1))
        top = jnp.max(now, axis=1, keepdims=True)
        expo = jnp.exp(now - top).astype(BF16)
        both = dot(expo, beside(v_ref[:, here], ones), NN)
        found.append((top, both[:, :LANES], both[:, LANES:]))
        if head % 2 == 1:
            (top0, ctx0, sums0), (top1, ctx1, sums1) = found[-2:]
            sums = jnp.where(second, sums1, sums0)
            ctx_ref[:, here] = (jnp.where(second, ctx1, ctx0) / sums).astype(BF16)
            level = jnp.where(second, top1, top0) + jnp.log(sums)
            high, middle, little = three_parts(-level)
            aug = jnp.where(
                spot == 4, high, jnp.where(spot == 5, middle, jnp.where(spot == 6, little, own))
            )
            aug_ref[:, here] = aug.astype(BF16)


def attend(rank, place, seg, x, factors, bq, bv, pairs, first, count, parts, weights=None, carry=()):
    packs, size = seg.shape
    rows, width = x.shape
    cut = pairs * LANES
    block = pl.BlockSpec((size, cut), lambda p, g: (first + p, g))
    vmem = pl.BlockSpec(memory_space=pltpu.VMEM)
    smem = pl.BlockSpec(memory_space=pltpu.SMEM)
    like = jax.ShapeDtypeStruct
    out_specs = [
        block,
        block,
        block,
        block,
        block,
        pl.BlockSpec((size, 2 * ADAPTER_RANK), lambda p, g: (first + p, 0)),
    ]
    out_shape = [like((rows, width), BF16)] * 5 + [like((rows, 2 * ADAPTER_RANK), BF16)]
    scratch = [pltpu.VMEM((8, width), F32), pltpu.VMEM((4 * ADAPTER_RANK, width), F32)]
    if parts is None:
        operands, specs = [weights, *carry], [vmem] + [ANY] * len(carry)
    else:
        operands, specs = parts.operands, [ANY] * len(parts.operands)
        out_specs.append(pl.BlockSpec((3, width, width), lambda p, g: (0, 0, 0)))
        out_shape.append(like((3, width, width), BF16))
        scratch.append(pltpu.SemaphoreType.DMA((parts.copies,)))
    return pl.pallas_call(
        functools.partial(attend_kernel, parts, first),
        grid=(count, width // cut),
        in_specs=[
            smem,
            smem,
            vmem,
            pl.BlockSpec((size, width), lambda p, g: (first + p, 0)),
            vmem,
            vmem,
            vmem,
        ]
        + specs,
        out_specs=out_specs,
        out_shape=out_shape,
        input_output_aliases={8 + at: at for at in range(len(carry))},
        scratch_shapes=scratch,
        compiler_params=pltpu.CompilerParams(vmem_limit_bytes=ATTEND_VMEM),
        cost_estimate=pl.CostEstimate(
            flops=1 if carry == () else 10**10, bytes_accessed=1, transcendentals=0
        ),
        name="project_and_attend",
    )(rank, place, seg, x, factors, bq, bv, *operands)


def dense_kernel(first, second, cut, rank_ref, place_ref, x_ref, ctx_ref, cot_ref, *rest):
    vectors, rest = rest[:7], rest[7:]
    bo_ref, bi_ref, bo2_ref, g1_ref, s1_ref, g2_ref, s2_ref = vectors
    one, two = len(first.operands), len(second.operands)
    near, far, rest = rest[:one], rest[one : one + two], rest[one + two :]
    out_ref, dh_ref, dctx_ref, ahead, outer, slope, semaphores = rest
    width = x_ref.shape[1]
    hidden = outer.shape[0]

    at = pl.program_id(0)
    rank, place = rank_ref[0], place_ref[0]
    start, *later = first.into(near, rank, place, in_columns(ahead, width), semaphores.at[0])
    later = sum(later + second.into(far, rank, place, in_columns(outer, width), semaphores.at[1]), [])

    @pl.when(at == 0)
    def _():
        for copy in start + later:
            copy.start()
        for copy in start:
            copy.wait()

    bo, bo2 = bo_ref[...].reshape(1, -1), bo2_ref[...].reshape(1, -1)
    g1, s1 = g1_ref[...].reshape(1, -1), s1_ref[...].reshape(1, -1)
    g2, s2 = g2_ref[...].reshape(1, -1), s2_ref[...].reshape(1, -1)
    inner_bias = bi_ref[...].reshape(1, -1)
    wo = lambda: ahead[:, :width]
    w1 = lambda j: ahead[:, width + j : width + j + cut]

    def stages(rows):
        h1 = x_ref[rows, :].astype(F32) + dot(ctx_ref[rows, :], wo(), NN) + bo
        norm1, rstd1 = layer_norm(h1)
        y1 = norm1 * g1 + s1
        y1_low = y1.astype(BF16)
        h2 = y1 + bo2
        yield
        for j in range(0, hidden, cut):
            inner = dot(y1_low, w1(j), NN) + inner_bias[:, j : j + cut]
            act, gradient = gelu_pair(inner)
            slope[rows, j : j + cut] = gradient
            h2 = h2 + dot(act.astype(BF16), outer[j : j + cut, :], NN)
            yield
        norm2, rstd2 = layer_norm(h2)
        out_ref[rows, :] = (norm2 * g2 + s2).astype(BF16)
        dh2 = norm_back(cot_ref[rows, :].astype(F32), norm2, rstd2, g2)
        df = dh2.astype(BF16)
        dy1 = dh2
        yield
        for j in range(0, hidden, cut):
            du = (dot(df, outer[j : j + cut, :], NT) * slope[rows, j : j + cut]).astype(BF16)
            dy1 = dy1 + dot(du, w1(j), NT)
            yield
        dh1 = norm_back(dy1, norm1, rstd1, g1).astype(BF16)
        dh_ref[rows, :] = dh1
        yield
        dctx_ref[rows, :] = dot(dh1, wo(), NT).astype(BF16)

    size = x_ref.shape[0] // 2
    blocks = [stages(slice(start, start + size)) for start in (0, size)]
    next(blocks[0])

    @pl.when(at == 0)
    def _():
        for copy in later:
            copy.wait()

    next(blocks[0])
    live = True
    while live:
        live = any([next(block, True) is None for block in reversed(blocks)])


def dense(rank, place, x, ctx, cot, vectors, first, second, size, cut):
    rows, width = x.shape
    hidden = vectors[1].shape[0]
    block = pl.BlockSpec((size, width), lambda i: (i, 0))
    smem = pl.BlockSpec(memory_space=pltpu.SMEM)
    return pl.pallas_call(
        functools.partial(dense_kernel, first, second, cut),
        grid=(rows // size,),
        in_specs=[smem, smem, block, block, block]
        + [pl.BlockSpec(memory_space=pltpu.VMEM)] * len(vectors)
        + [ANY] * (len(first.operands) + len(second.operands)),
        out_specs=[block] * 3,
        out_shape=[jax.ShapeDtypeStruct((rows, width), BF16)] * 3,
        scratch_shapes=[
            pltpu.VMEM((width, width + hidden), BF16),
            pltpu.VMEM((hidden, width), BF16),
            pltpu.VMEM((size, hidden), F32),
            pltpu.SemaphoreType.DMA((2, max(first.copies, second.copies))),
        ],
        compiler_params=pltpu.CompilerParams(vmem_limit_bytes=DENSE_VMEM),
        cost_estimate=pl.CostEstimate(
            flops=rows * width * (4 * width + 8 * hidden),
            bytes_accessed=12 * rows * width + 4 * width * hidden,
            transcendentals=2 * rows * hidden,
        ),
        name="dense_both_ways",
    )(rank, place, x, ctx, cot, *vectors, *first.operands, *second.operands)


def attend_back_kernel(seg_ref, x_ref, fac_ref, down_ref, *rest):
    q_ref, k_ref, v_ref, dctx_ref, ctx_ref, aug_ref, *rest = rest
    dq_ref, dk_ref, dv_ref, dlow_ref, grad_ref, low, total, table = rest
    pack, at = pl.program_id(0), pl.program_id(1)
    rows, width = q_ref.shape
    rank2 = 2 * ADAPTER_RANK
    columns = pl.ds(pl.multiple_of(at * width, LANES), width)

    @pl.when((pack == 0) & (at == 0))
    def _():
        table[...] = adapter_rows(fac_ref, 0, *table.shape)

    lane = lax.broadcasted_iota(jnp.int32, (rows, LANES), 1)
    seg = seg_ref[pl.ds(pl.program_id(0), 1), :].astype(F32).T.astype(jnp.int32)
    spot = jnp.bitwise_and(lane, LANES // 2 - 1)
    level = (spot >= 4) & (spot < 7)
    second = lane >= LANES // 2
    differ = (lane < 4) & (lane != seg)
    aug_ks = [
        jnp.where(differ, -MASKED, jnp.where(level & (second == bool(side)), 1.0, 0.0)).astype(BF16)
        for side in range(2)
    ]
    aug_v = jnp.where(lane < 3, 1.0, 0.0).astype(BF16)
    zero = BF16(0)
    half = LANES // 2
    scale = BF16(half ** (-0.5))
    for pair in range(width // LANES):
        here = slice(LANES * pair, LANES * (pair + 1))
        key = k_ref[:, here]
        query = q_ref[:, here] * scale
        grad = dctx_ref[:, here]
        values = beside(v_ref[:, here], aug_v)
        key = key * scale
        product = grad.astype(F32) * ctx_ref[:, here].astype(F32)
        dq = dk = dv = 0.0
        for side in range(2):
            mask = (lane // half) == side
            one_query = jnp.where(mask, query, zero)
            one_grad = jnp.where(mask, grad, zero)
            one_key = jnp.where(mask, key, zero)
            inner = -jnp.sum(jnp.where(mask, product, 0.0), axis=1, keepdims=True)
            high, middle, little = three_parts(inner)
            aug_d = jnp.where(
                lane == 0, high, jnp.where(lane == 1, middle, jnp.where(lane == 2, little, 0.0))
            ).astype(BF16)
            keys = beside(k_ref[:, here], aug_ks[side])
            probs = jnp.exp(dot(keys, beside(one_query, aug_ref[:, here]), NT))
            dprobs = dot(values, beside(one_grad, aug_d), NT)
            dscores = (probs * dprobs).astype(BF16)
            dv = dv + dot(probs.astype(BF16), one_grad, NN)
            dk = dk + dot(dscores, one_query, NN)
            dq = dq + dot(dscores, one_key, TN)
        dq_ref[:, here] = dq.astype(BF16)
        dk_ref[:, here] = dk.astype(BF16)
        dv_ref[:, here] = dv.astype(BF16)

    up = table[rank2 : 2 * rank2, columns]
    row = lax.broadcasted_iota(jnp.int32, up.shape, 0)
    up_q = jnp.where(row < ADAPTER_RANK, up, 0.0).astype(BF16)
    up_v = jnp.where(row < ADAPTER_RANK, 0.0, up).astype(BF16)
    dlow = dot(dq_ref[...], up_q, NT) + dot(dv_ref[...], up_v, NT)
    low[...] = dlow + jnp.where(at == 0, 0.0, low[...])
    down = down_ref[...]
    from_q = dot(down, dq_ref[...], TN)
    from_v = dot(down, dv_ref[...], TN)
    share = 2.0 * jnp.where(row < ADAPTER_RANK, from_q, from_v)
    later = pack > 0
    total[rank2 : 2 * rank2, columns] = share + jnp.where(
        later, total[rank2 : 2 * rank2, columns], 0.0
    )

    @pl.when(at == pl.num_programs(1) - 1)
    def _():
        dlow_low = (2.0 * low[...]).astype(BF16)
        dlow_ref[...] = dlow_low
        total[0:rank2, :] = dot(dlow_low, x_ref[...], TN) + jnp.where(
            later, total[0:rank2, :], 0.0
        )
        grad_ref[...] = total[...].astype(BF16)


def attend_back(seg, x, factors, down, q, k, v, dctx, ctx, aug, pairs):
    packs, size = seg.shape
    rows, width = x.shape
    cut = pairs * LANES
    rank2 = 2 * ADAPTER_RANK
    block = pl.BlockSpec((size, cut), lambda p, g: (p, g))
    whole = lambda shape: pl.BlockSpec(shape, lambda p, g: (0, 0), pipeline_mode=pl.Buffered(1))
    like = jax.ShapeDtypeStruct
    return pl.pallas_call(
        attend_back_kernel,
        grid=(packs, width // cut),
        in_specs=[
            pl.BlockSpec(memory_space=pltpu.VMEM),
            pl.BlockSpec((size, width), lambda p, g: (p, 0)),
            pl.BlockSpec(memory_space=pltpu.VMEM),
            pl.BlockSpec((size, rank2), lambda p, g: (p, 0)),
            block,
            block,
            block,
            block,
            block,
            block,
        ],
        out_specs=[
            block,
            block,
            block,
            pl.BlockSpec((size, rank2), lambda p, g: (p, 0)),
            whole((2 * rank2, width)),
        ],
        out_shape=[like((rows, width), BF16)] * 3
        + [like((rows, rank2), BF16), like((2 * rank2, width), BF16)],
        scratch_shapes=[pltpu.VMEM((size, rank2), F32)]
        + [pltpu.VMEM((2 * rank2, width), F32)] * 2,
        compiler_params=pltpu.CompilerParams(vmem_limit_bytes=BACK_VMEM),
        cost_estimate=pl.CostEstimate(
            flops=rows * width * 30 * size,
            bytes_accessed=24 * rows * width,
            transcendentals=rows * size * HEADS,
        ),
        name="attend_back",
    )(seg, x, factors, down, q, k, v, dctx, ctx, aug)


def input_kernel(first, dh_ref, dq_ref, dk_ref, dv_ref, dlow_ref, fac_ref, weights, *rest):
    out_ref = rest[-1]
    size, width = out_ref.shape
    block = slice(first, first + size)
    down = adapter_rows(fac_ref, 0, 2 * ADAPTER_RANK, width).astype(BF16)
    total = dh_ref[block, :].astype(F32) + dot(dlow_ref[block, :], down, NN)
    for at, grad in enumerate((dq_ref, dk_ref, dv_ref)):
        total = total + dot(grad[block, :], weights[at], NT)
    out_ref[...] = total.astype(BF16)


def input_back(dh, dq, dk, dv, dlow, factors, weights, size, at, carry):
    rows, width = dh.shape
    vmem = pl.BlockSpec(memory_space=pltpu.VMEM)
    return pl.pallas_call(
        functools.partial(input_kernel, at * size),
        grid=(1,),
        in_specs=[vmem] * 7 + [ANY] * len(carry),
        out_specs=pl.BlockSpec((size, width), lambda i: (at, 0)),
        out_shape=jax.ShapeDtypeStruct((rows, width), BF16),
        input_output_aliases={7 + i: i for i in range(len(carry))},
        compiler_params=pltpu.CompilerParams(vmem_limit_bytes=INPUT_VMEM),
        cost_estimate=pl.CostEstimate(
            flops=6 * size * width * width,
            bytes_accessed=10 * size * width,
            transcendentals=0,
        ),
        name="input_gradient",
    )(dh, dq, dk, dv, dlow, factors, weights, *carry)


def update_kernel(place_ref, near_ref, far_ref, fac_ref, held_ref, other_ref, *rest):
    grad_ref, new_ref, new_first_ref, new_second_ref, lines, table, first, second = rest
    place = place_ref[0]
    owners, length, lanes = fac_ref.shape
    grad = near_ref[...].astype(F32) + far_ref[...].astype(F32)
    rows, width = grad.shape
    step = width // lanes
    for at in range(step):
        lines[pl.ds(at, rows, stride=step), :] = grad[:, at * lanes : (at + 1) * lanes]
    for owner in range(owners):
        table[owner] = lines[owner * length : (owner + 1) * length, :]
    half = owners // 2
    for at in range(owners):
        ref = held_ref if at < half else other_ref
        owner = jnp.bitwise_xor(place, at)
        first[owner] = ref[at % half, 0]
        second[owner] = ref[at % half, 1]
    clip = jnp.minimum(1.0, 1.0 / (jnp.sqrt(jnp.sum(grad * grad)) + 1e-06))
    clipped = table[...] * clip
    new_first = 0.9 * first[...] + 0.1 * clipped
    new_second = 0.999 * second[...] + 0.001 * clipped * clipped
    first[...] = new_first
    second[...] = new_second
    grad_ref[...] = table[place]
    new_first_ref[...] = first[place]
    new_second_ref[...] = second[place]
    factors = fac_ref[...]
    owner = lax.broadcasted_iota(jnp.int32, factors.shape, 0)
    rate = jnp.where(owner < half, rate_low, rate_high)
    fix_first = 1.0 - 0.9**STEP
    fix_second = 1.0 - 0.999**STEP
    move = new_first / fix_first / (jnp.sqrt(new_second / fix_second) + 1e-08)
    new_ref[...] = factors - rate * (move + decay_rate * factors)


def update(place, near, far, factors, held, other):
    like = lambda shape: jax.ShapeDtypeStruct(shape, F32)
    owners, length, lanes = factors.shape
    vmem = pl.BlockSpec(memory_space=pltpu.VMEM)
    piece = like((length, lanes))
    return pl.pallas_call(
        update_kernel,
        in_specs=[pl.BlockSpec(memory_space=pltpu.SMEM)] + [vmem] * 5,
        out_shape=[piece, like(factors.shape), piece, piece],
        scratch_shapes=[pltpu.VMEM((owners * length, lanes), F32)]
        + [pltpu.VMEM(factors.shape, F32)] * 3,
        name="adapter_update",
    )(place, near, far, factors, held, other)


def bits(size):
    return [1 << at for at in range(size.bit_length() - 1)]


def swap(value, axis, size, flip):
    return lax.ppermute(value, axis, [(i, i ^ flip) for i in range(size)])


def cross(value, reps, wide):
    pairs = []
    for rank in range(reps):
        for place in range(wide):
            other = place ^ (1 if rank % 2 == 0 else 2)
            pairs.append((rank * wide + place, rank * wide + other))
    return lax.ppermute(value, ("rep", "wide"), pairs)


def fetch(mine, reps):
    held = [(0, mine)]
    for flip in bits(reps)[1:]:
        held += [(have ^ flip, swap(value, "rep", reps, flip)) for have, value in held]
    return held[1:]


def finish(parts, block_of, halves, crossed, reps, early=None):
    for side, values in enumerate((halves, crossed)):
        for flip, value in values:
            for core in range(2):
                piece = swap(value, "rep", reps, 1) if core else value
                if core and side == 0 and early is not None:
                    piece = gate(piece, early, GATE)
                rows = value.shape[-2]
                places = [(index, block, flip ^ core, (side,), rows, 1) for index, block in block_of]
                parts.add(piece, *places)


def across(halves, reps, wide):
    return [(flip, cross(value, reps, wide)) for flip, value in halves]


def together(*values):
    return lax.optimization_barrier(values)


def gate_kernel(value_ref, other_ref, out_ref):
    pass


def gate(value, other, flops=10**11):
    return pl.pallas_call(
        gate_kernel,
        in_specs=[ANY, ANY],
        out_specs=ANY,
        out_shape=jax.ShapeDtypeStruct(value.shape, value.dtype),
        input_output_aliases={0: 0},
        cost_estimate=pl.CostEstimate(flops=flops, bytes_accessed=1, transcendentals=0),
        name="gate",
    )(value, other)


def local(sizes, *args):
    (
        tokens,
        segment_ids,
        cotangent,
        w_query,
        w_key,
        w_value,
        w_output,
        w_inner,
        w_outer,
        b_query,
        b_value,
        *vectors,
        factors,
        first_moment,
        second_moment,
    ) = args
    reps, wide = sizes
    width = tokens.shape[1]
    packs, size = segment_ids.shape
    rank = lax.axis_index("rep").reshape(1)
    place = lax.axis_index("wide").reshape(1)
    table = factors.reshape(-1, LANES)

    hidden = w_inner.shape[1]
    side = side_of(place[0])
    heads = Parts()
    sent = []
    for block, shard in enumerate((w_query, w_key, w_value)):
        rows = shard.shape[0] // 2
        heads.add(shard, ((), block, 0, 0, rows, 2))
        sent.append(fetch(lax.dynamic_slice_in_dim(shard, side * rows, rows), reps))

    own_ahead = [w_output, w_inner]
    set_ahead = [(0, 0)] + [(1, start) for start in range(0, hidden, width)]
    near_ahead, mine_ahead = pack(place, own_ahead, [(set_ahead, width)])[0]
    flip, value = sent[0][-1]
    value, near_outer, *shards = together(value, w_outer, w_query, w_key, w_value)
    sent[0][-1] = (flip, value)
    for block, shard in enumerate(shards):
        heads.add(swap(shard, "rep", reps, 1), ((), block, 1, 0, shard.shape[0] // 2, 2))
    flip, value = sent[-1][-1]
    length = first_moment.shape[0] // LANES
    held = jnp.stack([first_moment, second_moment]).reshape(1, 2, length, LANES)
    value, mine_ahead, near_ahead, held = together(value, mine_ahead, near_ahead, held)
    sent[-1][-1] = (flip, value)
    flips = bits(wide)
    pending = swap(held, "wide", wide, flips[0])
    crossed = [across(halves, reps, wide) for halves in sent]
    (flip, value), whole_outer = crossed[-1][-1], w_outer
    value, whole_outer = together(value, whole_outer)
    crossed[-1][-1] = (flip, value)
    for block, (halves, others) in enumerate(zip(sent, crossed)):
        finish(heads, [((), block)], halves, others, reps)
    whole_outer = fetch(whole_outer, reps)
    halves_ahead = fetch(mine_ahead, reps)

    early = packs // 2
    arguments = (rank, place, segment_ids, tokens, table, b_query, b_value, 3)
    *attended, weights = attend(*arguments, 0, early, heads)
    weights, *values = together(weights, *[value for _, value in halves_ahead])
    values = [gate(value, weights, GATE) for value in values]
    halves_ahead = [(flip, value) for (flip, _), value in zip(halves_ahead, values)]
    crossed_ahead = across(halves_ahead, reps, wide)
    q, k, v, ctx, aug, down = attend(
        *arguments, early, packs - early, None, weights, attended
    )
    flips_outer, whole_outer = zip(*whole_outer)
    flips_ahead, crossed_ahead = zip(*crossed_ahead)
    down, pending, held, *values = together(down, pending, held, *crossed_ahead, *whole_outer)
    crossed_ahead = list(zip(flips_ahead, values))
    whole_outer = list(zip(flips_outer, values[len(flips_ahead) :]))
    for flip in flips[1:-1]:
        held = jnp.concatenate([held, pending])
        pending = swap(held, "wide", wide, flip)
    rows = w_output.shape[0] // 2
    ahead = Parts()
    ahead.add(w_output, ((), 0, 0, 0, rows, 2))
    columns = [(slice(None), slice(start, start + width)) for start in range(0, hidden, width)]
    ahead.add(w_inner, *[(at, 1 + block, 0, 0, rows, 2) for block, at in enumerate(columns)])
    blocks = range(len(set_ahead))
    near_ahead = swap(near_ahead, "rep", reps, 1)
    ahead.add(near_ahead, *[((s, at), at, 1, s, rows, 1) for at in blocks for s in range(2)])
    finish(ahead, [((at,), at) for at in blocks], halves_ahead, crossed_ahead, reps, down)
    rows = w_outer.shape[0] // 2
    outer = Parts()
    outer.add(w_outer, ((), 0, 0, 0, rows, 2))
    outer.add(swap(near_outer, "rep", reps, 1), ((), 0, 1, 0, rows, 2))
    for flip, value in whole_outer:
        outer.add(value, ((), 0, flip, 0, rows, 2))
        outer.add(swap(value, "rep", reps, 1), ((), 0, flip ^ 1, 0, rows, 2))
    layer_out, dh, dctx = dense(
        rank, place, tokens, ctx, cotangent, vectors, ahead, outer, size, 1024
    )
    dctx, pending, held = together(dctx, pending, held)
    held = jnp.concatenate([held, pending])
    other = swap(held, "wide", wide, flips[-1])
    dq, dk, dv, dlow, grad = attend_back(
        segment_ids, tokens, table, down, q, k, v, dctx, ctx, aug, 3
    )
    rounds = [("rep", reps, flip) for flip in bits(reps)]
    rounds += [("wide", wide, flip) for flip in bits(wide)]
    pieces = 4
    part = tokens.shape[0] // pieces
    input_grad = []
    for at, (axis, count, flip) in enumerate(rounds):
        far = swap(grad, axis, count, flip)
        start = at - (len(rounds) - pieces)
        if start >= 0:
            dh, grad = together(dh, grad)
            args = (dh, dq, dk, dv, dlow, table, weights, part, start)
            input_grad = [input_back(*args, input_grad)]
        if at < len(rounds) - 1:
            grad = grad + far
            if start >= 0:
                grad, *input_grad = together(grad, *input_grad)
    flat = factors.reshape(wide, length, LANES)
    new = update(place, grad, far, flat, held, other)
    piece, new_factors, new_first, new_second = [value.reshape(-1) for value in new]
    return (layer_out, input_grad[0], piece, new_factors, new_first, new_second)


def solution(mesh):
    rows = P(("rep", "wide"), None)
    shard = P("rep", None)
    piece = P("wide")
    placed = (rows,) * 3 + (shard,) * 6 + (P(),) * 10 + (piece,) * 2
    return jax.shard_map(
        functools.partial(local, (mesh.shape["rep"], mesh.shape["wide"])),
        mesh=mesh,
        in_specs=placed,
        out_specs=(rows, rows, piece, P(), piece, piece),
        check_vma=False,
    )
```

```python
import functools

import jax
import jax.numpy as jnp
from jax import lax
from jax.experimental import pallas as pl
from jax.experimental.pallas import tpu as pltpu
from jax.sharding import PartitionSpec as P

HEADS = 12
ADAPTER_RANK = 8
STEP = 10
LANES = 128
MASKED = 1e30

rate_low = 0.015
rate_high = 0.24
decay_rate = 0.01

BF16 = jnp.bfloat16
F32 = jnp.float32
NN = (((1,), (0,)), ((), ()))
NT = (((1,), (1,)), ((), ()))
TN = (((0,), (0,)), ((), ()))
ANY = pl.BlockSpec(memory_space=pl.ANY)
HBM = pl.BlockSpec(memory_space=pltpu.HBM)
VMEM_LIMIT = 56 * 2**20
LATE = 6 * 10**9
SMALL_VMEM = 8 * 2**20
INPUT_VMEM = 24 * 2**20
BACK_VMEM = 44 * 2**20
DENSE_VMEM = 56 * 2**20
ATTEND_VMEM = 56 * 2**20
GATE = 5 * 10**9


def dot(left, right, dims):
    return lax.dot_general(left, right, dims, preferred_element_type=F32)


def beside(*parts):
    return jnp.concatenate(parts, axis=1)


def mean(value):
    return jnp.mean(value, -1, keepdims=True)


def layer_norm(hidden):
    centre = hidden - mean(hidden)
    rstd = lax.rsqrt(mean(centre * centre) + 1e-05)
    return (centre * rstd, rstd)


def norm_back(grad, normal, rstd, gain):
    scaled = grad * gain
    return rstd * (scaled - mean(scaled) - normal * mean(scaled * normal))


def gelu_pair(value):
    below = 0.5 + 0.5 * lax.erf(value * 2.0 ** (-0.5))
    density = jnp.exp(-0.5 * value * value) * 0.3989422804014327
    return (value * below, below + value * density)


def adapter_rows(lines_ref, first, count, width):
    step = width // LANES
    return beside(
        *[lines_ref[pl.ds(first * step + at, count, stride=step), :] for at in range(step)]
    )


def three_parts(value):
    high = value.astype(BF16).astype(F32)
    rest = value - high
    middle = rest.astype(BF16).astype(F32)
    return (high, middle, rest - middle)


def rows_at(rank, flip, side, rows):
    return pl.multiple_of((jnp.bitwise_xor(rank, flip) * 2 + side) * rows, 16)


def side_of(place):
    return jnp.bitwise_and(jnp.bitwise_xor(place, place >> 1), 1)


class Parts:
    def __init__(self):
        self.operands, self.places = [], []

    def add(self, array, *places):
        self.places += [(len(self.operands),) + place for place in places]
        self.operands.append(array)

    @property
    def copies(self):
        return len(self.places)

    def into(self, refs, rank, place, views, semaphores):
        mine = side_of(place)
        found = [[] for _ in views]
        for at, (operand, index, block, flip, side, rows, halves) in enumerate(self.places):
            source = refs[operand].at[index] if index else refs[operand]
            if isinstance(side, tuple):
                side = jnp.bitwise_xor(mine, side[0])
            target = views[block](rows_at(rank, flip, side, rows), rows * halves)
            found[block].append(pltpu.make_async_copy(source, target, semaphores.at[at]))
        return found


def stacked(weights):
    def view(at):
        return lambda row, rows: weights.at[at, pl.ds(row, rows)]

    return [view(at) for at in range(weights.shape[0])]


def in_columns(weights, width):
    def view(start):
        return lambda row, rows: weights.at[pl.ds(row, rows), start : start + width]

    return [view(start) for start in range(0, weights.shape[1], width)]


def run_copies(copies):
    for copy in copies:
        copy.start()
    for copy in copies:
        copy.wait()


def pack_kernel(sets, count, place_ref, *rest):
    sources, rest = rest[:count], rest[count:]
    outs, rest = rest[: 2 * len(sets)], rest[2 * len(sets) :]
    holds, (arrive, leave) = rest[:-2], rest[-2:]
    side = side_of(place_ref[0])
    incoming, outgoing = [], []
    copy = pltpu.make_async_copy
    for blocks, near_ref, mine_ref, hold in zip(sets, outs[::2], outs[1::2], holds):
        rows, width = mine_ref.shape[1:]
        for block, (source, first) in enumerate(blocks):
            for half in range(2):
                part = sources[source].at[pl.ds(half * rows, rows), pl.ds(first, width)]
                incoming.append(copy(part, hold.at[half, block], arrive.at[len(incoming)]))
        outgoing.append((len(incoming), copy(hold.at[side], mine_ref, leave.at[len(outgoing)])))
        outgoing.append((len(incoming), copy(hold, near_ref, leave.at[len(outgoing)])))
    for one in incoming:
        one.start()
    done = 0
    for needed, one in outgoing:
        for other in incoming[done:needed]:
            other.wait()
        done = needed
        one.start()
    for _, one in outgoing:
        one.wait()


def pack(place, shards, sets):
    shapes = []
    holds = []
    copies = 0
    for blocks, width in sets:
        rows = shards[blocks[0][0]].shape[0] // 2
        holds.append((2, len(blocks), rows, width))
        shapes += [holds[-1], holds[-1][1:]]
        copies += 2 * len(blocks)
    found = pl.pallas_call(
        functools.partial(pack_kernel, [blocks for blocks, _ in sets], len(shards)),
        in_specs=[pl.BlockSpec(memory_space=pltpu.SMEM)] + [HBM] * len(shards),
        out_specs=[HBM] * len(shapes),
        out_shape=[jax.ShapeDtypeStruct(shape, BF16) for shape in shapes],
        scratch_shapes=[pltpu.VMEM(shape, BF16) for shape in holds]
        + [pltpu.SemaphoreType.DMA((copies,)), pltpu.SemaphoreType.DMA((len(shapes),))],
        compiler_params=pltpu.CompilerParams(vmem_limit_bytes=VMEM_LIMIT),
        name="pack_shards",
    )(place, *shards)
    return list(zip(found[::2], found[1::2]))


def attend_kernel(parts, first, rank_ref, place_ref, seg_ref, x_ref, fac_ref, bq_ref, bv_ref, *rest):
    at = pl.program_id(1)
    begin = (pl.program_id(0) == 0) & (at == 0)
    if parts is None:
        weights, rest = rest[0], rest[7:]
        q_ref, k_ref, v_ref, ctx_ref, aug_ref, down_ref, bias, table = rest
    else:
        shards, rest = rest[: len(parts.operands)], rest[len(parts.operands) :]
        q_ref, k_ref, v_ref, ctx_ref, aug_ref, down_ref, weights, bias, table, semaphores = rest

        @pl.when(begin)
        def _():
            blocks = parts.into(shards, rank_ref[0], place_ref[0], stacked(weights), semaphores)
            run_copies(sum(blocks, []))

    width = q_ref.shape[1]
    rows = x_ref.shape[0]

    @pl.when(begin)
    def _():
        bias[0:1, :] = bq_ref[...].reshape(1, -1)
        bias[1:2, :] = bv_ref[...].reshape(1, -1)
        table[...] = adapter_rows(fac_ref, 0, *table.shape)

    rank2 = 2 * ADAPTER_RANK
    columns = pl.ds(pl.multiple_of(at * width, LANES), width)
    x = x_ref[...]
    low = dot(x, table[0:rank2, :].astype(BF16), NT).astype(BF16)
    down_ref[...] = low
    up = table[rank2 : 2 * rank2, columns]
    row = lax.broadcasted_iota(jnp.int32, up.shape, 0)
    up_q = jnp.where(row < ADAPTER_RANK, up, 0.0).astype(BF16)
    up_v = jnp.where(row < ADAPTER_RANK, 0.0, up).astype(BF16)
    q_ref[...] = (dot(x, weights[0, :, columns], NN) + bias[0:1, columns] + 2.0 * dot(low, up_q, NN)).astype(BF16)
    k_ref[...] = dot(x, weights[1, :, columns], NN).astype(BF16)
    v_ref[...] = (dot(x, weights[2, :, columns], NN) + bias[1:2, columns] + 2.0 * dot(low, up_v, NN)).astype(BF16)

    lane = lax.broadcasted_iota(jnp.int32, (rows, LANES), 1)
    seg = seg_ref[pl.ds(first + pl.program_id(0), 1), :].astype(F32).T.astype(jnp.int32)
    own = jnp.where(lane == seg, 1.0, 0.0)
    aug_k = jnp.where((lane < 4) & (lane != seg), -MASKED, 0.0).astype(BF16)
    aug_q = own.astype(BF16)
    ones = jnp.ones((rows, LANES), BF16)
    half = LANES // 2
    scale = BF16(half ** (-0.5))
    second = lane >= half
    spot = jnp.bitwise_and(lane, half - 1)

    def scores(head):
        here = slice(LANES * (head // 2), LANES * (head // 2 + 1))
        query = jnp.where(second == (head % 2 == 1), q_ref[:, here] * scale, BF16(0))
        return dot(beside(query, aug_q), beside(k_ref[:, here], aug_k), NT)

    heads = 2 * width // LANES
    ahead = scores(0)
    found = []
    for head in range(heads):
        now = ahead
        if head + 1 < heads:
            ahead = scores(head + 1)
        here = slice(LANES * (head // 2), LANES * (head // 2 + 1))
        top = jnp.max(now, axis=1, keepdims=True)
        expo = jnp.exp(now - top).astype(BF16)
        both = dot(expo, beside(v_ref[:, here], ones), NN)
        found.append((top, both[:, :LANES], both[:, LANES:]))
        if head % 2 == 1:
            (top0, ctx0, sums0), (top1, ctx1, sums1) = found[-2:]
            sums = jnp.where(second, sums1, sums0)
            ctx_ref[:, here] = (jnp.where(second, ctx1, ctx0) / sums).astype(BF16)
            level = jnp.where(second, top1, top0) + jnp.log(sums)
            high, middle, little = three_parts(-level)
            aug = jnp.where(
                spot == 4, high, jnp.where(spot == 5, middle, jnp.where(spot == 6, little, own))
            )
            aug_ref[:, here] = aug.astype(BF16)


def attend(rank, place, seg, x, factors, bq, bv, pairs, first, count, parts, weights=None, carry=()):
    packs, size = seg.shape
    rows, width = x.shape
    cut = pairs * LANES
    block = pl.BlockSpec((size, cut), lambda p, g: (first + p, g))
    vmem = pl.BlockSpec(memory_space=pltpu.VMEM)
    smem = pl.BlockSpec(memory_space=pltpu.SMEM)
    like = jax.ShapeDtypeStruct
    out_specs = [
        block,
        block,
        block,
        block,
        block,
        pl.BlockSpec((size, 2 * ADAPTER_RANK), lambda p, g: (first + p, 0)),
    ]
    out_shape = [like((rows, width), BF16)] * 5 + [like((rows, 2 * ADAPTER_RANK), BF16)]
    scratch = [pltpu.VMEM((8, width), F32), pltpu.VMEM((4 * ADAPTER_RANK, width), F32)]
    if parts is None:
        operands, specs = [weights, *carry], [vmem] + [ANY] * len(carry)
    else:
        operands, specs = parts.operands, [ANY] * len(parts.operands)
        out_specs.append(pl.BlockSpec((3, width, width), lambda p, g: (0, 0, 0)))
        out_shape.append(like((3, width, width), BF16))
        scratch.append(pltpu.SemaphoreType.DMA((parts.copies,)))
    return pl.pallas_call(
        functools.partial(attend_kernel, parts, first),
        grid=(count, width // cut),
        in_specs=[
            smem,
            smem,
            vmem,
            pl.BlockSpec((size, width), lambda p, g: (first + p, 0)),
            vmem,
            vmem,
            vmem,
        ]
        + specs,
        out_specs=out_specs,
        out_shape=out_shape,
        input_output_aliases={8 + at: at for at in range(len(carry))},
        scratch_shapes=scratch,
        compiler_params=pltpu.CompilerParams(vmem_limit_bytes=ATTEND_VMEM),
        cost_estimate=pl.CostEstimate(
            flops=1 if carry == () else LATE, bytes_accessed=1, transcendentals=0
        ),
        name="project_and_attend",
    )(rank, place, seg, x, factors, bq, bv, *operands)


def dense_kernel(first, second, cut, rank_ref, place_ref, x_ref, ctx_ref, cot_ref, *rest):
    vectors, rest = rest[:7], rest[7:]
    bo_ref, bi_ref, bo2_ref, g1_ref, s1_ref, g2_ref, s2_ref = vectors
    one, two = len(first.operands), len(second.operands)
    near, far, rest = rest[:one], rest[one : one + two], rest[one + two :]
    out_ref, dh_ref, dctx_ref, ahead, outer, slope, semaphores = rest
    width = x_ref.shape[1]
    hidden = outer.shape[0]

    at = pl.program_id(0)
    rank, place = rank_ref[0], place_ref[0]
    start, *later = first.into(near, rank, place, in_columns(ahead, width), semaphores.at[0])
    later = sum(later + second.into(far, rank, place, in_columns(outer, width), semaphores.at[1]), [])

    @pl.when(at == 0)
    def _():
        for copy in start + later:
            copy.start()
        for copy in start:
            copy.wait()

    bo, bo2 = bo_ref[...].reshape(1, -1), bo2_ref[...].reshape(1, -1)
    g1, s1 = g1_ref[...].reshape(1, -1), s1_ref[...].reshape(1, -1)
    g2, s2 = g2_ref[...].reshape(1, -1), s2_ref[...].reshape(1, -1)
    inner_bias = bi_ref[...].reshape(1, -1)
    wo = lambda: ahead[:, :width]
    w1 = lambda j: ahead[:, width + j : width + j + cut]

    def stages(rows):
        h1 = x_ref[rows, :].astype(F32) + dot(ctx_ref[rows, :], wo(), NN) + bo
        norm1, rstd1 = layer_norm(h1)
        y1 = norm1 * g1 + s1
        y1_low = y1.astype(BF16)
        h2 = y1 + bo2
        yield
        for j in range(0, hidden, cut):
            inner = dot(y1_low, w1(j), NN) + inner_bias[:, j : j + cut]
            act, gradient = gelu_pair(inner)
            slope[rows, j : j + cut] = gradient
            h2 = h2 + dot(act.astype(BF16), outer[j : j + cut, :], NN)
            yield
        norm2, rstd2 = layer_norm(h2)
        out_ref[rows, :] = (norm2 * g2 + s2).astype(BF16)
        dh2 = norm_back(cot_ref[rows, :].astype(F32), norm2, rstd2, g2)
        df = dh2.astype(BF16)
        dy1 = dh2
        yield
        for j in range(0, hidden, cut):
            du = (dot(df, outer[j : j + cut, :], NT) * slope[rows, j : j + cut]).astype(BF16)
            dy1 = dy1 + dot(du, w1(j), NT)
            yield
        dh1 = norm_back(dy1, norm1, rstd1, g1).astype(BF16)
        dh_ref[rows, :] = dh1
        yield
        dctx_ref[rows, :] = dot(dh1, wo(), NT).astype(BF16)

    size = x_ref.shape[0] // 2
    blocks = [stages(slice(start, start + size)) for start in (0, size)]
    next(blocks[0])

    @pl.when(at == 0)
    def _():
        for copy in later:
            copy.wait()

    next(blocks[0])
    live = True
    while live:
        live = any([next(block, True) is None for block in reversed(blocks)])


def dense(rank, place, x, ctx, cot, vectors, first, second, size, cut):
    rows, width = x.shape
    hidden = vectors[1].shape[0]
    block = pl.BlockSpec((size, width), lambda i: (i, 0))
    smem = pl.BlockSpec(memory_space=pltpu.SMEM)
    return pl.pallas_call(
        functools.partial(dense_kernel, first, second, cut),
        grid=(rows // size,),
        in_specs=[smem, smem, block, block, block]
        + [pl.BlockSpec(memory_space=pltpu.VMEM)] * len(vectors)
        + [ANY] * (len(first.operands) + len(second.operands)),
        out_specs=[block] * 3,
        out_shape=[jax.ShapeDtypeStruct((rows, width), BF16)] * 3,
        scratch_shapes=[
            pltpu.VMEM((width, width + hidden), BF16),
            pltpu.VMEM((hidden, width), BF16),
            pltpu.VMEM((size, hidden), F32),
            pltpu.SemaphoreType.DMA((2, max(first.copies, second.copies))),
        ],
        compiler_params=pltpu.CompilerParams(vmem_limit_bytes=DENSE_VMEM),
        cost_estimate=pl.CostEstimate(
            flops=rows * width * (4 * width + 8 * hidden),
            bytes_accessed=12 * rows * width + 4 * width * hidden,
            transcendentals=2 * rows * hidden,
        ),
        name="dense_both_ways",
    )(rank, place, x, ctx, cot, *vectors, *first.operands, *second.operands)


def attend_back_kernel(seg_ref, x_ref, fac_ref, down_ref, *rest):
    q_ref, k_ref, v_ref, dctx_ref, ctx_ref, aug_ref, *rest = rest
    dq_ref, dk_ref, dv_ref, dlow_ref, grad_ref, low, total, table = rest
    pack, at = pl.program_id(0), pl.program_id(1)
    rows, width = q_ref.shape
    rank2 = 2 * ADAPTER_RANK
    columns = pl.ds(pl.multiple_of(at * width, LANES), width)

    @pl.when((pack == 0) & (at == 0))
    def _():
        table[...] = adapter_rows(fac_ref, 0, *table.shape)

    lane = lax.broadcasted_iota(jnp.int32, (rows, LANES), 1)
    seg = seg_ref[pl.ds(pl.program_id(0), 1), :].astype(F32).T.astype(jnp.int32)
    spot = jnp.bitwise_and(lane, LANES // 2 - 1)
    level = (spot >= 4) & (spot < 7)
    second = lane >= LANES // 2
    differ = (lane < 4) & (lane != seg)
    aug_ks = [
        jnp.where(differ, -MASKED, jnp.where(level & (second == bool(side)), 1.0, 0.0)).astype(BF16)
        for side in range(2)
    ]
    aug_v = jnp.where(lane < 3, 1.0, 0.0).astype(BF16)
    zero = BF16(0)
    half = LANES // 2
    scale = BF16(half ** (-0.5))
    for pair in range(width // LANES):
        here = slice(LANES * pair, LANES * (pair + 1))
        key = k_ref[:, here]
        query = q_ref[:, here] * scale
        grad = dctx_ref[:, here]
        values = beside(v_ref[:, here], aug_v)
        key = key * scale
        product = grad.astype(F32) * ctx_ref[:, here].astype(F32)
        dq = dk = dv = 0.0
        for side in range(2):
            mask = (lane // half) == side
            one_query = jnp.where(mask, query, zero)
            one_grad = jnp.where(mask, grad, zero)
            one_key = jnp.where(mask, key, zero)
            inner = -jnp.sum(jnp.where(mask, product, 0.0), axis=1, keepdims=True)
            high, middle, little = three_parts(inner)
            aug_d = jnp.where(
                lane == 0, high, jnp.where(lane == 1, middle, jnp.where(lane == 2, little, 0.0))
            ).astype(BF16)
            keys = beside(k_ref[:, here], aug_ks[side])
            probs = jnp.exp(dot(keys, beside(one_query, aug_ref[:, here]), NT))
            dprobs = dot(values, beside(one_grad, aug_d), NT)
            dscores = (probs * dprobs).astype(BF16)
            dv = dv + dot(probs.astype(BF16), one_grad, NN)
            dk = dk + dot(dscores, one_query, NN)
            dq = dq + dot(dscores, one_key, TN)
        dq_ref[:, here] = dq.astype(BF16)
        dk_ref[:, here] = dk.astype(BF16)
        dv_ref[:, here] = dv.astype(BF16)

    up = table[rank2 : 2 * rank2, columns]
    row = lax.broadcasted_iota(jnp.int32, up.shape, 0)
    up_q = jnp.where(row < ADAPTER_RANK, up, 0.0).astype(BF16)
    up_v = jnp.where(row < ADAPTER_RANK, 0.0, up).astype(BF16)
    dlow = dot(dq_ref[...], up_q, NT) + dot(dv_ref[...], up_v, NT)
    low[...] = dlow + jnp.where(at == 0, 0.0, low[...])
    down = down_ref[...]
    from_q = dot(down, dq_ref[...], TN)
    from_v = dot(down, dv_ref[...], TN)
    share = 2.0 * jnp.where(row < ADAPTER_RANK, from_q, from_v)
    later = pack > 0
    total[rank2 : 2 * rank2, columns] = share + jnp.where(
        later, total[rank2 : 2 * rank2, columns], 0.0
    )

    @pl.when(at == pl.num_programs(1) - 1)
    def _():
        dlow_low = (2.0 * low[...]).astype(BF16)
        dlow_ref[...] = dlow_low
        total[0:rank2, :] = dot(dlow_low, x_ref[...], TN) + jnp.where(
            later, total[0:rank2, :], 0.0
        )
        grad_ref[...] = total[...].astype(BF16)


def attend_back(seg, x, factors, down, q, k, v, dctx, ctx, aug, pairs):
    packs, size = seg.shape
    rows, width = x.shape
    cut = pairs * LANES
    rank2 = 2 * ADAPTER_RANK
    block = pl.BlockSpec((size, cut), lambda p, g: (p, g))
    whole = lambda shape: pl.BlockSpec(shape, lambda p, g: (0, 0), pipeline_mode=pl.Buffered(1))
    like = jax.ShapeDtypeStruct
    return pl.pallas_call(
        attend_back_kernel,
        grid=(packs, width // cut),
        in_specs=[
            pl.BlockSpec(memory_space=pltpu.VMEM),
            pl.BlockSpec((size, width), lambda p, g: (p, 0)),
            pl.BlockSpec(memory_space=pltpu.VMEM),
            pl.BlockSpec((size, rank2), lambda p, g: (p, 0)),
            block,
            block,
            block,
            block,
            block,
            block,
        ],
        out_specs=[
            block,
            block,
            block,
            pl.BlockSpec((size, rank2), lambda p, g: (p, 0)),
            whole((2 * rank2, width)),
        ],
        out_shape=[like((rows, width), BF16)] * 3
        + [like((rows, rank2), BF16), like((2 * rank2, width), BF16)],
        scratch_shapes=[pltpu.VMEM((size, rank2), F32)]
        + [pltpu.VMEM((2 * rank2, width), F32)] * 2,
        compiler_params=pltpu.CompilerParams(vmem_limit_bytes=BACK_VMEM),
        cost_estimate=pl.CostEstimate(
            flops=rows * width * 30 * size,
            bytes_accessed=24 * rows * width,
            transcendentals=rows * size * HEADS,
        ),
        name="attend_back",
    )(seg, x, factors, down, q, k, v, dctx, ctx, aug)


def input_kernel(first, dh_ref, dq_ref, dk_ref, dv_ref, dlow_ref, fac_ref, weights, *rest):
    out_ref = rest[-1]
    size, width = out_ref.shape
    block = slice(first, first + size)
    down = adapter_rows(fac_ref, 0, 2 * ADAPTER_RANK, width).astype(BF16)
    total = dh_ref[block, :].astype(F32) + dot(dlow_ref[block, :], down, NN)
    for at, grad in enumerate((dq_ref, dk_ref, dv_ref)):
        total = total + dot(grad[block, :], weights[at], NT)
    out_ref[...] = total.astype(BF16)


def input_back(dh, dq, dk, dv, dlow, factors, weights, size, at, carry):
    rows, width = dh.shape
    vmem = pl.BlockSpec(memory_space=pltpu.VMEM)
    return pl.pallas_call(
        functools.partial(input_kernel, at * size),
        grid=(1,),
        in_specs=[vmem] * 7 + [ANY] * len(carry),
        out_specs=pl.BlockSpec((size, width), lambda i: (at, 0)),
        out_shape=jax.ShapeDtypeStruct((rows, width), BF16),
        input_output_aliases={7 + i: i for i in range(len(carry))},
        compiler_params=pltpu.CompilerParams(vmem_limit_bytes=INPUT_VMEM),
        cost_estimate=pl.CostEstimate(
            flops=6 * size * width * width,
            bytes_accessed=10 * size * width,
            transcendentals=0,
        ),
        name="input_gradient",
    )(dh, dq, dk, dv, dlow, factors, weights, *carry)


def update_kernel(place_ref, near_ref, far_ref, fac_ref, held_ref, other_ref, *rest):
    grad_ref, new_ref, new_first_ref, new_second_ref, lines, table, first, second = rest
    place = place_ref[0]
    owners, length, lanes = fac_ref.shape
    grad = near_ref[...].astype(F32) + far_ref[...].astype(F32)
    rows, width = grad.shape
    step = width // lanes
    for at in range(step):
        lines[pl.ds(at, rows, stride=step), :] = grad[:, at * lanes : (at + 1) * lanes]
    for owner in range(owners):
        table[owner] = lines[owner * length : (owner + 1) * length, :]
    half = owners // 2
    for at in range(owners):
        ref = held_ref if at < half else other_ref
        owner = jnp.bitwise_xor(place, at)
        first[owner] = ref[at % half, 0]
        second[owner] = ref[at % half, 1]
    clip = jnp.minimum(1.0, 1.0 / (jnp.sqrt(jnp.sum(grad * grad)) + 1e-06))
    clipped = table[...] * clip
    new_first = 0.9 * first[...] + 0.1 * clipped
    new_second = 0.999 * second[...] + 0.001 * clipped * clipped
    first[...] = new_first
    second[...] = new_second
    grad_ref[...] = table[place]
    new_first_ref[...] = first[place]
    new_second_ref[...] = second[place]
    factors = fac_ref[...]
    owner = lax.broadcasted_iota(jnp.int32, factors.shape, 0)
    rate = jnp.where(owner < half, rate_low, rate_high)
    fix_first = 1.0 - 0.9**STEP
    fix_second = 1.0 - 0.999**STEP
    move = new_first / fix_first / (jnp.sqrt(new_second / fix_second) + 1e-08)
    new_ref[...] = factors - rate * (move + decay_rate * factors)


def update(place, near, far, factors, held, other):
    like = lambda shape: jax.ShapeDtypeStruct(shape, F32)
    owners, length, lanes = factors.shape
    vmem = pl.BlockSpec(memory_space=pltpu.VMEM)
    piece = like((length, lanes))
    return pl.pallas_call(
        update_kernel,
        in_specs=[pl.BlockSpec(memory_space=pltpu.SMEM)] + [vmem] * 5,
        out_shape=[piece, like(factors.shape), piece, piece],
        scratch_shapes=[pltpu.VMEM((owners * length, lanes), F32)]
        + [pltpu.VMEM(factors.shape, F32)] * 3,
        compiler_params=pltpu.CompilerParams(vmem_limit_bytes=SMALL_VMEM),
        name="adapter_update",
    )(place, near, far, factors, held, other)


def bits(size):
    return [1 << at for at in range(size.bit_length() - 1)]


def swap(value, axis, size, flip):
    return lax.ppermute(value, axis, [(i, i ^ flip) for i in range(size)])


def cross(value, reps, wide):
    pairs = []
    for rank in range(reps):
        for place in range(wide):
            other = place ^ (1 if rank % 2 == 0 else 2)
            pairs.append((rank * wide + place, rank * wide + other))
    return lax.ppermute(value, ("rep", "wide"), pairs)


def fetch(mine, reps):
    held = [(0, mine)]
    for flip in bits(reps)[1:]:
        held += [(have ^ flip, swap(value, "rep", reps, flip)) for have, value in held]
    return held[1:]


def finish(parts, block_of, halves, crossed, reps, early=None):
    for side, values in enumerate((halves, crossed)):
        for flip, value in values:
            for core in range(2):
                piece = swap(value, "rep", reps, 1) if core else value
                if core and side == 0 and early is not None:
                    piece = gate(piece, early, GATE)
                rows = value.shape[-2]
                places = [(index, block, flip ^ core, (side,), rows, 1) for index, block in block_of]
                parts.add(piece, *places)


def across(halves, reps, wide):
    return [(flip, cross(value, reps, wide)) for flip, value in halves]


def together(*values):
    return lax.optimization_barrier(values)


def gate_kernel(value_ref, other_ref, out_ref):
    pass


def gate(value, other, flops=10**11):
    return pl.pallas_call(
        gate_kernel,
        in_specs=[ANY, ANY],
        out_specs=ANY,
        out_shape=jax.ShapeDtypeStruct(value.shape, value.dtype),
        input_output_aliases={0: 0},
        cost_estimate=pl.CostEstimate(flops=flops, bytes_accessed=1, transcendentals=0),
        name="gate",
    )(value, other)


def local(sizes, *args):
    (
        tokens,
        segment_ids,
        cotangent,
        w_query,
        w_key,
        w_value,
        w_output,
        w_inner,
        w_outer,
        b_query,
        b_value,
        *vectors,
        factors,
        first_moment,
        second_moment,
    ) = args
    reps, wide = sizes
    width = tokens.shape[1]
    packs, size = segment_ids.shape
    rank = lax.axis_index("rep").reshape(1)
    place = lax.axis_index("wide").reshape(1)
    table = factors.reshape(-1, LANES)

    hidden = w_inner.shape[1]
    side = side_of(place[0])
    heads = Parts()
    sent = []
    for block, shard in enumerate((w_query, w_key, w_value)):
        rows = shard.shape[0] // 2
        heads.add(shard, ((), block, 0, 0, rows, 2))
        sent.append(fetch(lax.dynamic_slice_in_dim(shard, side * rows, rows), reps))

    own_ahead = [w_output, w_inner]
    set_ahead = [(0, 0)] + [(1, start) for start in range(0, hidden, width)]
    near_ahead, mine_ahead = pack(place, own_ahead, [(set_ahead, width)])[0]
    flip, value = sent[0][-1]
    value, near_outer, *shards = together(value, w_outer, w_query, w_key, w_value)
    sent[0][-1] = (flip, value)
    for block, shard in enumerate(shards):
        heads.add(swap(shard, "rep", reps, 1), ((), block, 1, 0, shard.shape[0] // 2, 2))
    flip, value = sent[-1][-1]
    length = first_moment.shape[0] // LANES
    held = jnp.stack([first_moment, second_moment]).reshape(1, 2, length, LANES)
    value, mine_ahead, near_ahead, held = together(value, mine_ahead, near_ahead, held)
    sent[-1][-1] = (flip, value)
    flips = bits(wide)
    pending = swap(held, "wide", wide, flips[0])
    crossed = [across(halves, reps, wide) for halves in sent]
    (flip, value), whole_outer = crossed[-1][-1], w_outer
    value, whole_outer = together(value, whole_outer)
    crossed[-1][-1] = (flip, value)
    for block, (halves, others) in enumerate(zip(sent, crossed)):
        finish(heads, [((), block)], halves, others, reps)
    whole_outer = fetch(whole_outer, reps)
    halves_ahead = fetch(mine_ahead, reps)

    early = packs // 2
    arguments = (rank, place, segment_ids, tokens, table, b_query, b_value, 3)
    *attended, weights = attend(*arguments, 0, early, heads)
    weights, *values = together(weights, *[value for _, value in halves_ahead])
    values = [gate(value, weights, GATE) for value in values]
    halves_ahead = [(flip, value) for (flip, _), value in zip(halves_ahead, values)]
    crossed_ahead = across(halves_ahead, reps, wide)
    q, k, v, ctx, aug, down = attend(
        *arguments, early, packs - early, None, weights, attended
    )
    flips_outer, whole_outer = zip(*whole_outer)
    flips_ahead, crossed_ahead = zip(*crossed_ahead)
    down, pending, held, *values = together(down, pending, held, *crossed_ahead, *whole_outer)
    crossed_ahead = list(zip(flips_ahead, values))
    whole_outer = list(zip(flips_outer, values[len(flips_ahead) :]))
    for flip in flips[1:-1]:
        held = jnp.concatenate([held, pending])
        pending = swap(held, "wide", wide, flip)
    rows = w_output.shape[0] // 2
    ahead = Parts()
    ahead.add(w_output, ((), 0, 0, 0, rows, 2))
    columns = [(slice(None), slice(start, start + width)) for start in range(0, hidden, width)]
    ahead.add(w_inner, *[(at, 1 + block, 0, 0, rows, 2) for block, at in enumerate(columns)])
    blocks = range(len(set_ahead))
    near_ahead = swap(near_ahead, "rep", reps, 1)
    ahead.add(near_ahead, *[((s, at), at, 1, s, rows, 1) for at in blocks for s in range(2)])
    finish(ahead, [((at,), at) for at in blocks], halves_ahead, crossed_ahead, reps, down)
    rows = w_outer.shape[0] // 2
    outer = Parts()
    outer.add(w_outer, ((), 0, 0, 0, rows, 2))
    outer.add(swap(near_outer, "rep", reps, 1), ((), 0, 1, 0, rows, 2))
    for flip, value in whole_outer:
        outer.add(value, ((), 0, flip, 0, rows, 2))
        outer.add(swap(value, "rep", reps, 1), ((), 0, flip ^ 1, 0, rows, 2))
    layer_out, dh, dctx = dense(
        rank, place, tokens, ctx, cotangent, vectors, ahead, outer, size, 1024
    )
    dctx, pending, held = together(dctx, pending, held)
    held = jnp.concatenate([held, pending])
    other = swap(held, "wide", wide, flips[-1])
    dq, dk, dv, dlow, grad = attend_back(
        segment_ids, tokens, table, down, q, k, v, dctx, ctx, aug, 3
    )
    rounds = [("rep", reps, flip) for flip in bits(reps)]
    rounds += [("wide", wide, flip) for flip in bits(wide)]
    pieces = 4
    part = tokens.shape[0] // pieces
    input_grad = []
    for at, (axis, count, flip) in enumerate(rounds):
        far = swap(grad, axis, count, flip)
        start = at - (len(rounds) - pieces)
        if start >= 0:
            dh, grad = together(dh, grad)
            args = (dh, dq, dk, dv, dlow, table, weights, part, start)
            input_grad = [input_back(*args, input_grad)]
        if at < len(rounds) - 1:
            grad = grad + far
            if start >= 0:
                grad, *input_grad = together(grad, *input_grad)
    flat = factors.reshape(wide, length, LANES)
    new = update(place, grad, far, flat, held, other)
    piece, new_factors, new_first, new_second = [value.reshape(-1) for value in new]
    return (layer_out, input_grad[0], piece, new_factors, new_first, new_second)


def solution(mesh):
    rows = P(("rep", "wide"), None)
    shard = P("rep", None)
    piece = P("wide")
    placed = (rows,) * 3 + (shard,) * 6 + (P(),) * 10 + (piece,) * 2
    return jax.shard_map(
        functools.partial(local, (mesh.shape["rep"], mesh.shape["wide"])),
        mesh=mesh,
        in_specs=placed,
        out_specs=(rows, rows, piece, P(), piece, piece),
        check_vma=False,
    )
```

```python
import functools

import jax
import jax.numpy as jnp
from jax import lax
from jax.experimental import pallas as pl
from jax.experimental.pallas import tpu as pltpu
from jax.sharding import PartitionSpec as P

HEADS = 12
ADAPTER_RANK = 8
STEP = 10
LANES = 128
MASKED = 1e30

rate_low = 0.015
rate_high = 0.24
decay_rate = 0.01

BF16 = jnp.bfloat16
F32 = jnp.float32
NN = (((1,), (0,)), ((), ()))
NT = (((1,), (1,)), ((), ()))
TN = (((0,), (0,)), ((), ()))
ANY = pl.BlockSpec(memory_space=pl.ANY)
HBM = pl.BlockSpec(memory_space=pltpu.HBM)
VMEM_LIMIT = 56 * 2**20
LATE = 6 * 10**9
SMALL_VMEM = 8 * 2**20
INPUT_VMEM = 24 * 2**20
BACK_VMEM = 44 * 2**20
DENSE_VMEM = 56 * 2**20
ATTEND_VMEM = 56 * 2**20
GATE = 5 * 10**9


def dot(left, right, dims):
    return lax.dot_general(left, right, dims, preferred_element_type=F32)


def beside(*parts):
    return jnp.concatenate(parts, axis=1)


def mean(value):
    return jnp.mean(value, -1, keepdims=True)


def layer_norm(hidden):
    centre = hidden - mean(hidden)
    rstd = lax.rsqrt(mean(centre * centre) + 1e-05)
    return (centre * rstd, rstd)


def norm_back(grad, normal, rstd, gain):
    scaled = grad * gain
    return rstd * (scaled - mean(scaled) - normal * mean(scaled * normal))


def gelu_pair(value):
    below = 0.5 + 0.5 * lax.erf(value * 2.0 ** (-0.5))
    density = jnp.exp(-0.5 * value * value) * 0.3989422804014327
    return (value * below, below + value * density)


def adapter_rows(lines_ref, first, count, width):
    step = width // LANES
    return beside(
        *[lines_ref[pl.ds(first * step + at, count, stride=step), :] for at in range(step)]
    )


def three_parts(value):
    high = value.astype(BF16).astype(F32)
    rest = value - high
    middle = rest.astype(BF16).astype(F32)
    return (high, middle, rest - middle)


def rows_at(rank, flip, side, rows):
    return pl.multiple_of((jnp.bitwise_xor(rank, flip) * 2 + side) * rows, 16)


def side_of(place):
    return jnp.bitwise_and(jnp.bitwise_xor(place, place >> 1), 1)


class Parts:
    def __init__(self):
        self.operands, self.places = [], []

    def add(self, array, *places):
        self.places += [(len(self.operands),) + place for place in places]
        self.operands.append(array)

    @property
    def copies(self):
        return len(self.places)

    def into(self, refs, rank, place, views, semaphores):
        mine = side_of(place)
        found = [[] for _ in views]
        for at, (operand, index, block, flip, side, rows, halves) in enumerate(self.places):
            source = refs[operand].at[index] if index else refs[operand]
            if isinstance(side, tuple):
                side = jnp.bitwise_xor(mine, side[0])
            target = views[block](rows_at(rank, flip, side, rows), rows * halves)
            found[block].append(pltpu.make_async_copy(source, target, semaphores.at[at]))
        return found


def stacked(weights):
    def view(at):
        return lambda row, rows: weights.at[at, pl.ds(row, rows)]

    return [view(at) for at in range(weights.shape[0])]


def in_columns(weights, width):
    def view(start):
        return lambda row, rows: weights.at[pl.ds(row, rows), start : start + width]

    return [view(start) for start in range(0, weights.shape[1], width)]


def run_copies(copies):
    for copy in copies:
        copy.start()
    for copy in copies:
        copy.wait()


def pack_kernel(sets, count, place_ref, *rest):
    sources, rest = rest[:count], rest[count:]
    outs, rest = rest[: 2 * len(sets)], rest[2 * len(sets) :]
    holds, (arrive, leave) = rest[:-2], rest[-2:]
    side = side_of(place_ref[0])
    incoming, outgoing = [], []
    copy = pltpu.make_async_copy
    for blocks, near_ref, mine_ref, hold in zip(sets, outs[::2], outs[1::2], holds):
        rows, width = mine_ref.shape[1:]
        for block, (source, first) in enumerate(blocks):
            for half in range(2):
                part = sources[source].at[pl.ds(half * rows, rows), pl.ds(first, width)]
                incoming.append(copy(part, hold.at[half, block], arrive.at[len(incoming)]))
        outgoing.append((len(incoming), copy(hold.at[side], mine_ref, leave.at[len(outgoing)])))
        outgoing.append((len(incoming), copy(hold, near_ref, leave.at[len(outgoing)])))
    for one in incoming:
        one.start()
    done = 0
    for needed, one in outgoing:
        for other in incoming[done:needed]:
            other.wait()
        done = needed
        one.start()
    for _, one in outgoing:
        one.wait()


def pack(place, shards, sets):
    shapes = []
    holds = []
    copies = 0
    for blocks, width in sets:
        rows = shards[blocks[0][0]].shape[0] // 2
        holds.append((2, len(blocks), rows, width))
        shapes += [holds[-1], holds[-1][1:]]
        copies += 2 * len(blocks)
    found = pl.pallas_call(
        functools.partial(pack_kernel, [blocks for blocks, _ in sets], len(shards)),
        in_specs=[pl.BlockSpec(memory_space=pltpu.SMEM)] + [HBM] * len(shards),
        out_specs=[HBM] * len(shapes),
        out_shape=[jax.ShapeDtypeStruct(shape, BF16) for shape in shapes],
        scratch_shapes=[pltpu.VMEM(shape, BF16) for shape in holds]
        + [pltpu.SemaphoreType.DMA((copies,)), pltpu.SemaphoreType.DMA((len(shapes),))],
        compiler_params=pltpu.CompilerParams(vmem_limit_bytes=VMEM_LIMIT),
        name="pack_shards",
    )(place, *shards)
    return list(zip(found[::2], found[1::2]))


def attend_kernel(parts, first, rank_ref, place_ref, seg_ref, x_ref, fac_ref, bq_ref, bv_ref, *rest):
    at = pl.program_id(1)
    begin = (pl.program_id(0) == 0) & (at == 0)
    if parts is None:
        weights, rest = rest[0], rest[8:]
        q_ref, k_ref, v_ref, ctx_ref, inverse_ref, expo_ref, down_ref, bias, table = rest
    else:
        shards, rest = rest[: len(parts.operands)], rest[len(parts.operands) :]
        q_ref, k_ref, v_ref, ctx_ref, inverse_ref, expo_ref, down_ref, *rest = rest
        weights, bias, table, semaphores = rest

        @pl.when(begin)
        def _():
            blocks = parts.into(shards, rank_ref[0], place_ref[0], stacked(weights), semaphores)
            run_copies(sum(blocks, []))

    width = q_ref.shape[1]
    rows = x_ref.shape[0]

    @pl.when(begin)
    def _():
        bias[0:1, :] = bq_ref[...].reshape(1, -1)
        bias[1:2, :] = bv_ref[...].reshape(1, -1)
        table[...] = adapter_rows(fac_ref, 0, *table.shape)

    rank2 = 2 * ADAPTER_RANK
    columns = pl.ds(pl.multiple_of(at * width, LANES), width)
    x = x_ref[...]
    low = dot(x, table[0:rank2, :].astype(BF16), NT).astype(BF16)
    down_ref[...] = low
    up = table[rank2 : 2 * rank2, columns]
    row = lax.broadcasted_iota(jnp.int32, up.shape, 0)
    up_q = jnp.where(row < ADAPTER_RANK, up, 0.0).astype(BF16)
    up_v = jnp.where(row < ADAPTER_RANK, 0.0, up).astype(BF16)
    q_ref[...] = (dot(x, weights[0, :, columns], NN) + bias[0:1, columns] + 2.0 * dot(low, up_q, NN)).astype(BF16)
    k_ref[...] = dot(x, weights[1, :, columns], NN).astype(BF16)
    v_ref[...] = (dot(x, weights[2, :, columns], NN) + bias[1:2, columns] + 2.0 * dot(low, up_v, NN)).astype(BF16)

    lane = lax.broadcasted_iota(jnp.int32, (rows, LANES), 1)
    seg = seg_ref[pl.ds(first + pl.program_id(0), 1), :].astype(F32).T.astype(jnp.int32)
    aug_k = jnp.where((lane < 4) & (lane != seg), -MASKED, 0.0).astype(BF16)
    aug_q = jnp.where(lane == seg, 1.0, 0.0).astype(BF16)
    ones = jnp.ones((rows, LANES), BF16)
    half = LANES // 2
    scale = BF16(half ** (-0.5))
    second = lane >= half

    def scores(head):
        here = slice(LANES * (head // 2), LANES * (head // 2 + 1))
        query = jnp.where(second == (head % 2 == 1), q_ref[:, here] * scale, BF16(0))
        return dot(beside(query, aug_q), beside(k_ref[:, here], aug_k), NT)

    heads = 2 * width // LANES
    ahead = scores(0)
    found = []
    for head in range(heads):
        now = ahead
        if head + 1 < heads:
            ahead = scores(head + 1)
        here = slice(LANES * (head // 2), LANES * (head // 2 + 1))
        expo = jnp.exp(now - jnp.max(now, axis=1, keepdims=True)).astype(BF16)
        expo_ref[head * rows : (head + 1) * rows, :] = expo
        both = dot(expo, beside(v_ref[:, here], ones), NN)
        found.append((both[:, :LANES], both[:, LANES:]))
        if head % 2 == 1:
            (ctx0, sums0), (ctx1, sums1) = found[-2:]
            inverse = 1.0 / jnp.where(second, sums1, sums0)
            inverse_ref[:, here] = inverse
            ctx_ref[:, here] = (jnp.where(second, ctx1, ctx0) * inverse).astype(BF16)


def attend(rank, place, seg, x, factors, bq, bv, pairs, first, count, parts, weights=None, carry=()):
    packs, size = seg.shape
    rows, width = x.shape
    cut = pairs * LANES
    groups = width // cut
    block = pl.BlockSpec((size, cut), lambda p, g: (first + p, g))
    vmem = pl.BlockSpec(memory_space=pltpu.VMEM)
    smem = pl.BlockSpec(memory_space=pltpu.SMEM)
    like = jax.ShapeDtypeStruct
    out_specs = [
        block,
        block,
        block,
        block,
        block,
        pl.BlockSpec((2 * pairs * size, size), lambda p, g: ((first + p) * groups + g, 0)),
        pl.BlockSpec((size, 2 * ADAPTER_RANK), lambda p, g: (first + p, 0)),
    ]
    out_shape = [like((rows, width), BF16)] * 4 + [like((rows, width), F32)]
    out_shape += [like((HEADS * rows, size), BF16), like((rows, 2 * ADAPTER_RANK), BF16)]
    scratch = [pltpu.VMEM((8, width), F32), pltpu.VMEM((4 * ADAPTER_RANK, width), F32)]
    if parts is None:
        operands, specs = [weights, *carry], [vmem] + [ANY] * len(carry)
    else:
        operands, specs = parts.operands, [ANY] * len(parts.operands)
        out_specs.append(pl.BlockSpec((3, width, width), lambda p, g: (0, 0, 0)))
        out_shape.append(like((3, width, width), BF16))
        scratch.append(pltpu.SemaphoreType.DMA((parts.copies,)))
    return pl.pallas_call(
        functools.partial(attend_kernel, parts, first),
        grid=(count, width // cut),
        in_specs=[
            smem,
            smem,
            vmem,
            pl.BlockSpec((size, width), lambda p, g: (first + p, 0)),
            vmem,
            vmem,
            vmem,
        ]
        + specs,
        out_specs=out_specs,
        out_shape=out_shape,
        input_output_aliases={8 + at: at for at in range(len(carry))},
        scratch_shapes=scratch,
        compiler_params=pltpu.CompilerParams(vmem_limit_bytes=ATTEND_VMEM),
        cost_estimate=pl.CostEstimate(
            flops=1 if carry == () else LATE, bytes_accessed=1, transcendentals=0
        ),
        name="project_and_attend",
    )(rank, place, seg, x, factors, bq, bv, *operands)


def dense_kernel(first, second, cut, rank_ref, place_ref, x_ref, ctx_ref, cot_ref, *rest):
    vectors, rest = rest[:7], rest[7:]
    bo_ref, bi_ref, bo2_ref, g1_ref, s1_ref, g2_ref, s2_ref = vectors
    one, two = len(first.operands), len(second.operands)
    near, far, rest = rest[:one], rest[one : one + two], rest[one + two :]
    out_ref, dh_ref, dctx_ref, ahead, outer, slope, semaphores = rest
    width = x_ref.shape[1]
    hidden = outer.shape[0]

    at = pl.program_id(0)
    rank, place = rank_ref[0], place_ref[0]
    start, *later = first.into(near, rank, place, in_columns(ahead, width), semaphores.at[0])
    later = sum(later + second.into(far, rank, place, in_columns(outer, width), semaphores.at[1]), [])

    @pl.when(at == 0)
    def _():
        for copy in start + later:
            copy.start()
        for copy in start:
            copy.wait()

    bo, bo2 = bo_ref[...].reshape(1, -1), bo2_ref[...].reshape(1, -1)
    g1, s1 = g1_ref[...].reshape(1, -1), s1_ref[...].reshape(1, -1)
    g2, s2 = g2_ref[...].reshape(1, -1), s2_ref[...].reshape(1, -1)
    inner_bias = bi_ref[...].reshape(1, -1)
    wo = lambda: ahead[:, :width]
    w1 = lambda j: ahead[:, width + j : width + j + cut]

    def stages(rows):
        h1 = x_ref[rows, :].astype(F32) + dot(ctx_ref[rows, :], wo(), NN) + bo
        norm1, rstd1 = layer_norm(h1)
        y1 = norm1 * g1 + s1
        y1_low = y1.astype(BF16)
        h2 = y1 + bo2
        yield
        for j in range(0, hidden, cut):
            inner = dot(y1_low, w1(j), NN) + inner_bias[:, j : j + cut]
            act, gradient = gelu_pair(inner)
            slope[rows, j : j + cut] = gradient
            h2 = h2 + dot(act.astype(BF16), outer[j : j + cut, :], NN)
            yield
        norm2, rstd2 = layer_norm(h2)
        out_ref[rows, :] = (norm2 * g2 + s2).astype(BF16)
        dh2 = norm_back(cot_ref[rows, :].astype(F32), norm2, rstd2, g2)
        df = dh2.astype(BF16)
        dy1 = dh2
        yield
        for j in range(0, hidden, cut):
            du = (dot(df, outer[j : j + cut, :], NT) * slope[rows, j : j + cut]).astype(BF16)
            dy1 = dy1 + dot(du, w1(j), NT)
            yield
        dh1 = norm_back(dy1, norm1, rstd1, g1).astype(BF16)
        dh_ref[rows, :] = dh1
        yield
        dctx_ref[rows, :] = dot(dh1, wo(), NT).astype(BF16)

    size = x_ref.shape[0] // 2
    blocks = [stages(slice(start, start + size)) for start in (0, size)]
    next(blocks[0])

    @pl.when(at == 0)
    def _():
        for copy in later:
            copy.wait()

    next(blocks[0])
    live = True
    while live:
        live = any([next(block, True) is None for block in reversed(blocks)])


def dense(rank, place, x, ctx, cot, vectors, first, second, size, cut):
    rows, width = x.shape
    hidden = vectors[1].shape[0]
    block = pl.BlockSpec((size, width), lambda i: (i, 0))
    smem = pl.BlockSpec(memory_space=pltpu.SMEM)
    return pl.pallas_call(
        functools.partial(dense_kernel, first, second, cut),
        grid=(rows // size,),
        in_specs=[smem, smem, block, block, block]
        + [pl.BlockSpec(memory_space=pltpu.VMEM)] * len(vectors)
        + [ANY] * (len(first.operands) + len(second.operands)),
        out_specs=[block] * 3,
        out_shape=[jax.ShapeDtypeStruct((rows, width), BF16)] * 3,
        scratch_shapes=[
            pltpu.VMEM((width, width + hidden), BF16),
            pltpu.VMEM((hidden, width), BF16),
            pltpu.VMEM((size, hidden), F32),
            pltpu.SemaphoreType.DMA((2, max(first.copies, second.copies))),
        ],
        compiler_params=pltpu.CompilerParams(vmem_limit_bytes=DENSE_VMEM),
        cost_estimate=pl.CostEstimate(
            flops=rows * width * (4 * width + 8 * hidden),
            bytes_accessed=12 * rows * width + 4 * width * hidden,
            transcendentals=2 * rows * hidden,
        ),
        name="dense_both_ways",
    )(rank, place, x, ctx, cot, *vectors, *first.operands, *second.operands)


def attend_back_kernel(x_ref, fac_ref, down_ref, *rest):
    q_ref, k_ref, v_ref, dctx_ref, ctx_ref, inverse_ref, expo_ref, *rest = rest
    dq_ref, dk_ref, dv_ref, dlow_ref, grad_ref, low, total, table = rest
    pack, at = pl.program_id(0), pl.program_id(1)
    rows, width = q_ref.shape
    rank2 = 2 * ADAPTER_RANK
    columns = pl.ds(pl.multiple_of(at * width, LANES), width)

    @pl.when((pack == 0) & (at == 0))
    def _():
        table[...] = adapter_rows(fac_ref, 0, *table.shape)

    lane = lax.broadcasted_iota(jnp.int32, (rows, LANES), 1)
    aug_v = jnp.where(lane < 3, 1.0, 0.0).astype(BF16)
    zero = BF16(0)
    half = LANES // 2
    scale = BF16(half ** (-0.5))
    for pair in range(width // LANES):
        here = slice(LANES * pair, LANES * (pair + 1))
        key = k_ref[:, here] * scale
        query = q_ref[:, here] * scale
        grad = (dctx_ref[:, here].astype(F32) * inverse_ref[:, here]).astype(BF16)
        values = beside(v_ref[:, here], aug_v)
        product = grad.astype(F32) * ctx_ref[:, here].astype(F32)
        dq = dk = dv = 0.0
        for side in range(2):
            mask = (lane // half) == side
            one_query = jnp.where(mask, query, zero)
            one_grad = jnp.where(mask, grad, zero)
            one_key = jnp.where(mask, key, zero)
            inner = -jnp.sum(jnp.where(mask, product, 0.0), axis=1, keepdims=True)
            high, middle, little = three_parts(inner)
            aug_d = jnp.where(
                lane == 0, high, jnp.where(lane == 1, middle, jnp.where(lane == 2, little, 0.0))
            ).astype(BF16)
            head = 2 * pair + side
            expo = expo_ref[head * rows : (head + 1) * rows, :]
            dprobs = dot(beside(one_grad, aug_d), values, NT)
            dscores = (expo.astype(F32) * dprobs).astype(BF16)
            dv = dv + dot(expo, one_grad, TN)
            dk = dk + dot(dscores, one_query, TN)
            dq = dq + dot(dscores, one_key, NN)
        dq_ref[:, here] = dq.astype(BF16)
        dk_ref[:, here] = dk.astype(BF16)
        dv_ref[:, here] = dv.astype(BF16)

    up = table[rank2 : 2 * rank2, columns]
    row = lax.broadcasted_iota(jnp.int32, up.shape, 0)
    up_q = jnp.where(row < ADAPTER_RANK, up, 0.0).astype(BF16)
    up_v = jnp.where(row < ADAPTER_RANK, 0.0, up).astype(BF16)
    dlow = dot(dq_ref[...], up_q, NT) + dot(dv_ref[...], up_v, NT)
    low[...] = dlow + jnp.where(at == 0, 0.0, low[...])
    down = down_ref[...]
    from_q = dot(down, dq_ref[...], TN)
    from_v = dot(down, dv_ref[...], TN)
    share = 2.0 * jnp.where(row < ADAPTER_RANK, from_q, from_v)
    later = pack > 0
    total[rank2 : 2 * rank2, columns] = share + jnp.where(
        later, total[rank2 : 2 * rank2, columns], 0.0
    )

    @pl.when(at == pl.num_programs(1) - 1)
    def _():
        dlow_low = (2.0 * low[...]).astype(BF16)
        dlow_ref[...] = dlow_low
        total[0:rank2, :] = dot(dlow_low, x_ref[...], TN) + jnp.where(
            later, total[0:rank2, :], 0.0
        )
        grad_ref[...] = total[...].astype(BF16)


def attend_back(x, factors, down, q, k, v, dctx, ctx, inverse, expo, pairs):
    size = expo.shape[1]
    rows, width = x.shape
    cut = pairs * LANES
    packs, groups = rows // size, width // cut
    rank2 = 2 * ADAPTER_RANK
    block = pl.BlockSpec((size, cut), lambda p, g: (p, g))
    whole = lambda shape: pl.BlockSpec(shape, lambda p, g: (0, 0), pipeline_mode=pl.Buffered(1))
    like = jax.ShapeDtypeStruct
    return pl.pallas_call(
        attend_back_kernel,
        grid=(packs, width // cut),
        in_specs=[
            pl.BlockSpec((size, width), lambda p, g: (p, 0)),
            pl.BlockSpec(memory_space=pltpu.VMEM),
            pl.BlockSpec((size, rank2), lambda p, g: (p, 0)),
            block,
            block,
            block,
            block,
            block,
            block,
            pl.BlockSpec((2 * pairs * size, size), lambda p, g: (p * groups + g, 0)),
        ],
        out_specs=[
            block,
            block,
            block,
            pl.BlockSpec((size, rank2), lambda p, g: (p, 0)),
            whole((2 * rank2, width)),
        ],
        out_shape=[like((rows, width), BF16)] * 3
        + [like((rows, rank2), BF16), like((2 * rank2, width), BF16)],
        scratch_shapes=[pltpu.VMEM((size, rank2), F32)]
        + [pltpu.VMEM((2 * rank2, width), F32)] * 2,
        compiler_params=pltpu.CompilerParams(vmem_limit_bytes=BACK_VMEM),
        cost_estimate=pl.CostEstimate(
            flops=rows * width * 30 * size,
            bytes_accessed=24 * rows * width,
            transcendentals=rows * size * HEADS,
        ),
        name="attend_back",
    )(x, factors, down, q, k, v, dctx, ctx, inverse, expo)


def input_kernel(first, dh_ref, dq_ref, dk_ref, dv_ref, dlow_ref, fac_ref, weights, *rest):
    out_ref = rest[-1]
    size, width = out_ref.shape
    block = slice(first, first + size)
    down = adapter_rows(fac_ref, 0, 2 * ADAPTER_RANK, width).astype(BF16)
    total = dh_ref[block, :].astype(F32) + dot(dlow_ref[block, :], down, NN)
    for at, grad in enumerate((dq_ref, dk_ref, dv_ref)):
        total = total + dot(grad[block, :], weights[at], NT)
    out_ref[...] = total.astype(BF16)


def input_back(dh, dq, dk, dv, dlow, factors, weights, size, at, carry):
    rows, width = dh.shape
    vmem = pl.BlockSpec(memory_space=pltpu.VMEM)
    return pl.pallas_call(
        functools.partial(input_kernel, at * size),
        grid=(1,),
        in_specs=[vmem] * 7 + [ANY] * len(carry),
        out_specs=pl.BlockSpec((size, width), lambda i: (at, 0)),
        out_shape=jax.ShapeDtypeStruct((rows, width), BF16),
        input_output_aliases={7 + i: i for i in range(len(carry))},
        compiler_params=pltpu.CompilerParams(vmem_limit_bytes=INPUT_VMEM),
        cost_estimate=pl.CostEstimate(
            flops=6 * size * width * width,
            bytes_accessed=10 * size * width,
            transcendentals=0,
        ),
        name="input_gradient",
    )(dh, dq, dk, dv, dlow, factors, weights, *carry)


def update_kernel(place_ref, near_ref, far_ref, fac_ref, held_ref, other_ref, *rest):
    grad_ref, new_ref, new_first_ref, new_second_ref, lines, table, first, second = rest
    place = place_ref[0]
    owners, length, lanes = fac_ref.shape
    grad = near_ref[...].astype(F32) + far_ref[...].astype(F32)
    rows, width = grad.shape
    step = width // lanes
    for at in range(step):
        lines[pl.ds(at, rows, stride=step), :] = grad[:, at * lanes : (at + 1) * lanes]
    for owner in range(owners):
        table[owner] = lines[owner * length : (owner + 1) * length, :]
    half = owners // 2
    for at in range(owners):
        ref = held_ref if at < half else other_ref
        owner = jnp.bitwise_xor(place, at)
        first[owner] = ref[at % half, 0]
        second[owner] = ref[at % half, 1]
    clip = jnp.minimum(1.0, 1.0 / (jnp.sqrt(jnp.sum(grad * grad)) + 1e-06))
    clipped = table[...] * clip
    new_first = 0.9 * first[...] + 0.1 * clipped
    new_second = 0.999 * second[...] + 0.001 * clipped * clipped
    first[...] = new_first
    second[...] = new_second
    grad_ref[...] = table[place]
    new_first_ref[...] = first[place]
    new_second_ref[...] = second[place]
    factors = fac_ref[...]
    owner = lax.broadcasted_iota(jnp.int32, factors.shape, 0)
    rate = jnp.where(owner < half, rate_low, rate_high)
    fix_first = 1.0 - 0.9**STEP
    fix_second = 1.0 - 0.999**STEP
    move = new_first / fix_first / (jnp.sqrt(new_second / fix_second) + 1e-08)
    new_ref[...] = factors - rate * (move + decay_rate * factors)


def update(place, near, far, factors, held, other):
    like = lambda shape: jax.ShapeDtypeStruct(shape, F32)
    owners, length, lanes = factors.shape
    vmem = pl.BlockSpec(memory_space=pltpu.VMEM)
    piece = like((length, lanes))
    return pl.pallas_call(
        update_kernel,
        in_specs=[pl.BlockSpec(memory_space=pltpu.SMEM)] + [vmem] * 5,
        out_shape=[piece, like(factors.shape), piece, piece],
        scratch_shapes=[pltpu.VMEM((owners * length, lanes), F32)]
        + [pltpu.VMEM(factors.shape, F32)] * 3,
        compiler_params=pltpu.CompilerParams(vmem_limit_bytes=SMALL_VMEM),
        name="adapter_update",
    )(place, near, far, factors, held, other)


def bits(size):
    return [1 << at for at in range(size.bit_length() - 1)]


def swap(value, axis, size, flip):
    return lax.ppermute(value, axis, [(i, i ^ flip) for i in range(size)])


def cross(value, reps, wide):
    pairs = []
    for rank in range(reps):
        for place in range(wide):
            other = place ^ (1 if rank % 2 == 0 else 2)
            pairs.append((rank * wide + place, rank * wide + other))
    return lax.ppermute(value, ("rep", "wide"), pairs)


def fetch(mine, reps):
    held = [(0, mine)]
    for flip in bits(reps)[1:]:
        held += [(have ^ flip, swap(value, "rep", reps, flip)) for have, value in held]
    return held[1:]


def finish(parts, block_of, halves, crossed, reps, early=None):
    for side, values in enumerate((halves, crossed)):
        for flip, value in values:
            for core in range(2):
                piece = swap(value, "rep", reps, 1) if core else value
                if core and side == 0 and early is not None:
                    piece = gate(piece, early, GATE)
                rows = value.shape[-2]
                places = [(index, block, flip ^ core, (side,), rows, 1) for index, block in block_of]
                parts.add(piece, *places)


def across(halves, reps, wide):
    return [(flip, cross(value, reps, wide)) for flip, value in halves]


def together(*values):
    return lax.optimization_barrier(values)


def gate_kernel(value_ref, other_ref, out_ref):
    pass


def gate(value, other, flops=10**11):
    return pl.pallas_call(
        gate_kernel,
        in_specs=[ANY, ANY],
        out_specs=ANY,
        out_shape=jax.ShapeDtypeStruct(value.shape, value.dtype),
        input_output_aliases={0: 0},
        cost_estimate=pl.CostEstimate(flops=flops, bytes_accessed=1, transcendentals=0),
        name="gate",
    )(value, other)


def local(sizes, *args):
    (
        tokens,
        segment_ids,
        cotangent,
        w_query,
        w_key,
        w_value,
        w_output,
        w_inner,
        w_outer,
        b_query,
        b_value,
        *vectors,
        factors,
        first_moment,
        second_moment,
    ) = args
    reps, wide = sizes
    width = tokens.shape[1]
    packs, size = segment_ids.shape
    rank = lax.axis_index("rep").reshape(1)
    place = lax.axis_index("wide").reshape(1)
    table = factors.reshape(-1, LANES)

    hidden = w_inner.shape[1]
    side = side_of(place[0])
    heads = Parts()
    sent = []
    for block, shard in enumerate((w_query, w_key, w_value)):
        rows = shard.shape[0] // 2
        heads.add(shard, ((), block, 0, 0, rows, 2))
        sent.append(fetch(lax.dynamic_slice_in_dim(shard, side * rows, rows), reps))

    own_ahead = [w_output, w_inner]
    set_ahead = [(0, 0)] + [(1, start) for start in range(0, hidden, width)]
    near_ahead, mine_ahead = pack(place, own_ahead, [(set_ahead, width)])[0]
    flip, value = sent[0][-1]
    value, near_outer, *shards = together(value, w_outer, w_query, w_key, w_value)
    sent[0][-1] = (flip, value)
    for block, shard in enumerate(shards):
        heads.add(swap(shard, "rep", reps, 1), ((), block, 1, 0, shard.shape[0] // 2, 2))
    flip, value = sent[-1][-1]
    length = first_moment.shape[0] // LANES
    held = jnp.stack([first_moment, second_moment]).reshape(1, 2, length, LANES)
    value, mine_ahead, near_ahead, held = together(value, mine_ahead, near_ahead, held)
    sent[-1][-1] = (flip, value)
    flips = bits(wide)
    pending = swap(held, "wide", wide, flips[0])
    crossed = [across(halves, reps, wide) for halves in sent]
    (flip, value), whole_outer = crossed[-1][-1], w_outer
    value, whole_outer = together(value, whole_outer)
    crossed[-1][-1] = (flip, value)
    for block, (halves, others) in enumerate(zip(sent, crossed)):
        finish(heads, [((), block)], halves, others, reps)
    whole_outer = fetch(whole_outer, reps)
    halves_ahead = fetch(mine_ahead, reps)

    early = packs // 2
    arguments = (rank, place, segment_ids, tokens, table, b_query, b_value, 3)
    *attended, weights = attend(*arguments, 0, early, heads)
    weights, *values = together(weights, *[value for _, value in halves_ahead])
    values = [gate(value, weights, GATE) for value in values]
    halves_ahead = [(flip, value) for (flip, _), value in zip(halves_ahead, values)]
    crossed_ahead = across(halves_ahead, reps, wide)
    q, k, v, ctx, inverse, expo, down = attend(
        *arguments, early, packs - early, None, weights, attended
    )
    flips_outer, whole_outer = zip(*whole_outer)
    flips_ahead, crossed_ahead = zip(*crossed_ahead)
    down, pending, held, *values = together(down, pending, held, *crossed_ahead, *whole_outer)
    crossed_ahead = list(zip(flips_ahead, values))
    whole_outer = list(zip(flips_outer, values[len(flips_ahead) :]))
    for flip in flips[1:-1]:
        held = jnp.concatenate([held, pending])
        pending = swap(held, "wide", wide, flip)
    rows = w_output.shape[0] // 2
    ahead = Parts()
    ahead.add(w_output, ((), 0, 0, 0, rows, 2))
    columns = [(slice(None), slice(start, start + width)) for start in range(0, hidden, width)]
    ahead.add(w_inner, *[(at, 1 + block, 0, 0, rows, 2) for block, at in enumerate(columns)])
    blocks = range(len(set_ahead))
    near_ahead = swap(near_ahead, "rep", reps, 1)
    ahead.add(near_ahead, *[((s, at), at, 1, s, rows, 1) for at in blocks for s in range(2)])
    finish(ahead, [((at,), at) for at in blocks], halves_ahead, crossed_ahead, reps, down)
    rows = w_outer.shape[0] // 2
    outer = Parts()
    outer.add(w_outer, ((), 0, 0, 0, rows, 2))
    outer.add(swap(near_outer, "rep", reps, 1), ((), 0, 1, 0, rows, 2))
    for flip, value in whole_outer:
        outer.add(value, ((), 0, flip, 0, rows, 2))
        outer.add(swap(value, "rep", reps, 1), ((), 0, flip ^ 1, 0, rows, 2))
    layer_out, dh, dctx = dense(
        rank, place, tokens, ctx, cotangent, vectors, ahead, outer, size, 1024
    )
    dctx, pending, held = together(dctx, pending, held)
    held = jnp.concatenate([held, pending])
    other = swap(held, "wide", wide, flips[-1])
    dq, dk, dv, dlow, grad = attend_back(
        tokens, table, down, q, k, v, dctx, ctx, inverse, expo, 3
    )
    rounds = [("rep", reps, flip) for flip in bits(reps)]
    rounds += [("wide", wide, flip) for flip in bits(wide)]
    pieces = 4
    part = tokens.shape[0] // pieces
    input_grad = []
    for at, (axis, count, flip) in enumerate(rounds):
        far = swap(grad, axis, count, flip)
        start = at - (len(rounds) - pieces)
        if start >= 0:
            dh, grad = together(dh, grad)
            args = (dh, dq, dk, dv, dlow, table, weights, part, start)
            input_grad = [input_back(*args, input_grad)]
        if at < len(rounds) - 1:
            grad = grad + far
            if start >= 0:
                grad, *input_grad = together(grad, *input_grad)
    flat = factors.reshape(wide, length, LANES)
    new = update(place, grad, far, flat, held, other)
    piece, new_factors, new_first, new_second = [value.reshape(-1) for value in new]
    return (layer_out, input_grad[0], piece, new_factors, new_first, new_second)


def solution(mesh):
    rows = P(("rep", "wide"), None)
    shard = P("rep", None)
    piece = P("wide")
    placed = (rows,) * 3 + (shard,) * 6 + (P(),) * 10 + (piece,) * 2
    return jax.shard_map(
        functools.partial(local, (mesh.shape["rep"], mesh.shape["wide"])),
        mesh=mesh,
        in_specs=placed,
        out_specs=(rows, rows, piece, P(), piece, piece),
        check_vma=False,
    )
```

```python
import functools

import jax
import jax.numpy as jnp
from jax import lax
from jax.experimental import pallas as pl
from jax.experimental.pallas import tpu as pltpu
from jax.sharding import PartitionSpec as P

HEADS = 12
ADAPTER_RANK = 8
STEP = 10
LANES = 128
MASKED = 1e30

rate_low = 0.015
rate_high = 0.24
decay_rate = 0.01

BF16 = jnp.bfloat16
F32 = jnp.float32
NN = (((1,), (0,)), ((), ()))
NT = (((1,), (1,)), ((), ()))
TN = (((0,), (0,)), ((), ()))
ANY = pl.BlockSpec(memory_space=pl.ANY)
HBM = pl.BlockSpec(memory_space=pltpu.HBM)
VMEM_LIMIT = 56 * 2**20
LATE = 6 * 10**9
SMALL_VMEM = 8 * 2**20
INPUT_VMEM = 24 * 2**20
BACK_VMEM = 44 * 2**20
DENSE_VMEM = 56 * 2**20
ATTEND_VMEM = 56 * 2**20
GATE = 5 * 10**9


def dot(left, right, dims):
    return lax.dot_general(left, right, dims, preferred_element_type=F32)


def beside(*parts):
    return jnp.concatenate(parts, axis=1)


def mean(value):
    return jnp.mean(value, -1, keepdims=True)


def layer_norm(hidden):
    centre = hidden - mean(hidden)
    rstd = lax.rsqrt(mean(centre * centre) + 1e-05)
    return (centre * rstd, rstd)


def norm_back(grad, normal, rstd, gain):
    scaled = grad * gain
    return rstd * (scaled - mean(scaled) - normal * mean(scaled * normal))


def gelu_pair(value):
    below = 0.5 + 0.5 * lax.erf(value * 2.0 ** (-0.5))
    density = jnp.exp(-0.5 * value * value) * 0.3989422804014327
    return (value * below, below + value * density)


def adapter_rows(lines_ref, first, count, width):
    step = width // LANES
    return beside(
        *[lines_ref[pl.ds(first * step + at, count, stride=step), :] for at in range(step)]
    )


def three_parts(value):
    high = value.astype(BF16).astype(F32)
    rest = value - high
    middle = rest.astype(BF16).astype(F32)
    return (high, middle, rest - middle)


def rows_at(rank, flip, side, rows):
    return pl.multiple_of((jnp.bitwise_xor(rank, flip) * 2 + side) * rows, 16)


def side_of(place):
    return jnp.bitwise_and(jnp.bitwise_xor(place, place >> 1), 1)


class Parts:
    def __init__(self):
        self.operands, self.places = [], []

    def add(self, array, *places):
        self.places += [(len(self.operands),) + place for place in places]
        self.operands.append(array)

    @property
    def copies(self):
        return len(self.places)

    def into(self, refs, rank, place, views, semaphores):
        mine = side_of(place)
        found = [[] for _ in views]
        for at, (operand, index, block, flip, side, rows, halves) in enumerate(self.places):
            source = refs[operand].at[index] if index else refs[operand]
            if isinstance(side, tuple):
                side = jnp.bitwise_xor(mine, side[0])
            target = views[block](rows_at(rank, flip, side, rows), rows * halves)
            found[block].append(pltpu.make_async_copy(source, target, semaphores.at[at]))
        return found


def stacked(weights):
    def view(at):
        return lambda row, rows: weights.at[at, pl.ds(row, rows)]

    return [view(at) for at in range(weights.shape[0])]


def in_columns(weights, width):
    def view(start):
        return lambda row, rows: weights.at[pl.ds(row, rows), start : start + width]

    return [view(start) for start in range(0, weights.shape[1], width)]


def run_copies(copies):
    for copy in copies:
        copy.start()
    for copy in copies:
        copy.wait()


def pack_kernel(sets, count, place_ref, *rest):
    sources, rest = rest[:count], rest[count:]
    outs, rest = rest[: 2 * len(sets)], rest[2 * len(sets) :]
    holds, (arrive, leave) = rest[:-2], rest[-2:]
    side = side_of(place_ref[0])
    incoming, outgoing = [], []
    copy = pltpu.make_async_copy
    for blocks, near_ref, mine_ref, hold in zip(sets, outs[::2], outs[1::2], holds):
        rows, width = mine_ref.shape[1:]
        for block, (source, first) in enumerate(blocks):
            for half in range(2):
                part = sources[source].at[pl.ds(half * rows, rows), pl.ds(first, width)]
                incoming.append(copy(part, hold.at[half, block], arrive.at[len(incoming)]))
        outgoing.append((len(incoming), copy(hold.at[side], mine_ref, leave.at[len(outgoing)])))
        outgoing.append((len(incoming), copy(hold, near_ref, leave.at[len(outgoing)])))
    for one in incoming:
        one.start()
    done = 0
    for needed, one in outgoing:
        for other in incoming[done:needed]:
            other.wait()
        done = needed
        one.start()
    for _, one in outgoing:
        one.wait()


def pack(place, shards, sets):
    shapes = []
    holds = []
    copies = 0
    for blocks, width in sets:
        rows = shards[blocks[0][0]].shape[0] // 2
        holds.append((2, len(blocks), rows, width))
        shapes += [holds[-1], holds[-1][1:]]
        copies += 2 * len(blocks)
    found = pl.pallas_call(
        functools.partial(pack_kernel, [blocks for blocks, _ in sets], len(shards)),
        in_specs=[pl.BlockSpec(memory_space=pltpu.SMEM)] + [HBM] * len(shards),
        out_specs=[HBM] * len(shapes),
        out_shape=[jax.ShapeDtypeStruct(shape, BF16) for shape in shapes],
        scratch_shapes=[pltpu.VMEM(shape, BF16) for shape in holds]
        + [pltpu.SemaphoreType.DMA((copies,)), pltpu.SemaphoreType.DMA((len(shapes),))],
        compiler_params=pltpu.CompilerParams(vmem_limit_bytes=VMEM_LIMIT),
        name="pack_shards",
    )(place, *shards)
    return list(zip(found[::2], found[1::2]))


def attend_kernel(parts, first, rank_ref, place_ref, seg_ref, x_ref, fac_ref, bq_ref, bv_ref, *rest):
    at = pl.program_id(1)
    begin = (pl.program_id(0) == 0) & (at == 0)
    if parts is None:
        weights, rest = rest[0], rest[8:]
        q_ref, k_ref, v_ref, ctx_ref, inverse_ref, expo_ref, down_ref, bias, table = rest
    else:
        shards, rest = rest[: len(parts.operands)], rest[len(parts.operands) :]
        q_ref, k_ref, v_ref, ctx_ref, inverse_ref, expo_ref, down_ref, *rest = rest
        weights, bias, table, semaphores = rest

        @pl.when(begin)
        def _():
            blocks = parts.into(shards, rank_ref[0], place_ref[0], stacked(weights), semaphores)
            run_copies(sum(blocks, []))

    width = q_ref.shape[1]
    rows = x_ref.shape[0]

    @pl.when(begin)
    def _():
        bias[0:1, :] = bq_ref[...].reshape(1, -1)
        bias[1:2, :] = bv_ref[...].reshape(1, -1)
        table[...] = adapter_rows(fac_ref, 0, *table.shape)

    rank2 = 2 * ADAPTER_RANK
    columns = pl.ds(pl.multiple_of(at * width, LANES), width)
    x = x_ref[...]
    low = dot(x, table[0:rank2, :].astype(BF16), NT).astype(BF16)
    down_ref[...] = low
    up = table[rank2 : 2 * rank2, columns]
    row = lax.broadcasted_iota(jnp.int32, up.shape, 0)
    up_q = jnp.where(row < ADAPTER_RANK, up, 0.0).astype(BF16)
    up_v = jnp.where(row < ADAPTER_RANK, 0.0, up).astype(BF16)
    q_ref[...] = (dot(x, weights[0, :, columns], NN) + bias[0:1, columns] + 2.0 * dot(low, up_q, NN)).astype(BF16)
    k_ref[...] = dot(x, weights[1, :, columns], NN).astype(BF16)
    v_ref[...] = (dot(x, weights[2, :, columns], NN) + bias[1:2, columns] + 2.0 * dot(low, up_v, NN)).astype(BF16)

    lane = lax.broadcasted_iota(jnp.int32, (rows, LANES), 1)
    seg = seg_ref[pl.ds(first + pl.program_id(0), 1), :].astype(F32).T.astype(jnp.int32)
    aug_k = jnp.where((lane < 4) & (lane != seg), -MASKED, 0.0).astype(BF16)
    aug_q = jnp.where(lane == seg, 1.0, 0.0).astype(BF16)
    ones = jnp.ones((rows, LANES), BF16)
    half = LANES // 2
    scale = BF16(half ** (-0.5))
    second = lane >= half

    def scores(head):
        here = slice(LANES * (head // 2), LANES * (head // 2 + 1))
        query = jnp.where(second == (head % 2 == 1), q_ref[:, here] * scale, BF16(0))
        return dot(beside(query, aug_q), beside(k_ref[:, here], aug_k), NT)

    heads = 2 * width // LANES
    ahead = scores(0)
    found = []
    for head in range(heads):
        now = ahead
        if head + 1 < heads:
            ahead = scores(head + 1)
        here = slice(LANES * (head // 2), LANES * (head // 2 + 1))
        expo = jnp.exp(now - jnp.max(now, axis=1, keepdims=True)).astype(BF16)
        expo_ref[head * rows : (head + 1) * rows, :] = expo
        both = dot(expo, beside(v_ref[:, here], ones), NN)
        found.append((both[:, :LANES], both[:, LANES:]))
        if head % 2 == 1:
            (ctx0, sums0), (ctx1, sums1) = found[-2:]
            inverse = 1.0 / jnp.where(second, sums1, sums0)
            inverse_ref[:, here] = inverse
            ctx_ref[:, here] = (jnp.where(second, ctx1, ctx0) * inverse).astype(BF16)


def attend(rank, place, seg, x, factors, bq, bv, pairs, first, count, parts, weights=None, carry=()):
    packs, size = seg.shape
    rows, width = x.shape
    cut = pairs * LANES
    groups = width // cut
    block = pl.BlockSpec((size, cut), lambda p, g: (first + p, g))
    vmem = pl.BlockSpec(memory_space=pltpu.VMEM)
    smem = pl.BlockSpec(memory_space=pltpu.SMEM)
    like = jax.ShapeDtypeStruct
    out_specs = [
        block,
        block,
        block,
        block,
        block,
        pl.BlockSpec((2 * pairs * size, size), lambda p, g: ((first + p) * groups + g, 0)),
        pl.BlockSpec((size, 2 * ADAPTER_RANK), lambda p, g: (first + p, 0)),
    ]
    out_shape = [like((rows, width), BF16)] * 4 + [like((rows, width), F32)]
    out_shape += [like((HEADS * rows, size), BF16), like((rows, 2 * ADAPTER_RANK), BF16)]
    scratch = [pltpu.VMEM((8, width), F32), pltpu.VMEM((4 * ADAPTER_RANK, width), F32)]
    if parts is None:
        operands, specs = [weights, *carry], [vmem] + [ANY] * len(carry)
    else:
        operands, specs = parts.operands, [ANY] * len(parts.operands)
        out_specs.append(pl.BlockSpec((3, width, width), lambda p, g: (0, 0, 0)))
        out_shape.append(like((3, width, width), BF16))
        scratch.append(pltpu.SemaphoreType.DMA((parts.copies,)))
    return pl.pallas_call(
        functools.partial(attend_kernel, parts, first),
        grid=(count, width // cut),
        in_specs=[
            smem,
            smem,
            vmem,
            pl.BlockSpec((size, width), lambda p, g: (first + p, 0)),
            vmem,
            vmem,
            vmem,
        ]
        + specs,
        out_specs=out_specs,
        out_shape=out_shape,
        input_output_aliases={8 + at: at for at in range(len(carry))},
        scratch_shapes=scratch,
        compiler_params=pltpu.CompilerParams(vmem_limit_bytes=ATTEND_VMEM),
        cost_estimate=pl.CostEstimate(
            flops=1 if carry == () else LATE, bytes_accessed=1, transcendentals=0
        ),
        name="project_and_attend",
    )(rank, place, seg, x, factors, bq, bv, *operands)


def dense_kernel(first, second, cut, rank_ref, place_ref, x_ref, ctx_ref, cot_ref, *rest):
    vectors, rest = rest[:7], rest[7:]
    bo_ref, bi_ref, bo2_ref, g1_ref, s1_ref, g2_ref, s2_ref = vectors
    one, two = len(first.operands), len(second.operands)
    near, far, rest = rest[:one], rest[one : one + two], rest[one + two :]
    out_ref, dh_ref, dctx_ref, ahead, outer, slope, semaphores = rest
    width = x_ref.shape[1]
    hidden = outer.shape[0]

    at = pl.program_id(0)
    rank, place = rank_ref[0], place_ref[0]
    start, *later = first.into(near, rank, place, in_columns(ahead, width), semaphores.at[0])
    later = sum(later + second.into(far, rank, place, in_columns(outer, width), semaphores.at[1]), [])

    @pl.when(at == 0)
    def _():
        for copy in start + later:
            copy.start()
        for copy in start:
            copy.wait()

    bo, bo2 = bo_ref[...].reshape(1, -1), bo2_ref[...].reshape(1, -1)
    g1, s1 = g1_ref[...].reshape(1, -1), s1_ref[...].reshape(1, -1)
    g2, s2 = g2_ref[...].reshape(1, -1), s2_ref[...].reshape(1, -1)
    inner_bias = bi_ref[...].reshape(1, -1)
    wo = lambda: ahead[:, :width]
    w1 = lambda j: ahead[:, width + j : width + j + cut]

    def stages(rows):
        h1 = x_ref[rows, :].astype(F32) + dot(ctx_ref[rows, :], wo(), NN) + bo
        norm1, rstd1 = layer_norm(h1)
        y1 = norm1 * g1 + s1
        y1_low = y1.astype(BF16)
        h2 = y1 + bo2
        yield
        for j in range(0, hidden, cut):
            inner = dot(y1_low, w1(j), NN) + inner_bias[:, j : j + cut]
            act, gradient = gelu_pair(inner)
            slope[rows, j : j + cut] = gradient
            h2 = h2 + dot(act.astype(BF16), outer[j : j + cut, :], NN)
            yield
        norm2, rstd2 = layer_norm(h2)
        out_ref[rows, :] = (norm2 * g2 + s2).astype(BF16)
        dh2 = norm_back(cot_ref[rows, :].astype(F32), norm2, rstd2, g2)
        df = dh2.astype(BF16)
        dy1 = dh2
        yield
        for j in range(0, hidden, cut):
            du = (dot(df, outer[j : j + cut, :], NT) * slope[rows, j : j + cut]).astype(BF16)
            dy1 = dy1 + dot(du, w1(j), NT)
            yield
        dh1 = norm_back(dy1, norm1, rstd1, g1).astype(BF16)
        dh_ref[rows, :] = dh1
        yield
        dctx_ref[rows, :] = dot(dh1, wo(), NT).astype(BF16)

    size = x_ref.shape[0] // 2
    blocks = [stages(slice(start, start + size)) for start in (0, size)]
    next(blocks[0])

    @pl.when(at == 0)
    def _():
        for copy in later:
            copy.wait()

    next(blocks[0])
    live = True
    while live:
        live = any([next(block, True) is None for block in reversed(blocks)])


def dense(rank, place, x, ctx, cot, vectors, first, second, size, cut):
    rows, width = x.shape
    hidden = vectors[1].shape[0]
    block = pl.BlockSpec((size, width), lambda i: (i, 0))
    smem = pl.BlockSpec(memory_space=pltpu.SMEM)
    return pl.pallas_call(
        functools.partial(dense_kernel, first, second, cut),
        grid=(rows // size,),
        in_specs=[smem, smem, block, block, block]
        + [pl.BlockSpec(memory_space=pltpu.VMEM)] * len(vectors)
        + [ANY] * (len(first.operands) + len(second.operands)),
        out_specs=[block] * 3,
        out_shape=[jax.ShapeDtypeStruct((rows, width), BF16)] * 3,
        scratch_shapes=[
            pltpu.VMEM((width, width + hidden), BF16),
            pltpu.VMEM((hidden, width), BF16),
            pltpu.VMEM((size, hidden), F32),
            pltpu.SemaphoreType.DMA((2, max(first.copies, second.copies))),
        ],
        compiler_params=pltpu.CompilerParams(vmem_limit_bytes=DENSE_VMEM),
        cost_estimate=pl.CostEstimate(
            flops=rows * width * (4 * width + 8 * hidden),
            bytes_accessed=12 * rows * width + 4 * width * hidden,
            transcendentals=2 * rows * hidden,
        ),
        name="dense_both_ways",
    )(rank, place, x, ctx, cot, *vectors, *first.operands, *second.operands)


def attend_back_kernel(x_ref, fac_ref, down_ref, *rest):
    q_ref, k_ref, v_ref, dctx_ref, ctx_ref, inverse_ref, expo_ref, *rest = rest
    dq_ref, dk_ref, dv_ref, dlow_ref, grad_ref, low, total, table = rest
    pack, at = pl.program_id(0), pl.program_id(1)
    rows, width = q_ref.shape
    rank2 = 2 * ADAPTER_RANK
    columns = pl.ds(pl.multiple_of(at * width, LANES), width)

    @pl.when((pack == 0) & (at == 0))
    def _():
        table[...] = adapter_rows(fac_ref, 0, *table.shape)

    lane = lax.broadcasted_iota(jnp.int32, (rows, LANES), 1)
    aug_v = jnp.where(lane < 3, 1.0, 0.0).astype(BF16)
    zero = BF16(0)
    half = LANES // 2
    scale = BF16(half ** (-0.5))
    for pair in range(width // LANES):
        here = slice(LANES * pair, LANES * (pair + 1))
        key = k_ref[:, here] * scale
        query = q_ref[:, here] * scale
        grad = (dctx_ref[:, here].astype(F32) * inverse_ref[:, here]).astype(BF16)
        values = beside(v_ref[:, here], aug_v)
        product = grad.astype(F32) * ctx_ref[:, here].astype(F32)
        dq = dk = dv = 0.0
        for side in range(2):
            mask = (lane // half) == side
            one_query = jnp.where(mask, query, zero)
            one_grad = jnp.where(mask, grad, zero)
            one_key = jnp.where(mask, key, zero)
            inner = -jnp.sum(jnp.where(mask, product, 0.0), axis=1, keepdims=True)
            high, middle, little = three_parts(inner)
            aug_d = jnp.where(
                lane == 0, high, jnp.where(lane == 1, middle, jnp.where(lane == 2, little, 0.0))
            ).astype(BF16)
            head = 2 * pair + side
            expo = expo_ref[head * rows : (head + 1) * rows, :]
            dprobs = dot(beside(one_grad, aug_d), values, NT)
            dscores = (expo.astype(F32) * dprobs).astype(BF16)
            dv = dv + dot(expo, one_grad, TN)
            dk = dk + dot(dscores, one_query, TN)
            dq = dq + dot(dscores, one_key, NN)
        dq_ref[:, here] = dq.astype(BF16)
        dk_ref[:, here] = dk.astype(BF16)
        dv_ref[:, here] = dv.astype(BF16)

    up = table[rank2 : 2 * rank2, columns]
    row = lax.broadcasted_iota(jnp.int32, up.shape, 0)
    up_q = jnp.where(row < ADAPTER_RANK, up, 0.0).astype(BF16)
    up_v = jnp.where(row < ADAPTER_RANK, 0.0, up).astype(BF16)
    dlow = dot(dq_ref[...], up_q, NT) + dot(dv_ref[...], up_v, NT)
    low[...] = dlow + jnp.where(at == 0, 0.0, low[...])
    down = down_ref[...]
    from_q = dot(down, dq_ref[...], TN)
    from_v = dot(down, dv_ref[...], TN)
    share = 2.0 * jnp.where(row < ADAPTER_RANK, from_q, from_v)
    later = pack > 0
    total[rank2 : 2 * rank2, columns] = share + jnp.where(
        later, total[rank2 : 2 * rank2, columns], 0.0
    )

    @pl.when(at == pl.num_programs(1) - 1)
    def _():
        dlow_low = (2.0 * low[...]).astype(BF16)
        dlow_ref[...] = dlow_low
        total[0:rank2, :] = dot(dlow_low, x_ref[...], TN) + jnp.where(
            later, total[0:rank2, :], 0.0
        )
        grad_ref[...] = total[...].astype(BF16)


def attend_back(x, factors, down, q, k, v, dctx, ctx, inverse, expo, pairs):
    size = expo.shape[1]
    rows, width = x.shape
    cut = pairs * LANES
    packs, groups = rows // size, width // cut
    rank2 = 2 * ADAPTER_RANK
    block = pl.BlockSpec((size, cut), lambda p, g: (p, g))
    whole = lambda shape: pl.BlockSpec(shape, lambda p, g: (0, 0), pipeline_mode=pl.Buffered(1))
    like = jax.ShapeDtypeStruct
    return pl.pallas_call(
        attend_back_kernel,
        grid=(packs, width // cut),
        in_specs=[
            pl.BlockSpec((size, width), lambda p, g: (p, 0)),
            pl.BlockSpec(memory_space=pltpu.VMEM),
            pl.BlockSpec((size, rank2), lambda p, g: (p, 0)),
            block,
            block,
            block,
            block,
            block,
            block,
            pl.BlockSpec((2 * pairs * size, size), lambda p, g: (p * groups + g, 0)),
        ],
        out_specs=[
            block,
            block,
            block,
            pl.BlockSpec((size, rank2), lambda p, g: (p, 0)),
            whole((2 * rank2, width)),
        ],
        out_shape=[like((rows, width), BF16)] * 3
        + [like((rows, rank2), BF16), like((2 * rank2, width), BF16)],
        scratch_shapes=[pltpu.VMEM((size, rank2), F32)]
        + [pltpu.VMEM((2 * rank2, width), F32)] * 2,
        compiler_params=pltpu.CompilerParams(vmem_limit_bytes=BACK_VMEM),
        cost_estimate=pl.CostEstimate(
            flops=rows * width * 30 * size,
            bytes_accessed=24 * rows * width,
            transcendentals=rows * size * HEADS,
        ),
        name="attend_back",
    )(x, factors, down, q, k, v, dctx, ctx, inverse, expo)


def input_kernel(first, dh_ref, dq_ref, dk_ref, dv_ref, dlow_ref, fac_ref, weights, *rest):
    out_ref = rest[-1]
    size, width = out_ref.shape
    block = slice(first, first + size)
    down = adapter_rows(fac_ref, 0, 2 * ADAPTER_RANK, width).astype(BF16)
    total = dh_ref[block, :].astype(F32) + dot(dlow_ref[block, :], down, NN)
    for at, grad in enumerate((dq_ref, dk_ref, dv_ref)):
        total = total + dot(grad[block, :], weights[at], NT)
    out_ref[...] = total.astype(BF16)


def input_back(dh, dq, dk, dv, dlow, factors, weights, size, at, carry):
    rows, width = dh.shape
    vmem = pl.BlockSpec(memory_space=pltpu.VMEM)
    return pl.pallas_call(
        functools.partial(input_kernel, at * size),
        grid=(1,),
        in_specs=[vmem] * 7 + [ANY] * len(carry),
        out_specs=pl.BlockSpec((size, width), lambda i: (at, 0)),
        out_shape=jax.ShapeDtypeStruct((rows, width), BF16),
        input_output_aliases={7 + i: i for i in range(len(carry))},
        compiler_params=pltpu.CompilerParams(vmem_limit_bytes=INPUT_VMEM),
        cost_estimate=pl.CostEstimate(
            flops=6 * size * width * width,
            bytes_accessed=10 * size * width,
            transcendentals=0,
        ),
        name="input_gradient",
    )(dh, dq, dk, dv, dlow, factors, weights, *carry)


def update_kernel(place_ref, near_ref, far_ref, fac_ref, held_ref, other_ref, *rest):
    grad_ref, new_ref, new_first_ref, new_second_ref, lines, table, first, second = rest
    place = place_ref[0]
    owners, length, lanes = fac_ref.shape
    grad = near_ref[...].astype(F32) + far_ref[...].astype(F32)
    rows, width = grad.shape
    step = width // lanes
    for at in range(step):
        lines[pl.ds(at, rows, stride=step), :] = grad[:, at * lanes : (at + 1) * lanes]
    for owner in range(owners):
        table[owner] = lines[owner * length : (owner + 1) * length, :]
    half = owners // 2
    for at in range(owners):
        ref = held_ref if at < half else other_ref
        owner = jnp.bitwise_xor(place, at)
        first[owner] = ref[at % half, 0]
        second[owner] = ref[at % half, 1]
    clip = jnp.minimum(1.0, 1.0 / (jnp.sqrt(jnp.sum(grad * grad)) + 1e-06))
    clipped = table[...] * clip
    new_first = 0.9 * first[...] + 0.1 * clipped
    new_second = 0.999 * second[...] + 0.001 * clipped * clipped
    first[...] = new_first
    second[...] = new_second
    grad_ref[...] = table[place]
    new_first_ref[...] = first[place]
    new_second_ref[...] = second[place]
    factors = fac_ref[...]
    owner = lax.broadcasted_iota(jnp.int32, factors.shape, 0)
    rate = jnp.where(owner < half, rate_low, rate_high)
    fix_first = 1.0 - 0.9**STEP
    fix_second = 1.0 - 0.999**STEP
    move = new_first / fix_first / (jnp.sqrt(new_second / fix_second) + 1e-08)
    new_ref[...] = factors - rate * (move + decay_rate * factors)


def update(place, near, far, factors, held, other):
    like = lambda shape: jax.ShapeDtypeStruct(shape, F32)
    owners, length, lanes = factors.shape
    vmem = pl.BlockSpec(memory_space=pltpu.VMEM)
    piece = like((length, lanes))
    return pl.pallas_call(
        update_kernel,
        in_specs=[pl.BlockSpec(memory_space=pltpu.SMEM)] + [vmem] * 5,
        out_shape=[piece, like(factors.shape), piece, piece],
        scratch_shapes=[pltpu.VMEM((owners * length, lanes), F32)]
        + [pltpu.VMEM(factors.shape, F32)] * 3,
        compiler_params=pltpu.CompilerParams(vmem_limit_bytes=SMALL_VMEM),
        name="adapter_update",
    )(place, near, far, factors, held, other)


def bits(size):
    return [1 << at for at in range(size.bit_length() - 1)]


def swap(value, axis, size, flip):
    return lax.ppermute(value, axis, [(i, i ^ flip) for i in range(size)])


def cross(value, reps, wide):
    pairs = []
    for rank in range(reps):
        for place in range(wide):
            other = place ^ (1 if rank % 2 == 0 else 2)
            pairs.append((rank * wide + place, rank * wide + other))
    return lax.ppermute(value, ("rep", "wide"), pairs)


def fetch(mine, reps):
    held = [(0, mine)]
    for flip in bits(reps)[1:]:
        held += [(have ^ flip, swap(value, "rep", reps, flip)) for have, value in held]
    return held[1:]


def finish(parts, block_of, halves, crossed, reps, early=None):
    for side, values in enumerate((halves, crossed)):
        for flip, value in values:
            for core in range(2):
                piece = swap(value, "rep", reps, 1) if core else value
                if core and side == 0 and early is not None:
                    piece = gate(piece, early, GATE)
                rows = value.shape[-2]
                places = [(index, block, flip ^ core, (side,), rows, 1) for index, block in block_of]
                parts.add(piece, *places)


def across(halves, reps, wide):
    return [(flip, cross(value, reps, wide)) for flip, value in halves]


def together(*values):
    return lax.optimization_barrier(values)


def gate_kernel(value_ref, other_ref, out_ref):
    pass


def gate(value, other, flops=10**11):
    return pl.pallas_call(
        gate_kernel,
        in_specs=[ANY, ANY],
        out_specs=ANY,
        out_shape=jax.ShapeDtypeStruct(value.shape, value.dtype),
        input_output_aliases={0: 0},
        cost_estimate=pl.CostEstimate(flops=flops, bytes_accessed=1, transcendentals=0),
        name="gate",
    )(value, other)


def local(sizes, *args):
    (
        tokens,
        segment_ids,
        cotangent,
        w_query,
        w_key,
        w_value,
        w_output,
        w_inner,
        w_outer,
        b_query,
        b_value,
        *vectors,
        factors,
        first_moment,
        second_moment,
    ) = args
    reps, wide = sizes
    width = tokens.shape[1]
    packs, size = segment_ids.shape
    rank = lax.axis_index("rep").reshape(1)
    place = lax.axis_index("wide").reshape(1)
    table = factors.reshape(-1, LANES)

    hidden = w_inner.shape[1]
    side = side_of(place[0])
    heads = Parts()
    sent = []
    for block, shard in enumerate((w_query, w_key, w_value)):
        rows = shard.shape[0] // 2
        heads.add(shard, ((), block, 0, 0, rows, 2))
        sent.append(fetch(lax.dynamic_slice_in_dim(shard, side * rows, rows), reps))

    own_ahead = [w_output, w_inner]
    set_ahead = [(0, 0)] + [(1, start) for start in range(0, hidden, width)]
    near_ahead, mine_ahead = pack(place, own_ahead, [(set_ahead, width)])[0]
    flip, value = sent[0][-1]
    value, near_outer, *shards = together(value, w_outer, w_query, w_key, w_value)
    sent[0][-1] = (flip, value)
    for block, shard in enumerate(shards):
        heads.add(swap(shard, "rep", reps, 1), ((), block, 1, 0, shard.shape[0] // 2, 2))
    flip, value = sent[-1][-1]
    length = first_moment.shape[0] // LANES
    held = jnp.stack([first_moment, second_moment]).reshape(1, 2, length, LANES)
    value, mine_ahead, near_ahead, held = together(value, mine_ahead, near_ahead, held)
    sent[-1][-1] = (flip, value)
    flips = bits(wide)
    pending = swap(held, "wide", wide, flips[0])
    crossed = [across(halves, reps, wide) for halves in sent]
    (flip, value), whole_outer = crossed[-1][-1], w_outer
    value, whole_outer = together(value, whole_outer)
    crossed[-1][-1] = (flip, value)
    for block, (halves, others) in enumerate(zip(sent, crossed)):
        finish(heads, [((), block)], halves, others, reps)
    whole_outer = fetch(whole_outer, reps)
    halves_ahead = fetch(mine_ahead, reps)

    early = packs // 2
    arguments = (rank, place, segment_ids, tokens, table, b_query, b_value, 2)
    *attended, weights = attend(*arguments, 0, early, heads)
    weights, *values = together(weights, *[value for _, value in halves_ahead])
    values = [gate(value, weights, GATE) for value in values]
    halves_ahead = [(flip, value) for (flip, _), value in zip(halves_ahead, values)]
    crossed_ahead = across(halves_ahead, reps, wide)
    q, k, v, ctx, inverse, expo, down = attend(
        *arguments, early, packs - early, None, weights, attended
    )
    flips_outer, whole_outer = zip(*whole_outer)
    flips_ahead, crossed_ahead = zip(*crossed_ahead)
    down, pending, held, *values = together(down, pending, held, *crossed_ahead, *whole_outer)
    crossed_ahead = list(zip(flips_ahead, values))
    whole_outer = list(zip(flips_outer, values[len(flips_ahead) :]))
    for flip in flips[1:-1]:
        held = jnp.concatenate([held, pending])
        pending = swap(held, "wide", wide, flip)
    rows = w_output.shape[0] // 2
    ahead = Parts()
    ahead.add(w_output, ((), 0, 0, 0, rows, 2))
    columns = [(slice(None), slice(start, start + width)) for start in range(0, hidden, width)]
    ahead.add(w_inner, *[(at, 1 + block, 0, 0, rows, 2) for block, at in enumerate(columns)])
    blocks = range(len(set_ahead))
    near_ahead = swap(near_ahead, "rep", reps, 1)
    ahead.add(near_ahead, *[((s, at), at, 1, s, rows, 1) for at in blocks for s in range(2)])
    finish(ahead, [((at,), at) for at in blocks], halves_ahead, crossed_ahead, reps, down)
    rows = w_outer.shape[0] // 2
    outer = Parts()
    outer.add(w_outer, ((), 0, 0, 0, rows, 2))
    outer.add(swap(near_outer, "rep", reps, 1), ((), 0, 1, 0, rows, 2))
    for flip, value in whole_outer:
        outer.add(value, ((), 0, flip, 0, rows, 2))
        outer.add(swap(value, "rep", reps, 1), ((), 0, flip ^ 1, 0, rows, 2))
    layer_out, dh, dctx = dense(
        rank, place, tokens, ctx, cotangent, vectors, ahead, outer, size, 1024
    )
    dctx, pending, held = together(dctx, pending, held)
    held = jnp.concatenate([held, pending])
    other = swap(held, "wide", wide, flips[-1])
    dq, dk, dv, dlow, grad = attend_back(
        tokens, table, down, q, k, v, dctx, ctx, inverse, expo, 3
    )
    rounds = [("rep", reps, flip) for flip in bits(reps)]
    rounds += [("wide", wide, flip) for flip in bits(wide)]
    pieces = 4
    part = tokens.shape[0] // pieces
    input_grad = []
    for at, (axis, count, flip) in enumerate(rounds):
        far = swap(grad, axis, count, flip)
        start = at - (len(rounds) - pieces)
        if start >= 0:
            dh, grad = together(dh, grad)
            args = (dh, dq, dk, dv, dlow, table, weights, part, start)
            input_grad = [input_back(*args, input_grad)]
        if at < len(rounds) - 1:
            grad = grad + far
            if start >= 0:
                grad, *input_grad = together(grad, *input_grad)
    flat = factors.reshape(wide, length, LANES)
    new = update(place, grad, far, flat, held, other)
    piece, new_factors, new_first, new_second = [value.reshape(-1) for value in new]
    return (layer_out, input_grad[0], piece, new_factors, new_first, new_second)


def solution(mesh):
    rows = P(("rep", "wide"), None)
    shard = P("rep", None)
    piece = P("wide")
    placed = (rows,) * 3 + (shard,) * 6 + (P(),) * 10 + (piece,) * 2
    return jax.shard_map(
        functools.partial(local, (mesh.shape["rep"], mesh.shape["wide"])),
        mesh=mesh,
        in_specs=placed,
        out_specs=(rows, rows, piece, P(), piece, piece),
        check_vma=False,
    )
```
